256 devices in a mesh: grp: 2 (over core), zon: 16 (over z, y_hi), mer: 8 (over x, y_lo).
Axes of the slice: x: 4, y: 4 (y_hi: 2, y_lo: 2; y = y_hi * 2 + y_lo), z: 8, core: 2. Of those that a mesh axis runs over, the one named last changes fastest.
Arguments:
- model_state: float32 [4, 6, 512, 2048], P(None, 'grp', 'mer', 'zon'), may hold values from -4 to 4
- control: float32 [4, 6, 512, 2048], P('grp', None, 'mer', 'zon'), may hold values from -6 to 6
- error_std: float32 [4, 6, 512, 2048], P('grp', None, 'mer', 'zon'), may hold values from 0.3 to 3
- bottom_level: int32 [512, 2048], P('mer', 'zon'), may hold values from 0 to 6
- obs_count: int32 [2, 8, 16], P('grp', 'mer', 'zon'), may hold values from 1 to 256, as said below
- obs_corner: int32 [2, 8, 16, 256], P('grp', 'mer', 'zon'), may hold values from 0 to 98174, as said below
- obs_weight: float32 [2, 8, 16, 4, 256], P('grp', 'mer', 'zon'), may hold values from 0 to 1, as said below
- obs_value: float32 [2, 8, 16, 256], P('grp', 'mer', 'zon'), may hold values from -5 to 5
- obs_precision: float32 [2, 8, 16, 256], P('grp', 'mer', 'zon'), may hold values from 0.25 to 4
Outputs:
- gradient: float32 [4, 6, 512, 2048], P('grp', None, 'mer', 'zon')
The draws below stay inside these ranges and needn't reach their ends.
Inputs may be any that keep to these rules, and one draw needn't show every extreme that they name: `obs_count`: at least one live observation in every block, exactly 256 in some block. `obs_corner`: each slot's four interpolation cells lie in its own tile; padded slots also hold valid indices. `obs_weight`: the four weights of a slot are nonnegative and sum to one.
All inputs are finite; a program needn't handle non-finite values.
Results may differ from the reference program's by a relative error of at most 0.0003.
Values may be sent and summed in bfloat16 or wider, within the bound.
No kernel may reach another device: no remote copies, remote signals or barrier semaphores. Data moves between devices by JAX's collectives and lax.ppermute only.
A program may use at most 64 MiB of HBM per device.

```python
import math
import jax
import jax.numpy as jnp
from jax import lax

FIELDS = 4
CX = 128
CY = 64
LEV = 6
CAP = 256
SWEEPS = 10
NX = 2048
NY = 512
N_GRP = 2
N_ZON = 16
N_MER = 8


def draw_obs_count(key, part):
    blocks = N_GRP * N_MER * N_ZON
    first_key, secondary_key = jax.random.split(key)
    counts = jax.random.randint(first_key, (blocks,), 1, CAP + 1)
    chosen = jax.random.randint(secondary_key, (), 0, blocks)
    counts = jnp.where(jnp.arange(blocks) == chosen, CAP, counts)
    return counts.reshape(N_GRP, N_MER, N_ZON).astype(jnp.int32)


def draw_obs_corner(key, part):
    keys = jax.random.split(key, 5)
    full_shape = (N_GRP, N_MER, N_ZON, CAP)
    field_pick = jax.random.randint(keys[0], full_shape, 0, 2)
    level_pick = jax.random.randint(keys[1], full_shape, 0, LEV)
    row_pick = jax.random.randint(keys[2], full_shape, 0, CY - 1)
    column = jax.random.randint(keys[3], full_shape, 0, CX - 1)
    corner = ((field_pick * LEV + level_pick) * CY + row_pick) * CX + column
    flattened = corner.reshape(-1)
    slots = flattened.shape[0]
    high_pos = jax.random.randint(keys[4], (), 0, slots)
    low_pos = (high_pos + 1) % slots
    positions = jnp.arange(slots)
    flattened = jnp.where(positions == high_pos, 2 * LEV * CY * CX - CX - 2, flattened)
    flattened = jnp.where(positions == low_pos, 0, flattened)
    return flattened.reshape(full_shape).astype(jnp.int32)


def draw_obs_weight(key, part):
    first_key, secondary_key = jax.random.split(key)
    full_shape = (N_GRP, N_MER, N_ZON, CAP)
    frac_x = jax.random.uniform(first_key, full_shape, jnp.float32)
    frac_y = jax.random.uniform(secondary_key, full_shape, jnp.float32)
    weights = jnp.stack([(1.0 - frac_x) * (1.0 - frac_y), frac_x * (1.0 - frac_y), (1.0 - frac_x) * frac_y, frac_x * frac_y], axis=3)
    return weights.astype(jnp.float32)


def place_ends(result, own_key, low, top_value):
    index_at = [jax.random.randint(jax.random.fold_in(own_key, axis), (), 0, length) for axis, length in enumerate(result.shape)]
    widest = result.shape.index(max(result.shape))
    beside = index_at[:widest] + [(index_at[widest] + 1) % result.shape[widest]] + index_at[widest + 1:]
    return result.at[tuple(index_at)].set(low).at[tuple(beside)].set(top_value)


def block_scale(own_key, extent, cuts, low, high):
    def one(dim, parts):
        steps = jax.random.uniform(jax.random.fold_in(jax.random.fold_in(own_key, 6), dim), (parts,), jnp.float32, low / len(cuts), high / len(cuts))
        return jnp.repeat(jnp.exp(steps), extent[dim] // parts).reshape((-1,) + (1,) * (len(extent) - dim - 1))

    gain = one(*cuts[0])
    for cut in cuts[1:]:
        gain = gain * one(*cut)
    return gain


def gaussian(own_key, extent, spread, limit, cuts=(), kind=jnp.bfloat16):
    values = jax.random.normal(own_key, extent, jnp.float32) * spread
    if len(cuts) > 0:
        values = block_scale(own_key, extent, cuts, -0.22, 0.18) * values
    return jnp.clip(values, min=-limit, max=limit).astype(kind)


def setup_inputs(seed: int = 0) -> dict:
    key_of = jax.random.split(jax.random.key(seed), 10)
    return {
        "model_state": gaussian(key_of[0], (FIELDS, LEV, NY, NX), 1.0, 4.0, ((1, 2), (2, 8), (3, 16)), jnp.float32),
        "control": gaussian(key_of[1], (FIELDS, LEV, NY, NX), 1.0, 6.0, ((0, 2), (2, 8), (3, 16)), jnp.float32),
        "error_std": jnp.clip(jnp.exp(math.log(3.0) - 2.3025851 * jax.random.uniform(key_of[2], (FIELDS, LEV, NY, NX), jnp.float32) ** block_scale(key_of[2], (FIELDS, LEV, NY, NX), ((0, 2), (2, 8), (3, 16)), -0.2, 0.2)), 0.3, 3.0),
        "bottom_level": place_ends(jax.random.randint(key_of[3], (NY, NX), 0, LEV + 1), jax.random.fold_in(key_of[3], 1), 0, LEV).astype(jnp.int32),
        "obs_count": draw_obs_count(jax.random.fold_in(key_of[9], 71), 0),
        "obs_corner": draw_obs_corner(jax.random.fold_in(key_of[9], 71), 0),
        "obs_weight": draw_obs_weight(jax.random.fold_in(key_of[9], 71), 0),
        "obs_value": gaussian(key_of[7], (N_GRP, N_MER, N_ZON, CAP), 1.0, 5.0, ((0, 2), (1, 8), (2, 16)), jnp.float32),
        "obs_precision": jnp.clip(jnp.exp(math.log(4.0) - 2.7725887 * jax.random.uniform(key_of[8], (N_GRP, N_MER, N_ZON, CAP), jnp.float32) ** block_scale(key_of[8], (N_GRP, N_MER, N_ZON, CAP), ((0, 2), (1, 8), (2, 16)), -0.2, 0.2)), 0.25, 4.0),
    }


SMOOTHING = 0.2
ADVECTION = 0.1
MIXING = 0.15


def extend(field_now, width):
    wrapped = jnp.concatenate([field_now[..., -width:], field_now, field_now[..., :width]], axis=-1)
    padding = [(0, 0)] * (field_now.ndim - 2) + [(width, width), (0, 0)]
    return jnp.pad(wrapped, padding)


def flux_sum(padded, mask_pad):
    centre = padded[..., 1:-1, 1:-1]
    summed = mask_pad[..., 1:-1, 2:] * (padded[..., 1:-1, 2:] - centre)
    summed = summed + mask_pad[..., 1:-1, :-2] * (padded[..., 1:-1, :-2] - centre)
    summed = summed + mask_pad[..., 2:, 1:-1] * (padded[..., 2:, 1:-1] - centre)
    summed = summed + mask_pad[..., :-2, 1:-1] * (padded[..., :-2, 1:-1] - centre)
    return mask_pad[..., 1:-1, 1:-1] * summed


def one_sweep(padded, mask_pad):
    return padded[..., 1:-1, 1:-1] + SMOOTHING * flux_sum(padded, mask_pad)


def reference(model_state, control, error_std, bottom_level, obs_count, obs_corner, obs_weight, obs_value, obs_precision):
    wet_mask = (lax.iota(jnp.int32, LEV)[:, None, None] < bottom_level[None]).astype(jnp.float32)
    mask_one = extend(wet_mask, 1)

    def advance(pieces):
        level_state, depth_level_mask = pieces
        padded = extend(level_state, 1)
        masked = padded * depth_level_mask
        centre = padded[:, 1:-1, 1:-1]
        grad_x = 0.5 * (masked[:, 1:-1, 2:] - masked[:, 1:-1, :-2])
        grad_y = 0.5 * (masked[:, 2:, 1:-1] - masked[:, :-2, 1:-1])
        shifted_values = centre - ADVECTION * (centre[2] * grad_x + centre[3] * grad_y) + MIXING * flux_sum(padded, depth_level_mask)
        return depth_level_mask[1:-1, 1:-1] * shifted_values

    prior_estimate = jnp.moveaxis(lax.map(advance, (jnp.moveaxis(model_state, 1, 0), mask_one)), 0, 1)

    def smooth(field_stack):
        def one_field(field_now):
            return lax.fori_loop(0, SWEEPS, lambda sweep_index, current: one_sweep(extend(current, 1), mask_one), field_now)
        return lax.map(one_field, field_stack)

    pair_index = lax.iota(jnp.int32, N_GRP)[:, None, None, None]
    mer_row = lax.iota(jnp.int32, N_MER)[None, :, None, None]
    zon_col = lax.iota(jnp.int32, N_ZON)[None, None, :, None]
    column = obs_corner % CX
    remainder = obs_corner // CX
    row_pick = remainder % CY
    remainder = remainder // CY
    level_pick = remainder % LEV
    field_pick = remainder // LEV
    global_index = (((2 * pair_index + field_pick) * LEV + level_pick) * NY + mer_row * CY + row_pick) * NX + zon_col * CX + column
    offsets = jnp.array([0, 1, NX, NX + 1], jnp.int32)
    corners = (global_index[..., None, :] + offsets[:, None]).astype(jnp.int32)
    live_slot = (lax.iota(jnp.int32, CAP) < obs_count[..., None]).astype(jnp.float32)

    def observe(field_stack):
        return jnp.sum(obs_weight * field_stack.reshape(-1)[corners], axis=3)

    innovation = live_slot * (obs_value - observe(prior_estimate))
    increment = wet_mask * error_std * smooth(control)
    misfit = live_slot * obs_precision * (observe(increment) - innovation)
    adjoint_obs = jnp.zeros((FIELDS * LEV * NY * NX,), jnp.float32).at[corners.reshape(-1)].add((obs_weight * misfit[..., None, :]).reshape(-1))
    adjoint_obs = adjoint_obs.reshape(control.shape)
    return control + smooth(wet_mask * error_std * adjoint_obs)
```

```python
import functools

import jax
import jax.numpy as jnp
from jax import lax
from jax.experimental import pallas as pl
from jax.experimental.pallas import tpu as pltpu
from jax.sharding import PartitionSpec as P

SWEEPS = 10
SMOOTHING = 0.2
ADVECTION = 0.1
MIXING = 0.15

PAIR = 2
LEVELS = 6
HALF = 3
PLANES = PAIR * LEVELS
ROWS = 64
COLS = 128
HALO = SWEEPS
EDGE = 16
GAP = 2 * HALO
PITCH = COLS + GAP
TILES = -(-PLANES * PITCH // COLS)
BOTTOM_LANE = 240
TALL = ROWS + 2 * EDGE
PAD = 8
DEEP = TALL + 2 * PAD
TRAVEL = jnp.bfloat16
F32 = jnp.float32


def lanes(rows):
    return lax.broadcasted_iota(jnp.int32, (rows, COLS), 1)


def between(lane, low, high):
    if low <= 0:
        return lane < high
    if high >= COLS:
        return lane >= low
    return (lane >= low) & (lane < high)


def roll(value, shift):
    shift %= COLS
    return value if shift == 0 else pltpu.roll(value, shift, 1)


def runs(tile, source):
    found = []
    for lane in range(COLS):
        where = source(tile * COLS + lane)
        if found and found[-1][0] == where:
            found[-1][2] = lane + 1
        else:
            found.append([where, lane, lane + 1])
    return found


def value_source(at):
    plane, inside = divmod(at, PITCH)
    if plane >= PLANES:
        return None
    if inside < HALO:
        return ("halo", (GAP * plane + inside) // COLS)
    if inside >= HALO + COLS:
        return ("halo", (GAP * plane + inside - COLS) // COLS)
    return ("core", plane)


def depth_source(at):
    plane, inside = divmod(at, PITCH)
    return None if plane >= PLANES else (plane, inside // COLS)


def core_place(plane):
    return divmod(plane * PITCH + HALO, COLS)


def strips(read, lane, east, west):
    for plane in range(PLANES):
        turned = roll(read(plane), GAP * plane + HALO)
        for half, start in ((east, GAP * plane), (west, GAP * plane + HALO)):
            for part in range(2):
                low = max(start - part * COLS, 0)
                high = min(start + HALO - part * COLS, COLS)
                if low < high:
                    half[part] = jnp.where(between(lane, low, high), turned, half[part])
    return east, west


def send_strips(east, west, even, first_ref, second_ref):
    for part in range(2):
        here = slice(part * COLS, (part + 1) * COLS)
        first_ref[:, here] = jnp.where(even, east[part], west[part]).astype(TRAVEL)
        second_ref[:, here] = jnp.where(even, west[part], east[part]).astype(TRAVEL)


def zonal_even():
    return lax.axis_index("zon") % 2 == 0


def meridional_even():
    return lax.axis_index("mer") % 2 == 0


def sides(first, second, even):
    first, second = first.astype(F32), second.astype(F32)
    return jnp.where(even, second, first), jnp.where(even, first, second)


def pack_kernel(model_ref, control_ref, bottom_ref, first_ref, second_ref):
    lane = lanes(ROWS)
    blank = jnp.zeros((ROWS, COLS), F32)
    east, west = strips(
        lambda p: control_ref[p // LEVELS, p % LEVELS], lane, [blank, blank], [blank, blank]
    )
    depth = bottom_ref[...].astype(F32)
    low = BOTTOM_LANE - COLS
    mark = between(lane, low, low + HALO)
    east[1] = jnp.where(mark, roll(depth, low - (COLS - HALO)), east[1])
    west[1] = jnp.where(mark, roll(depth, low), west[1])
    for q in range(4 * HALF):
        value = model_ref[q // HALF, q % HALF]
        for half, column, start in (
            (east, value[:, COLS - 1 :], GAP * q + 15),
            (west, value[:, :1], GAP * q + 5),
        ):
            part, at = divmod(start, COLS)
            coarse = column.astype(TRAVEL).astype(F32)
            half[part] = jnp.where(lane == at, coarse, half[part])
            half[part] = jnp.where(lane == at + 1, column - coarse, half[part])
    send_strips(east, west, zonal_even(), first_ref, second_ref)


def place(read, first_ref, second_ref, even, lane, x_ref):
    before, after, both = [], [], []
    for part in range(2):
        here = slice(part * COLS, (part + 1) * COLS)
        low, high = sides(first_ref[:, here], second_ref[:, here], even)
        before.append(low)
        after.append(high)
        both.append(jnp.where((lane + part * COLS) % GAP < HALO, low, high))
    turned = {}
    for tile in range(TILES):
        value = jnp.zeros((ROWS, COLS), F32)
        for source, low, high in runs(tile, value_source):
            if source is None:
                continue
            kind, index = source
            if kind == "core":
                if index not in turned:
                    turned[index] = roll(read(index), GAP * index + HALO)
                piece = turned[index]
            else:
                piece = both[index]
            whole = low == 0 and high == COLS
            value = piece if whole else jnp.where(between(lane, low, high), piece, value)
        x_ref[tile] = value
    return before, after


def edge_rows(even):
    return (
        pl.multiple_of(jnp.where(even, ROWS - EDGE, 0), EDGE),
        pl.multiple_of(jnp.where(even, 0, ROWS - EDGE), EDGE),
    )


def widen_kernel(
    model_ref, control_ref, bottom_ref, first_ref, second_ref, x_ref, depth_ref, a_ref, b_ref, rows_ref
):
    lane = lanes(ROWS)
    before, after = place(
        lambda p: control_ref[p // LEVELS, p % LEVELS], first_ref, second_ref, zonal_even(), lane, x_ref
    )
    depth = roll(bottom_ref[...].astype(F32), HALO)
    low = BOTTOM_LANE - COLS
    depth_ref[0] = jnp.where(lane < HALO, roll(before[1], -low), depth)
    depth_ref[1] = jnp.where(
        lane < HALO, depth, jnp.where(lane < GAP, roll(after[1], HALO - low), 0.0)
    )
    even = meridional_even()
    for start, row, out_ref in zip(
        edge_rows(even), (jnp.where(even, ROWS - 1, 0), jnp.where(even, 0, ROWS - 1)), (a_ref, b_ref)
    ):
        for tile in range(TILES):
            out_ref[tile] = x_ref[tile, pl.ds(start, EDGE), :].astype(TRAVEL)
        for part in range(2):
            out_ref[TILES + part] = depth_ref[part, pl.ds(start, EDGE), :].astype(TRAVEL)
        rows_ref[...] = jnp.zeros((EDGE, COLS), F32)
        for q in range(4 * HALF):
            rows_ref[q : q + 1, :] = model_ref[q // HALF, q % HALF, pl.ds(row, 1), :]
        value = rows_ref[...]
        coarse = value.astype(TRAVEL)
        out_ref[TILES + 2] = coarse
        out_ref[TILES + 3] = (value - coarse.astype(F32)).astype(TRAVEL)


def rewiden_kernel(field_ref, first_ref, second_ref, x_ref, a_ref, b_ref):
    place(lambda p: field_ref[p], first_ref, second_ref, zonal_even(), lanes(ROWS), x_ref)
    for start, out_ref in zip(edge_rows(meridional_even()), (a_ref, b_ref)):
        for tile in range(TILES):
            out_ref[tile] = x_ref[tile, pl.ds(start, EDGE), :].astype(TRAVEL)


def background_kernel(
    model_ref, bottom_ref, first_ref, second_ref, depth_ref, a_ref, b_ref, keep_ref, send_ref, tall_ref
):
    lane = lanes(ROWS)
    group = lax.axis_index("grp")
    even_zon, even_mer = zonal_even(), meridional_even()
    before, after = [], []
    for part in range(2):
        here = slice(part * COLS, (part + 1) * COLS)
        low, high = sides(first_ref[:, here], second_ref[:, here], even_zon)
        before.append(low)
        after.append(high)

    def halo_rows(index):
        return sides(a_ref[index], b_ref[index], even_mer)

    def stand(value, above, below):
        tall_ref[8 : 8 + ROWS, :] = value
        tall_ref[7:8, :] = above
        tall_ref[8 + ROWS : 9 + ROWS, :] = below
        return tall_ref[7 : 7 + ROWS, :], tall_ref[9 : 9 + ROWS, :]

    depth = bottom_ref[...].astype(F32)
    depth_east = jnp.where(lane == COLS - 1, roll(depth_ref[1], COLS - 1 - HALO), roll(depth, -1))
    depth_west = jnp.where(lane == 0, roll(depth_ref[0], 1 - HALO), roll(depth, 1))
    edge_lane = lanes(EDGE)
    flat = [
        jnp.where(edge_lane < COLS - HALO, roll(main, -HALO), roll(rest, -HALO))
        for main, rest in zip(halo_rows(TILES), halo_rows(TILES + 1))
    ]
    depth_below, depth_above = stand(depth, flat[0][EDGE - 1 :], flat[1][:1])
    coarse, fine = halo_rows(TILES + 2), halo_rows(TILES + 3)
    low_rows, high_rows = coarse[0] + fine[0], coarse[1] + fine[1]
    for level in range(HALF):
        here = (group * HALF + level).astype(F32)
        wet, wet_e, wet_w, wet_n, wet_s = (
            jnp.where(value > here, 1.0, 0.0)
            for value in (depth, depth_east, depth_west, depth_above, depth_below)
        )
        flow_x, flow_y = model_ref[2, level], model_ref[3, level]
        for field in range(4):
            q = field * HALF + level
            value = model_ref[field, level]
            part, at = divmod(GAP * q + 5, COLS)
            column = after[part][:, at : at + 1] + after[part][:, at + 1 : at + 2]
            east = jnp.where(lane == COLS - 1, column, roll(value, -1))
            part, at = divmod(GAP * q + 15, COLS)
            column = before[part][:, at : at + 1] + before[part][:, at + 1 : at + 2]
            west = jnp.where(lane == 0, column, roll(value, 1))
            south, north = stand(value, low_rows[q : q + 1], high_rows[q : q + 1])
            grad_x = 0.5 * (wet_e * east - wet_w * west)
            grad_y = 0.5 * (wet_n * north - wet_s * south)
            flux = (
                wet_e * (east - value)
                + wet_w * (west - value)
                + wet_n * (north - value)
                + wet_s * (south - value)
            )
            result = wet * (
                value - ADVECTION * (flow_x * grad_x + flow_y * grad_y) + MIXING * (wet * flux)
            )
            own = group == field // 2

            @pl.when(own)
            def _():
                keep_ref[field % 2, level] = result

            @pl.when(jnp.logical_not(own))
            def _():
                send_ref[field % 2, level] = result


def neighbour_sums(read, start, rows, use):
    lane = lanes(rows)
    first, last = lane == 0, lane == COLS - 1
    turned = {}

    def turn(tile, shift):
        tile %= TILES
        if (tile, shift) not in turned:
            turned[tile, shift] = roll(read(tile, start, rows), shift)
        return turned[tile, shift]

    for tile in range(TILES):
        centre = read(tile, start, rows)
        east = jnp.where(last, turn(tile + 1, -1), turn(tile, -1))
        west = jnp.where(first, turn(tile - 1, 1), turn(tile, 1))
        total = (east + west) + (read(tile, start - 1, rows) + read(tile, start + 1, rows))
        use(tile, centre, total)


def sweep_all(wide_ref, keep_ref, give_ref):
    def sweep(source, target, start, rows):
        def read(tile, at, count):
            return wide_ref[source, tile, pl.ds(at, count), :]

        def use(tile, centre, total):
            here = pl.ds(start, rows)
            wide_ref[target, tile, here, :] = (
                keep_ref[tile, here, :] * centre + give_ref[tile, here, :] * total
            )

        neighbour_sums(read, start, rows, use)

    sweep(0, 1, PAD, TALL)

    def step(index, carry):
        source = (index + 1) % 2
        sweep(source, 1 - source, 2 * PAD, TALL - 2 * PAD)
        return carry

    lax.fori_loop(0, SWEEPS - 1, step, 0)


def fill_wide(x_ref, a_ref, b_ref, wide_ref, mask_ref):
    even = meridional_even()
    for tile in range(TILES):
        low, high = sides(a_ref[tile], b_ref[tile], even)
        value = jnp.concatenate([low, x_ref[tile], high], axis=0)
        if mask_ref is not None:
            value = value * mask_ref[tile, PAD : PAD + TALL, :]
        wide_ref[0, tile, PAD : PAD + TALL, :] = value


def plane_of(wide_ref, plane, lane):
    tile, offset = core_place(plane)
    here = slice(PAD + EDGE, PAD + EDGE + ROWS)
    value = wide_ref[0, tile, here, :]
    if offset:
        value = jnp.where(lane >= offset, value, wide_ref[0, tile + 1, here, :])
    return roll(value, -offset)


def smooth_kernel(x_ref, depth_ref, a_ref, b_ref, out_ref, keep_ref, give_ref, wide_ref, mask_ref):
    even = meridional_even()
    tall_lane = lanes(TALL)
    low = [sides(a_ref[TILES + part], b_ref[TILES + part], even) for part in range(2)]
    depth = [jnp.concatenate([low[p][0], depth_ref[p], low[p][1]], axis=0) for p in range(2)]
    for tile in range(TILES):
        value = jnp.zeros((TALL, COLS), F32)
        for source, start, stop in runs(tile, depth_source):
            if source is None:
                continue
            plane, part = source
            wet = jnp.where(roll(depth[part], GAP * plane) > (plane % LEVELS), 1.0, 0.0)
            value = jnp.where(between(tall_lane, start, stop), wet, value)
        mask_ref[tile, :PAD, :] = jnp.zeros((PAD, COLS), F32)
        mask_ref[tile, PAD + TALL :, :] = jnp.zeros((PAD, COLS), F32)
        mask_ref[tile, PAD : PAD + TALL, :] = value

    def use(tile, centre, total):
        here = slice(PAD, PAD + TALL)
        keep_ref[tile, here, :] = centre * (1.0 - SMOOTHING * total)
        give_ref[tile, here, :] = SMOOTHING * centre

    neighbour_sums(lambda t, at, n: mask_ref[t, at : at + n, :], PAD, TALL, use)
    fill_wide(x_ref, a_ref, b_ref, wide_ref, mask_ref)
    sweep_all(wide_ref, keep_ref, give_ref)
    lane = lanes(ROWS)
    for plane in range(PLANES):
        out_ref[plane] = plane_of(wide_ref, plane, lane)


def gradient_kernel(x_ref, a_ref, b_ref, keep_ref, give_ref, control_ref, out_ref, wide_ref):
    fill_wide(x_ref, a_ref, b_ref, wide_ref, None)
    sweep_all(wide_ref, keep_ref, give_ref)
    lane = lanes(ROWS)
    for plane in range(PLANES):
        f, k = divmod(plane, LEVELS)
        out_ref[f, k] = control_ref[f, k] + plane_of(wide_ref, plane, lane)


def split(value):
    coarse = value.astype(jnp.bfloat16)
    return jnp.concatenate([coarse, (value - coarse.astype(F32)).astype(jnp.bfloat16)], axis=1)


def join(value):
    return value[:, :COLS] + value[:, COLS:]


def observe_kernel(
    count_ref,
    smooth_ref,
    error_ref,
    bottom_ref,
    keep_ref,
    other_ref,
    corner_ref,
    weight_ref,
    value_ref,
    precision_ref,
    field_ref,
    first_ref,
    second_ref,
    total_ref,
):
    group = lax.axis_index("grp")
    slots = corner_ref.shape[-1]
    depth = bottom_ref[...]
    for plane in range(PLANES):
        f, k = divmod(plane, LEVELS)
        scale = jnp.where(depth > k, error_ref[f, k], 0.0)
        held = group == k // HALF
        prior = jnp.where(held, keep_ref[f, k % HALF], other_ref[f, k % HALF])
        total_ref[plane * ROWS : (plane + 1) * ROWS, :] = scale * smooth_ref[plane] + prior
    corner = corner_ref[0, 0]
    row = (corner >> 7).astype(F32)
    column = (corner & (COLS - 1)).astype(F32)
    stacked = jnp.concatenate(
        [weight_ref[0, 0, 0], value_ref[0, 0], precision_ref[0, 0], row, column], axis=0
    )
    tall = jnp.transpose(stacked)
    row_tall = jnp.concatenate([tall[:, 6:7], tall[:, 6:7] + 1.0], axis=0)
    cells = PLANES * ROWS
    wide_row = lax.broadcasted_iota(jnp.int32, (2 * slots, cells), 1).astype(F32)
    pick = jnp.where(wide_row == row_tall, 1.0, 0.0).astype(jnp.bfloat16)
    seen = join(jnp.dot(pick, split(total_ref[...]), preferred_element_type=F32))
    lane = lanes(slots).astype(F32)
    at, beside = lane == tall[:, 7:8], lane == tall[:, 7:8] + 1.0
    lower = jnp.where(at, tall[:, 0:1], jnp.where(beside, tall[:, 1:2], 0.0))
    upper = jnp.where(at, tall[:, 2:3], jnp.where(beside, tall[:, 3:4], 0.0))
    observed = jnp.sum(lower * seen[:slots] + upper * seen[slots:], axis=1, keepdims=True)
    live = lax.broadcasted_iota(jnp.int32, (slots, 1), 0) < count_ref[0, 0, 0]
    misfit = jnp.where(live, tall[:, 5:6] * (observed - tall[:, 4:5]), 0.0)
    spread = jnp.concatenate([lower * misfit, upper * misfit], axis=0)
    tall_row = lax.broadcasted_iota(jnp.int32, (cells, slots), 0).astype(F32)
    back = jnp.concatenate(
        [
            jnp.where(tall_row == row, 1.0, 0.0).astype(jnp.bfloat16),
            jnp.where(tall_row == row + 1.0, 1.0, 0.0).astype(jnp.bfloat16),
        ],
        axis=1,
    )
    total_ref[...] = join(jnp.dot(back, split(spread), preferred_element_type=F32))
    for plane in range(PLANES):
        f, k = divmod(plane, LEVELS)
        scale = jnp.where(depth > k, error_ref[f, k], 0.0)
        field_ref[plane] = scale * total_ref[plane * ROWS : (plane + 1) * ROWS, :]
    blank = jnp.zeros((ROWS, COLS), F32)
    east, west = strips(
        lambda p: field_ref[p], lanes(ROWS), [blank, blank], [blank, blank]
    )
    send_strips(east, west, zonal_even(), first_ref, second_ref)


def call(kernel, outs, scratch=(), scalars=0, name=None):
    def run(*args):
        return pl.pallas_call(
            kernel,
            out_shape=[jax.ShapeDtypeStruct(shape, kind) for shape, kind in outs],
            in_specs=[
                pl.BlockSpec(memory_space=pltpu.SMEM if i < scalars else pltpu.VMEM)
                for i in range(len(args))
            ],
            out_specs=[pl.BlockSpec(memory_space=pltpu.VMEM) for _ in outs],
            scratch_shapes=[pltpu.VMEM(shape, kind) for shape, kind in scratch],
            compiler_params=pltpu.CompilerParams(vmem_limit_bytes=24 * 2**20),
            name=name,
        )(*args)

    return run


def swap(value, axis, shift, wrap):
    size = lax.axis_size(axis)
    pairs = []
    for i in range(shift, size + shift - 1, 2):
        j = i + 1
        if j < size or wrap:
            pairs += [(i, j % size), (j % size, i)]
    return lax.ppermute(value, axis, pairs)


def exchange(first, second, axis, wrap):
    return swap(first, axis, 0, wrap), swap(second, axis, 1, wrap)


ZONAL = ((ROWS, 2 * COLS), TRAVEL)
WIDE = ((TILES, ROWS, COLS), F32)


def body(
    model_state,
    control,
    error_std,
    bottom_level,
    obs_count,
    obs_corner,
    obs_weight,
    obs_value,
    obs_precision,
):
    first, second = call(pack_kernel, [ZONAL, ZONAL], name="pack")(
        model_state, control, bottom_level
    )
    zon = exchange(first, second, "zon", True)
    message = ((TILES + 4, EDGE, COLS), TRAVEL)
    x, depth, first, second = call(
        widen_kernel,
        [WIDE, ((2, ROWS, COLS), F32), message, message],
        [((EDGE, COLS), F32)],
        name="widen",
    )(model_state, control, bottom_level, *zon)
    mer = exchange(first, second, "mer", False)
    part = ((PAIR, HALF, ROWS, COLS), F32)
    keep, send = call(
        background_kernel, [part, part], [((ROWS + 16, COLS), F32)], name="background"
    )(model_state, bottom_level, *zon, depth, *mer)
    other = lax.ppermute(send, "grp", [(0, 1), (1, 0)])
    deep = ((TILES, DEEP, COLS), F32)
    smoothed, keep_coef, give_coef = call(
        smooth_kernel,
        [((PLANES, ROWS, COLS), F32), deep, deep],
        [((2, TILES, DEEP, COLS), F32), deep],
        name="smooth",
    )(x, depth, *mer)
    field, first, second = call(
        observe_kernel,
        [((PLANES, ROWS, COLS), F32), ZONAL, ZONAL],
        [((PLANES * ROWS, COLS), F32)],
        scalars=1,
        name="observe",
    )(
        obs_count,
        smoothed,
        error_std,
        bottom_level,
        keep,
        other,
        obs_corner,
        obs_weight,
        obs_value,
        obs_precision,
    )
    zon = exchange(first, second, "zon", True)
    message = ((TILES, EDGE, COLS), TRAVEL)
    x, first, second = call(rewiden_kernel, [WIDE, message, message], name="rewiden")(field, *zon)
    mer = exchange(first, second, "mer", False)
    return call(
        gradient_kernel,
        [(control.shape, F32)],
        [((2, TILES, DEEP, COLS), F32)],
        name="gradient",
    )(x, *mer, keep_coef, give_coef, control)[0]


def solution(mesh):
    return jax.shard_map(
        body,
        mesh=mesh,
        in_specs=(
            P(None, "grp", "mer", "zon"),
            P("grp", None, "mer", "zon"),
            P("grp", None, "mer", "zon"),
            P("mer", "zon"),
            P("grp", "mer", "zon"),
            P("grp", "mer", "zon", None),
            P("grp", "mer", "zon", None, None),
            P("grp", "mer", "zon", None),
            P("grp", "mer", "zon", None),
        ),
        out_specs=P("grp", None, "mer", "zon"),
        check_vma=False,
    )
```

```python
import jax
import jax.numpy as jnp
from jax import lax
from jax.experimental import pallas as pl
from jax.experimental.pallas import tpu as pltpu
from jax.sharding import PartitionSpec as P

SWEEPS = 10
SMOOTHING = 0.2
ADVECTION = 0.1
MIXING = 0.15

PAIR = 2
LEVELS = 6
HALF = 3
FIELDS = 4
PLANES = PAIR * LEVELS
STEPPED = FIELDS * HALF
ROWS = 64
COLS = 128
HALO = SWEEPS
EDGE = 16
TALL = ROWS + 2 * EDGE
PAD = 8
DEEP = TALL + 2 * PAD
BAND = 3 * HALO
LANES = COLS // BAND
BANDS = PLANES // LANES
DEPTH_ROW = PLANES * HALO
MODEL_ROW = DEPTH_ROW + HALO
LONG = 160
SHORT = 128
MODEL_LANE = 16
TRAVEL = jnp.bfloat16
F32 = jnp.float32
VMEM = pltpu.VMEM


def lanes(rows):
    return lax.broadcasted_iota(jnp.int32, (rows, COLS), 1)


def window(lane, start, width):
    start %= COLS
    stop = start + width
    if stop > COLS:
        return (lane >= start) | (lane < stop - COLS)
    return (lane >= start) & (lane < stop)


def roll(value, shift):
    shift %= COLS
    return value if shift == 0 else pltpu.roll(value, shift, 1)


def even_on(axis):
    return lax.axis_index(axis) % 2 == 0


def sides(first, second, even):
    first, second = first.astype(F32), second.astype(F32)
    return jnp.where(even, second, first), jnp.where(even, first, second)


def turn(plane):
    return BAND * (plane % LANES) + 2 * HALO


def stage(low_ref, high_ref, low, high):
    for plane in range(PLANES):
        here = slice(plane * HALO, (plane + 1) * HALO)
        low_ref[here, :] = low(plane)
        high_ref[here, :] = high(plane)


def send_rows(low_ref, high_ref, first_ref, second_ref):
    even = even_on("mer")
    low, high = low_ref[...], high_ref[...]
    first_ref[...] = jnp.where(even, high, low).astype(TRAVEL)
    second_ref[...] = jnp.where(even, low, high).astype(TRAVEL)


def start_kernel(
    model_ref,
    control_ref,
    bottom_ref,
    first_ref,
    second_ref,
    control_low,
    control_high,
    model_low,
    model_high,
    bottom_low,
    bottom_high,
    low_ref,
    high_ref,
    sems,
):
    ends = pl.ds(0, EDGE), pl.ds(ROWS - EDGE, EDGE)
    tips = pl.ds(0, 8), pl.ds(ROWS - 8, 8)
    copies = [
        pltpu.make_async_copy(control_ref.at[:, :, ends[0], :], control_low, sems.at[0]),
        pltpu.make_async_copy(control_ref.at[:, :, ends[1], :], control_high, sems.at[1]),
        pltpu.make_async_copy(model_ref.at[:, :, tips[0], :], model_low, sems.at[2]),
        pltpu.make_async_copy(model_ref.at[:, :, tips[1], :], model_high, sems.at[3]),
        pltpu.make_async_copy(bottom_ref.at[ends[0], :], bottom_low, sems.at[4]),
        pltpu.make_async_copy(bottom_ref.at[ends[1], :], bottom_high, sems.at[5]),
    ]
    for copy in copies:
        copy.start()
    for copy in copies:
        copy.wait()
    stage(
        low_ref,
        high_ref,
        lambda p: control_low[p // LEVELS, p % LEVELS, :HALO, :],
        lambda p: control_high[p // LEVELS, p % LEVELS, EDGE - HALO :, :],
    )
    low_ref[DEPTH_ROW:MODEL_ROW, :] = bottom_low[:HALO, :].astype(F32)
    high_ref[DEPTH_ROW:MODEL_ROW, :] = bottom_high[EDGE - HALO :, :].astype(F32)
    for q in range(STEPPED):
        for ref, value in (
            (low_ref, model_low[q // HALF, q % HALF, :1, :]),
            (high_ref, model_high[q // HALF, q % HALF, 7:, :]),
        ):
            coarse = value.astype(TRAVEL).astype(F32)
            at = MODEL_ROW + q
            ref[at : at + 1, :] = coarse
            ref[at + STEPPED : at + STEPPED + 1, :] = value - coarse
    rest = MODEL_ROW + 2 * STEPPED
    low_ref[rest:, :] = jnp.zeros((LONG - rest, COLS), F32)
    high_ref[rest:, :] = jnp.zeros((LONG - rest, COLS), F32)
    send_rows(low_ref, high_ref, first_ref, second_ref)


def stand(value, low, high):
    blank = jnp.zeros((EDGE - HALO, COLS), F32)
    return jnp.concatenate([blank, low, value, high, blank], axis=0)


def raise_planes(read, first_ref, second_ref, low_ref, high_ref, tall_ref):
    low, high = sides(first_ref[...], second_ref[...], even_on("mer"))
    low_ref[...] = low
    high_ref[...] = high
    blank = jnp.zeros((EDGE - HALO, COLS), F32)
    for plane in range(PLANES):
        here = slice(plane * HALO, (plane + 1) * HALO)
        tall_ref[plane, : EDGE - HALO, :] = blank
        tall_ref[plane, EDGE - HALO : EDGE, :] = low_ref[here, :]
        tall_ref[plane, EDGE : EDGE + ROWS, :] = read(plane)
        tall_ref[plane, EDGE + ROWS : EDGE + ROWS + HALO, :] = high_ref[here, :]
        tall_ref[plane, EDGE + ROWS + HALO :, :] = blank


def cut_bands(tall_ref, west_ref, east_ref):
    lane = lanes(TALL)
    blank = jnp.zeros((TALL, COLS), F32)
    to_east, to_west = blank, blank
    for group in range(BANDS):
        west = east = go_east = go_west = blank
        for j in range(LANES):
            plane = group * LANES + j
            turned = roll(tall_ref[plane], turn(plane))
            at = BAND * j
            west = jnp.where(window(lane, at + 2 * HALO, 2 * HALO), turned, west)
            east = jnp.where(window(lane, at, 2 * HALO), turned, east)
            go_east = jnp.where(window(lane, at + HALO, HALO), turned, go_east)
            go_west = jnp.where(window(lane, at + 2 * HALO, HALO), turned, go_west)
        west_ref[group] = west
        east_ref[group] = east
        to_east = to_east + roll(go_east, HALO * group)
        to_west = to_west + roll(go_west, HALO * group)
    return to_east, to_west


def send_columns(part, to_east, to_west, first_ref, second_ref):
    even = even_on("zon")
    here = slice(part * COLS, (part + 1) * COLS)
    first_ref[:, here] = jnp.where(even, to_east, to_west).astype(TRAVEL)
    second_ref[:, here] = jnp.where(even, to_west, to_east).astype(TRAVEL)


def first_columns_kernel(
    model_ref,
    control_ref,
    bottom_ref,
    a_ref,
    b_ref,
    tall_ref,
    depth_ref,
    west_ref,
    east_ref,
    first_ref,
    second_ref,
    low_ref,
    high_ref,
):
    raise_planes(
        lambda p: control_ref[p // LEVELS, p % LEVELS], a_ref, b_ref, low_ref, high_ref, tall_ref
    )
    send_columns(0, *cut_bands(tall_ref, west_ref, east_ref), first_ref, second_ref)
    depth = stand(
        bottom_ref[...].astype(F32),
        low_ref[DEPTH_ROW:MODEL_ROW, :],
        high_ref[DEPTH_ROW:MODEL_ROW, :],
    )
    depth_ref[...] = depth
    tall_lane = lanes(TALL)
    lane = lanes(ROWS)
    to_east = to_west = jnp.zeros((ROWS, COLS), F32)
    for q in range(STEPPED):
        value = model_ref[q // HALF, q % HALF]
        at = MODEL_LANE + 2 * q
        column = value[:, COLS - 1 :]
        coarse = column.astype(TRAVEL).astype(F32)
        to_east = jnp.where(lane == at, coarse, to_east)
        to_east = jnp.where(lane == at + 1, column - coarse, to_east)
        column = value[:, :1]
        coarse = column.astype(TRAVEL).astype(F32)
        to_west = jnp.where(lane == at - 1, coarse, to_west)
        to_west = jnp.where(lane == at - 2, column - coarse, to_west)
    blank = jnp.zeros((EDGE, COLS), F32)
    mark = tall_lane < HALO
    send_columns(
        1,
        jnp.where(mark, roll(depth, HALO), jnp.concatenate([blank, to_east, blank], axis=0)),
        jnp.where(mark, depth, jnp.concatenate([blank, to_west, blank], axis=0)),
        first_ref,
        second_ref,
    )


def next_columns_kernel(
    field_ref, a_ref, b_ref, tall_ref, west_ref, east_ref, first_ref, second_ref, low_ref, high_ref
):
    raise_planes(lambda p: field_ref[p], a_ref, b_ref, low_ref, high_ref, tall_ref)
    send_columns(0, *cut_bands(tall_ref, west_ref, east_ref), first_ref, second_ref)


def base_step(model_ref, depth_ref, a_ref, b_ref, base_ref, low_ref, high_ref, tall_ref):
    lane = lanes(ROWS)
    group = lax.axis_index("grp")
    low, high = sides(a_ref[...], b_ref[...], even_on("mer"))
    low_ref[...] = low
    high_ref[...] = high
    core = slice(EDGE, EDGE + ROWS)
    south, north = slice(EDGE - 1, EDGE + ROWS - 1), slice(EDGE + 1, EDGE + ROWS + 1)
    depth = depth_ref[core, :]
    around = (
        depth,
        jnp.where(lane == COLS - 1, 0.0, roll(depth, -1)),
        jnp.where(lane == 0, 0.0, roll(depth, 1)),
        depth_ref[north, :],
        depth_ref[south, :],
    )
    for level in range(HALF):
        here = (group * HALF + level).astype(F32)
        wet, wet_e, wet_w, wet_n, wet_s = (jnp.where(v > here, 1.0, 0.0) for v in around)
        count = MIXING * (wet_e + wet_w + wet_n + wet_s)
        flow_x = 0.5 * ADVECTION * model_ref[2, level]
        flow_y = 0.5 * ADVECTION * model_ref[3, level]
        give_e, give_w = wet_e * (MIXING - flow_x), wet_w * (MIXING + flow_x)
        give_n, give_s = wet_n * (MIXING - flow_y), wet_s * (MIXING + flow_y)
        for field in range(FIELDS):
            at = MODEL_ROW + field * HALF + level
            value = model_ref[field, level]
            tall_ref[8 : 8 + ROWS, :] = value
            tall_ref[7:8, :] = low_ref[at : at + 1, :] + low_ref[at + STEPPED : at + STEPPED + 1, :]
            tall_ref[8 + ROWS : 9 + ROWS, :] = (
                high_ref[at : at + 1, :] + high_ref[at + STEPPED : at + STEPPED + 1, :]
            )
            base_ref[field, level] = wet * (
                value * (1.0 - count)
                + give_e * roll(value, -1)
                + give_w * roll(value, 1)
                + give_n * tall_ref[9 : 9 + ROWS, :]
                + give_s * tall_ref[7 : 7 + ROWS, :]
            )


def background_kernel(model_ref, depth_ref, base_ref, first_ref, second_ref, keep_ref, send_ref):
    lane = lanes(ROWS)
    group = lax.axis_index("grp")
    core = slice(EDGE, EDGE + ROWS)
    before, after = sides(first_ref[core, COLS:], second_ref[core, COLS:], even_on("zon"))
    at_west, at_east = lane == 0, lane == COLS - 1
    beside = jnp.where(at_west, roll(before, 1 - HALO), jnp.where(at_east, roll(after, -1), 0.0))
    depth = jnp.minimum(depth_ref[core, :], beside)
    columns = jnp.where(lane % 2 == 0, before + roll(before, -1), after + roll(after, 1))
    sign = jnp.where(at_west, 0.5 * ADVECTION, -0.5 * ADVECTION)
    for level in range(HALF):
        wet = depth > (group * HALF + level).astype(F32)
        gain = jnp.where(wet, MIXING + sign * model_ref[2, level], 0.0)
        loss = jnp.where(wet, MIXING, 0.0)
        for field in range(FIELDS):
            halo = roll(columns, -(MODEL_LANE + 2 * (field * HALF + level)))
            result = base_ref[field, level] + (gain * halo - loss * model_ref[field, level])
            own = group == field // 2

            @pl.when(own)
            def _():
                keep_ref[field % 2, level] = result

            @pl.when(jnp.logical_not(own))
            def _():
                send_ref[field % 2, level] = result


def neighbour_sum(ref, index, start, rows):
    here = ref[index, pl.ds(start, rows), :]
    return here, (roll(here, -1) + roll(here, 1)) + (
        ref[index, pl.ds(start - 1, rows), :] + ref[index, pl.ds(start + 1, rows), :]
    )


def coefficients(mask_ref, count, keep_ref, give_ref):
    for index in range(count):
        wet, total = neighbour_sum(mask_ref, index, PAD, TALL)
        keep_ref[index, PAD : PAD + TALL, :] = wet * (1.0 - SMOOTHING * total)
        give_ref[index, PAD : PAD + TALL, :] = SMOOTHING * wet


def sweep_all(count, masks, keep_ref, give_ref, one_ref, two_ref):
    def sweep(source_ref, target_ref, start, rows):
        for index in range(count):
            here, total = neighbour_sum(source_ref, index, start, rows)
            at = pl.ds(start, rows)
            target_ref[index, at, :] = (
                keep_ref[index % masks, at, :] * here + give_ref[index % masks, at, :] * total
            )

    sweep(one_ref, two_ref, PAD, TALL)
    sweep(two_ref, one_ref, 2 * PAD, TALL - 2 * PAD)

    def step(index, carry):
        sweep(one_ref, two_ref, 2 * PAD, TALL - 2 * PAD)
        sweep(two_ref, one_ref, 2 * PAD, TALL - 2 * PAD)
        return carry

    lax.fori_loop(0, SWEEPS // 2 - 1, step, 0)


def clear_pads(ref, count):
    for index in range(count):
        ref[index, :PAD, :] = jnp.zeros((PAD, COLS), F32)
        ref[index, PAD + TALL :, :] = jnp.zeros((PAD, COLS), F32)


CORE = slice(PAD + EDGE, PAD + EDGE + ROWS)
BODY = slice(PAD, PAD + TALL)


def first_interior_kernel(
    tall_ref,
    depth_ref,
    model_ref,
    a_ref,
    b_ref,
    inner_ref,
    keep_ref,
    give_ref,
    base_ref,
    mask_ref,
    one_ref,
    two_ref,
    low_ref,
    high_ref,
    stand_ref,
):
    base_step(model_ref, depth_ref, a_ref, b_ref, base_ref, low_ref, high_ref, stand_ref)
    clear_pads(mask_ref, LEVELS)
    clear_pads(one_ref, PLANES)
    depth = depth_ref[...]
    for level in range(LEVELS):
        wet = jnp.where(depth > level, 1.0, 0.0)
        mask_ref[level, BODY, :] = wet
        for field in range(PAIR):
            plane = field * LEVELS + level
            one_ref[plane, BODY, :] = wet * tall_ref[plane]
    coefficients(mask_ref, LEVELS, keep_ref, give_ref)
    sweep_all(PLANES, LEVELS, keep_ref, give_ref, one_ref, two_ref)
    for plane in range(PLANES):
        inner_ref[plane] = one_ref[plane, CORE, :]


def next_interior_kernel(tall_ref, keep_ref, give_ref, inner_ref, one_ref, two_ref):
    clear_pads(one_ref, PLANES)
    for plane in range(PLANES):
        one_ref[plane, BODY, :] = tall_ref[plane]
    sweep_all(PLANES, LEVELS, keep_ref, give_ref, one_ref, two_ref)
    for plane in range(PLANES):
        inner_ref[plane] = one_ref[plane, CORE, :]


def fill_bands(first_ref, second_ref, west_ref, east_ref, one_ref, mask_ref):
    lane = lanes(TALL)
    before, after = sides(first_ref[:, :COLS], second_ref[:, :COLS], even_on("zon"))
    clear_pads(one_ref, 2 * BANDS)
    in_west = (lane >= HALO) & ((lane - HALO) % BAND < HALO)
    in_east = (lane >= 2 * HALO) & ((lane - 2 * HALO) % BAND < HALO)
    for group in range(BANDS):
        west = jnp.where(in_west, roll(before, -HALO * group), west_ref[group])
        east = jnp.where(in_east, roll(after, -HALO * group), east_ref[group])
        for index, value in ((group, west), (BANDS + group, east)):
            if mask_ref is not None:
                value = value * mask_ref[index, BODY, :]
            one_ref[index, BODY, :] = value


def join_bands(one_ref, plane, inner, lane):
    group, j = divmod(plane, LANES)
    value = jnp.where(
        window(lane, BAND * j + 2 * HALO, HALO),
        one_ref[group, CORE, :],
        one_ref[BANDS + group, CORE, :],
    )
    edge = (lane < HALO) | (lane >= COLS - HALO)
    return jnp.where(edge, roll(value, -turn(plane)), inner)


def first_bands_kernel(
    first_ref,
    second_ref,
    west_ref,
    east_ref,
    depth_ref,
    inner_ref,
    out_ref,
    keep_ref,
    give_ref,
    mask_ref,
    one_ref,
    two_ref,
):
    tall_lane = lanes(TALL)
    clear_pads(mask_ref, 2 * BANDS)
    before, after = sides(first_ref[:, COLS:], second_ref[:, COLS:], even_on("zon"))
    depth = depth_ref[...]
    blank = jnp.zeros((TALL, COLS), F32)
    west, east = [blank] * BANDS, [blank] * BANDS
    for j in range(LANES):
        at = BAND * j
        turned = roll(depth, turn(j))
        low = jnp.where(window(tall_lane, at + HALO, HALO), roll(before, at + HALO), turned)
        high = jnp.where(window(tall_lane, at + 2 * HALO, HALO), roll(after, at + 2 * HALO), turned)
        for group in range(BANDS):
            level = (group * LANES + j) % LEVELS
            west[group] = jnp.where(
                window(tall_lane, at + HALO, BAND), jnp.where(low > level, 1.0, 0.0), west[group]
            )
            east[group] = jnp.where(
                window(tall_lane, at, BAND), jnp.where(high > level, 1.0, 0.0), east[group]
            )
    for group in range(BANDS):
        mask_ref[group, BODY, :] = west[group]
        mask_ref[BANDS + group, BODY, :] = east[group]
    coefficients(mask_ref, 2 * BANDS, keep_ref, give_ref)
    fill_bands(first_ref, second_ref, west_ref, east_ref, one_ref, mask_ref)
    sweep_all(2 * BANDS, 2 * BANDS, keep_ref, give_ref, one_ref, two_ref)
    lane = lanes(ROWS)
    for plane in range(PLANES):
        out_ref[plane] = join_bands(one_ref, plane, inner_ref[plane], lane)


def gradient_kernel(
    first_ref,
    second_ref,
    west_ref,
    east_ref,
    inner_ref,
    keep_ref,
    give_ref,
    control_ref,
    out_ref,
    one_ref,
    two_ref,
):
    fill_bands(first_ref, second_ref, west_ref, east_ref, one_ref, None)
    sweep_all(2 * BANDS, 2 * BANDS, keep_ref, give_ref, one_ref, two_ref)
    lane = lanes(ROWS)
    for plane in range(PLANES):
        f, k = divmod(plane, LEVELS)
        out_ref[f, k] = control_ref[f, k] + join_bands(one_ref, plane, inner_ref[plane], lane)


def split(value):
    coarse = value.astype(jnp.bfloat16)
    return jnp.concatenate([coarse, (value - coarse.astype(F32)).astype(jnp.bfloat16)], axis=1)


def join(value):
    return value[:, :COLS] + value[:, COLS:]


def observe_kernel(
    count_ref,
    smooth_ref,
    error_ref,
    bottom_ref,
    keep_ref,
    other_ref,
    corner_ref,
    weight_ref,
    value_ref,
    precision_ref,
    field_ref,
    first_ref,
    second_ref,
    total_ref,
    low_ref,
    high_ref,
):
    group = lax.axis_index("grp")
    slots = corner_ref.shape[-1]
    depth = bottom_ref[...]
    for plane in range(PLANES):
        f, k = divmod(plane, LEVELS)
        scale = jnp.where(depth > k, error_ref[f, k], 0.0)
        held = group == k // HALF
        prior = jnp.where(held, keep_ref[f, k % HALF], other_ref[f, k % HALF])
        total_ref[plane * ROWS : (plane + 1) * ROWS, :] = scale * smooth_ref[plane] + prior
    corner = corner_ref[0, 0]
    row = (corner >> 7).astype(F32)
    column = (corner & (COLS - 1)).astype(F32)
    stacked = jnp.concatenate(
        [weight_ref[0, 0, 0], value_ref[0, 0], precision_ref[0, 0], row, column], axis=0
    )
    tall = jnp.transpose(stacked)
    row_tall = jnp.concatenate([tall[:, 6:7], tall[:, 6:7] + 1.0], axis=0)
    cells = PLANES * ROWS
    wide_row = lax.broadcasted_iota(jnp.int32, (2 * slots, cells), 1).astype(F32)
    pick = jnp.where(wide_row == row_tall, 1.0, 0.0).astype(jnp.bfloat16)
    seen = join(jnp.dot(pick, split(total_ref[...]), preferred_element_type=F32))
    lane = lanes(slots).astype(F32)
    at, beside = lane == tall[:, 7:8], lane == tall[:, 7:8] + 1.0
    lower = jnp.where(at, tall[:, 0:1], jnp.where(beside, tall[:, 1:2], 0.0))
    upper = jnp.where(at, tall[:, 2:3], jnp.where(beside, tall[:, 3:4], 0.0))
    observed = jnp.sum(lower * seen[:slots] + upper * seen[slots:], axis=1, keepdims=True)
    live = lax.broadcasted_iota(jnp.int32, (slots, 1), 0) < count_ref[0, 0, 0]
    misfit = jnp.where(live, tall[:, 5:6] * (observed - tall[:, 4:5]), 0.0)
    spread = jnp.concatenate([lower * misfit, upper * misfit], axis=0)
    tall_row = lax.broadcasted_iota(jnp.int32, (cells, slots), 0).astype(F32)
    back = jnp.concatenate(
        [
            jnp.where(tall_row == row, 1.0, 0.0).astype(jnp.bfloat16),
            jnp.where(tall_row == row + 1.0, 1.0, 0.0).astype(jnp.bfloat16),
        ],
        axis=1,
    )
    total_ref[...] = join(jnp.dot(back, split(spread), preferred_element_type=F32))
    for plane in range(PLANES):
        f, k = divmod(plane, LEVELS)
        scale = jnp.where(depth > k, error_ref[f, k], 0.0)
        field_ref[plane] = scale * total_ref[plane * ROWS : (plane + 1) * ROWS, :]
    stage(
        low_ref,
        high_ref,
        lambda p: field_ref[p, :HALO, :],
        lambda p: field_ref[p, ROWS - HALO :, :],
    )
    blank = jnp.zeros((SHORT - DEPTH_ROW, COLS), F32)
    low_ref[DEPTH_ROW:, :] = blank
    high_ref[DEPTH_ROW:, :] = blank
    send_rows(low_ref, high_ref, first_ref, second_ref)


def call(kernel, outs, scratch=(), scalars=0, remote=False, work=0):
    space = pltpu.HBM if remote else VMEM

    def run(*args):
        return pl.pallas_call(
            kernel,
            out_shape=[jax.ShapeDtypeStruct(shape, kind) for shape, kind in outs],
            in_specs=[
                pl.BlockSpec(memory_space=pltpu.SMEM if i < scalars else space)
                for i in range(len(args))
            ],
            out_specs=[pl.BlockSpec(memory_space=VMEM) for _ in outs],
            scratch_shapes=list(scratch),
            compiler_params=pltpu.CompilerParams(vmem_limit_bytes=24 * 2**20),
            cost_estimate=pl.CostEstimate(
                flops=work, bytes_accessed=work // 10, transcendentals=0
            )
            if work
            else None,
            name=kernel.__name__.removesuffix("_kernel"),
        )(*args)

    return run


def swap(value, axis, shift, wrap):
    size = lax.axis_size(axis)
    pairs = []
    for i in range(shift, size + shift - 1, 2):
        j = i + 1
        if j < size or wrap:
            pairs += [(i, j % size), (j % size, i)]
    return lax.ppermute(value, axis, pairs)


def exchange(first, second, axis, wrap):
    return swap(first, axis, 0, wrap), swap(second, axis, 1, wrap)


FULL = ((PLANES, ROWS, COLS), F32)
RAISED = ((PLANES, TALL, COLS), F32)
SIDE = ((BANDS, TALL, COLS), F32)
STEP = ((FIELDS, HALF, ROWS, COLS), F32)
PART = ((PAIR, HALF, ROWS, COLS), F32)
MASKS = ((LEVELS, DEEP, COLS), F32)
STRIP = ((2 * BANDS, DEEP, COLS), F32)


def rows_of(count):
    return ((count, COLS), TRAVEL)


def columns_of(count):
    return ((TALL, count * COLS), TRAVEL)


def body(
    model_state,
    control,
    error_std,
    bottom_level,
    obs_count,
    obs_corner,
    obs_weight,
    obs_value,
    obs_precision,
):
    dma = pltpu.SemaphoreType.DMA
    long, short = VMEM((LONG, COLS), F32), VMEM((SHORT, COLS), F32)
    first, second = call(
        start_kernel,
        [rows_of(LONG)] * 2,
        [VMEM((PAIR, LEVELS, EDGE, COLS), F32)] * 2
        + [VMEM((FIELDS, HALF, 8, COLS), F32)] * 2
        + [VMEM((EDGE, COLS), jnp.int32)] * 2
        + [long, long, dma((6,))],
        remote=True,
    )(model_state, control, bottom_level)
    mer = exchange(first, second, "mer", False)
    tall, depth, west, east, first, second = call(
        first_columns_kernel,
        [RAISED, ((TALL, COLS), F32), SIDE, SIDE, columns_of(2), columns_of(2)],
        [long, long],
    )(model_state, control, bottom_level, *mer)
    zon = exchange(first, second, "zon", True)
    inner, keep_coef, give_coef, base = call(
        first_interior_kernel,
        [FULL, MASKS, MASKS, STEP],
        [VMEM(*MASKS)]
        + [VMEM((PLANES, DEEP, COLS), F32)] * 2
        + [long, long, VMEM((ROWS + 16, COLS), F32)],
        work=10**7,
    )(tall, depth, model_state, *mer)
    keep, send = call(background_kernel, [PART, PART])(model_state, depth, base, *zon)
    other = lax.ppermute(send, "grp", [(0, 1), (1, 0)])
    smoothed, keep_band, give_band = call(
        first_bands_kernel, [FULL, STRIP, STRIP], [VMEM(*STRIP)] * 3, work=10**7
    )(*zon, west, east, depth, inner)
    field, first, second = call(
        observe_kernel,
        [FULL, rows_of(SHORT), rows_of(SHORT)],
        [VMEM((PLANES * ROWS, COLS), F32), short, short],
        scalars=1,
    )(
        obs_count,
        smoothed,
        error_std,
        bottom_level,
        keep,
        other,
        obs_corner,
        obs_weight,
        obs_value,
        obs_precision,
    )
    mer = exchange(first, second, "mer", False)
    tall, west, east, first, second = call(
        next_columns_kernel, [RAISED, SIDE, SIDE, columns_of(1), columns_of(1)], [short, short]
    )(field, *mer)
    zon = exchange(first, second, "zon", True)
    (inner,) = call(
        next_interior_kernel, [FULL], [VMEM((PLANES, DEEP, COLS), F32)] * 2, work=10**7
    )(tall, keep_coef, give_coef)
    return call(gradient_kernel, [(control.shape, F32)], [VMEM(*STRIP)] * 2)(
        *zon, west, east, inner, keep_band, give_band, control
    )[0]


def solution(mesh):
    return jax.shard_map(
        body,
        mesh=mesh,
        in_specs=(
            P(None, "grp", "mer", "zon"),
            P("grp", None, "mer", "zon"),
            P("grp", None, "mer", "zon"),
            P("mer", "zon"),
            P("grp", "mer", "zon"),
            P("grp", "mer", "zon", None),
            P("grp", "mer", "zon", None, None),
            P("grp", "mer", "zon", None),
            P("grp", "mer", "zon", None),
        ),
        out_specs=P("grp", None, "mer", "zon"),
        check_vma=False,
    )
```

```python
import jax
import jax.numpy as jnp
from jax import lax
from jax.experimental import pallas as pl
from jax.experimental.pallas import tpu as pltpu
from jax.sharding import PartitionSpec as P

SWEEPS = 10
SMOOTHING = 0.2
ADVECTION = 0.1
MIXING = 0.15

PAIR = 2
LEVELS = 6
HALF = 3
FIELDS = 4
PLANES = PAIR * LEVELS
STEPPED = FIELDS * HALF
ROWS = 64
COLS = 128
HALO = SWEEPS
EDGE = 16
TALL = ROWS + 2 * EDGE
PAD = 8
DEEP = TALL + 2 * PAD
BAND = 3 * HALO
LANES = COLS // BAND
BANDS = PLANES // LANES
DEPTH_ROW = PLANES * HALO
MODEL_ROW = DEPTH_ROW + HALO
LONG = 160
SHORT = 128
MODEL_LANE = 16
TRAVEL = jnp.bfloat16
F32 = jnp.float32
VMEM = pltpu.VMEM
GRANT, GRANT_MORE, GRANT_MOST = 24, 40, 53.7


def lanes(rows):
    return lax.broadcasted_iota(jnp.int32, (rows, COLS), 1)


def window(lane, start, width):
    start %= COLS
    stop = start + width
    if stop > COLS:
        return (lane >= start) | (lane < stop - COLS)
    return (lane >= start) & (lane < stop)


def roll(value, shift):
    shift %= COLS
    return value if shift == 0 else pltpu.roll(value, shift, 1)


def mer_sides(first, second):
    low, high = sides(first, second, even_on("mer"))
    index = lax.axis_index("mer")
    return jnp.where(index == 0, 0.0, low), jnp.where(index == lax.axis_size("mer") - 1, 0.0, high)


def even_on(axis):
    return lax.axis_index(axis) % 2 == 0


def sides(first, second, even):
    first, second = first.astype(F32), second.astype(F32)
    return jnp.where(even, second, first), jnp.where(even, first, second)


def turn(plane):
    return BAND * (plane % LANES) + 2 * HALO


def stage(low_ref, high_ref, low, high):
    for plane in range(PLANES):
        here = slice(plane * HALO, (plane + 1) * HALO)
        low_ref[here, :] = low(plane)
        high_ref[here, :] = high(plane)


def send_rows(low_ref, high_ref, first_ref, second_ref):
    even = even_on("mer")
    low, high = low_ref[...], high_ref[...]
    first_ref[...] = jnp.where(even, high, low).astype(TRAVEL)
    second_ref[...] = jnp.where(even, low, high).astype(TRAVEL)


def start_kernel(
    model_ref,
    control_ref,
    bottom_ref,
    first_ref,
    second_ref,
    control_low,
    control_high,
    model_low,
    model_high,
    bottom_low,
    bottom_high,
    low_ref,
    high_ref,
    sems,
):
    ends = pl.ds(0, EDGE), pl.ds(ROWS - EDGE, EDGE)
    tips = pl.ds(0, 8), pl.ds(ROWS - 8, 8)
    copies = [
        pltpu.make_async_copy(control_ref.at[:, :, ends[0], :], control_low, sems.at[0]),
        pltpu.make_async_copy(control_ref.at[:, :, ends[1], :], control_high, sems.at[1]),
        pltpu.make_async_copy(model_ref.at[:, :, tips[0], :], model_low, sems.at[2]),
        pltpu.make_async_copy(model_ref.at[:, :, tips[1], :], model_high, sems.at[3]),
        pltpu.make_async_copy(bottom_ref.at[ends[0], :], bottom_low, sems.at[4]),
        pltpu.make_async_copy(bottom_ref.at[ends[1], :], bottom_high, sems.at[5]),
    ]
    for copy in copies:
        copy.start()
    for copy in copies:
        copy.wait()
    stage(
        low_ref,
        high_ref,
        lambda p: control_low[p // LEVELS, p % LEVELS, :HALO, :],
        lambda p: control_high[p // LEVELS, p % LEVELS, EDGE - HALO :, :],
    )
    low_ref[DEPTH_ROW:MODEL_ROW, :] = bottom_low[:HALO, :].astype(F32)
    high_ref[DEPTH_ROW:MODEL_ROW, :] = bottom_high[EDGE - HALO :, :].astype(F32)
    for q in range(STEPPED):
        for ref, value in (
            (low_ref, model_low[q // HALF, q % HALF, :1, :]),
            (high_ref, model_high[q // HALF, q % HALF, 7:, :]),
        ):
            coarse = value.astype(TRAVEL).astype(F32)
            at = MODEL_ROW + q
            ref[at : at + 1, :] = coarse
            ref[at + STEPPED : at + STEPPED + 1, :] = value - coarse
    rest = MODEL_ROW + 2 * STEPPED
    low_ref[rest:, :] = jnp.zeros((LONG - rest, COLS), F32)
    high_ref[rest:, :] = jnp.zeros((LONG - rest, COLS), F32)
    send_rows(low_ref, high_ref, first_ref, second_ref)


def stand(value, low, high):
    blank = jnp.zeros((EDGE - HALO, COLS), F32)
    return jnp.concatenate([blank, low, value, high, blank], axis=0)


def stand_core(value):
    blank = jnp.zeros((EDGE, COLS), F32)
    return jnp.concatenate([blank, value, blank], axis=0)


def model_columns(model_ref, east_ref, west_ref):
    lane = lanes(ROWS)
    to_east = to_west = jnp.zeros((ROWS, COLS), F32)
    for q in range(STEPPED):
        value = model_ref[q // HALF, q % HALF]
        at = MODEL_LANE + 2 * q
        column = value[:, COLS - 1 :]
        coarse = column.astype(TRAVEL).astype(F32)
        to_east = jnp.where(lane == at, coarse, to_east)
        to_east = jnp.where(lane == at + 1, column - coarse, to_east)
        column = value[:, :1]
        coarse = column.astype(TRAVEL).astype(F32)
        to_west = jnp.where(lane == at - 1, coarse, to_west)
        to_west = jnp.where(lane == at - 2, column - coarse, to_west)
    east_ref[...] = to_east
    west_ref[...] = to_west


def raise_planes(read, first_ref, second_ref, low_ref, high_ref, tall_ref):
    low, high = mer_sides(first_ref[...], second_ref[...])
    low_ref[...] = low
    high_ref[...] = high
    blank = jnp.zeros((EDGE - HALO, COLS), F32)
    for plane in range(PLANES):
        here = slice(plane * HALO, (plane + 1) * HALO)
        tall_ref[plane, : EDGE - HALO, :] = blank
        tall_ref[plane, EDGE - HALO : EDGE, :] = low_ref[here, :]
        tall_ref[plane, EDGE : EDGE + ROWS, :] = read(plane)
        tall_ref[plane, EDGE + ROWS : EDGE + ROWS + HALO, :] = high_ref[here, :]
        tall_ref[plane, EDGE + ROWS + HALO :, :] = blank


def cut_bands(tall_ref, west_ref, east_ref):
    lane = lanes(TALL)
    blank = jnp.zeros((TALL, COLS), F32)
    to_east, to_west = blank, blank
    for group in range(BANDS):
        west = east = go_east = go_west = blank
        for j in range(LANES):
            plane = group * LANES + j
            turned = roll(tall_ref[plane], turn(plane))
            at = BAND * j
            west = jnp.where(window(lane, at + 2 * HALO, 2 * HALO), turned, west)
            east = jnp.where(window(lane, at, 2 * HALO), turned, east)
            go_east = jnp.where(window(lane, at + HALO, HALO), turned, go_east)
            go_west = jnp.where(window(lane, at + 2 * HALO, HALO), turned, go_west)
        west_ref[group] = west
        east_ref[group] = east
        to_east = to_east + roll(go_east, HALO * group)
        to_west = to_west + roll(go_west, HALO * group)
    return to_east, to_west


def send_columns(part, to_east, to_west, first_ref, second_ref):
    even = even_on("zon")
    here = slice(part * COLS, (part + 1) * COLS)
    first_ref[:, here] = jnp.where(even, to_east, to_west).astype(TRAVEL)
    second_ref[:, here] = jnp.where(even, to_west, to_east).astype(TRAVEL)


def first_columns_kernel(
    control_ref,
    bottom_ref,
    model_east_ref,
    model_west_ref,
    a_ref,
    b_ref,
    tall_ref,
    depth_ref,
    west_ref,
    east_ref,
    first_ref,
    second_ref,
    low_ref,
    high_ref,
):
    raise_planes(
        lambda p: control_ref[p // LEVELS, p % LEVELS], a_ref, b_ref, low_ref, high_ref, tall_ref
    )
    send_columns(0, *cut_bands(tall_ref, west_ref, east_ref), first_ref, second_ref)
    depth = stand(
        bottom_ref[...].astype(F32),
        low_ref[DEPTH_ROW:MODEL_ROW, :],
        high_ref[DEPTH_ROW:MODEL_ROW, :],
    )
    depth_ref[...] = depth
    mark = lanes(TALL) < HALO
    send_columns(
        1,
        jnp.where(mark, roll(depth, HALO), stand_core(model_east_ref[...])),
        jnp.where(mark, depth, stand_core(model_west_ref[...])),
        first_ref,
        second_ref,
    )


def next_columns_kernel(
    field_ref, a_ref, b_ref, tall_ref, west_ref, east_ref, first_ref, second_ref, low_ref, high_ref
):
    raise_planes(lambda p: field_ref[p], a_ref, b_ref, low_ref, high_ref, tall_ref)
    send_columns(0, *cut_bands(tall_ref, west_ref, east_ref), first_ref, second_ref)


def base_step(model_ref, depth_ref, a_ref, b_ref, base_ref, low_ref, high_ref, tall_ref):
    lane = lanes(ROWS)
    group = lax.axis_index("grp")
    low, high = mer_sides(a_ref[...], b_ref[...])
    low_ref[...] = low
    high_ref[...] = high
    core = slice(EDGE, EDGE + ROWS)
    south, north = slice(EDGE - 1, EDGE + ROWS - 1), slice(EDGE + 1, EDGE + ROWS + 1)
    depth = depth_ref[core, :]
    around = (
        depth,
        jnp.where(lane == COLS - 1, 0.0, roll(depth, -1)),
        jnp.where(lane == 0, 0.0, roll(depth, 1)),
        depth_ref[north, :],
        depth_ref[south, :],
    )
    for level in range(HALF):
        here = (group * HALF + level).astype(F32)
        wet, wet_e, wet_w, wet_n, wet_s = (jnp.where(v > here, 1.0, 0.0) for v in around)
        count = MIXING * (wet_e + wet_w + wet_n + wet_s)
        flow_x = 0.5 * ADVECTION * model_ref[2, level]
        flow_y = 0.5 * ADVECTION * model_ref[3, level]
        give_e, give_w = wet_e * (MIXING - flow_x), wet_w * (MIXING + flow_x)
        give_n, give_s = wet_n * (MIXING - flow_y), wet_s * (MIXING + flow_y)
        for field in range(FIELDS):
            at = MODEL_ROW + field * HALF + level
            value = model_ref[field, level]
            tall_ref[8 : 8 + ROWS, :] = value
            tall_ref[7:8, :] = low_ref[at : at + 1, :] + low_ref[at + STEPPED : at + STEPPED + 1, :]
            tall_ref[8 + ROWS : 9 + ROWS, :] = (
                high_ref[at : at + 1, :] + high_ref[at + STEPPED : at + STEPPED + 1, :]
            )
            base_ref[field, level] = wet * (
                value * (1.0 - count)
                + give_e * roll(value, -1)
                + give_w * roll(value, 1)
                + give_n * tall_ref[9 : 9 + ROWS, :]
                + give_s * tall_ref[7 : 7 + ROWS, :]
            )


def background_kernel(model_ref, depth_ref, base_ref, first_ref, second_ref, keep_ref, send_ref):
    lane = lanes(ROWS)
    group = lax.axis_index("grp")
    core = slice(EDGE, EDGE + ROWS)
    before, after = sides(first_ref[core, COLS:], second_ref[core, COLS:], even_on("zon"))
    at_west, at_east = lane == 0, lane == COLS - 1
    beside = jnp.where(at_west, roll(before, 1 - HALO), jnp.where(at_east, roll(after, -1), 0.0))
    depth = jnp.minimum(depth_ref[core, :], beside)
    columns = jnp.where(lane % 2 == 0, before + roll(before, -1), after + roll(after, 1))
    sign = jnp.where(at_west, 0.5 * ADVECTION, -0.5 * ADVECTION)
    for level in range(HALF):
        wet = depth > (group * HALF + level).astype(F32)
        gain = jnp.where(wet, MIXING + sign * model_ref[2, level], 0.0)
        loss = jnp.where(wet, MIXING, 0.0)
        for out_ref, pair in ((keep_ref, group), (send_ref, 1 - group)):
            for f in range(PAIR):
                field = PAIR * pair + f
                at = MODEL_LANE + 2 * (field * HALF + level)
                halo = pltpu.roll(columns, COLS - at, 1)
                out_ref[f, level] = base_ref[field, level] + (
                    gain * halo - loss * model_ref[field, level]
                )


def neighbour_sum(ref, index, start, rows):
    here = ref[index, pl.ds(start, rows), :]
    return here, (roll(here, -1) + roll(here, 1)) + (
        ref[index, pl.ds(start - 1, rows), :] + ref[index, pl.ds(start + 1, rows), :]
    )


def coefficients(mask_ref, count, keep_ref, give_ref):
    for index in range(count):
        wet, total = neighbour_sum(mask_ref, index, PAD, TALL)
        keep_ref[index, PAD : PAD + TALL, :] = wet * (1.0 - SMOOTHING * total)
        give_ref[index, PAD : PAD + TALL, :] = SMOOTHING * wet


def sweep_all(count, masks, keep_ref, give_ref, one_ref, two_ref):
    def sweep(source_ref, target_ref, start, rows):
        for index in range(count):
            here, total = neighbour_sum(source_ref, index, start, rows)
            at = pl.ds(start, rows)
            target_ref[index, at, :] = (
                keep_ref[index % masks, at, :] * here + give_ref[index % masks, at, :] * total
            )

    sweep(one_ref, two_ref, PAD, TALL)
    sweep(two_ref, one_ref, 2 * PAD, TALL - 2 * PAD)

    def step(index, carry):
        sweep(one_ref, two_ref, 2 * PAD, TALL - 2 * PAD)
        sweep(two_ref, one_ref, 2 * PAD, TALL - 2 * PAD)
        return carry

    lax.fori_loop(0, SWEEPS // 2 - 1, step, 0)


def clear_pads(ref, count):
    for index in range(count):
        ref[index, :PAD, :] = jnp.zeros((PAD, COLS), F32)
        ref[index, PAD + TALL :, :] = jnp.zeros((PAD, COLS), F32)


CORE = slice(PAD + EDGE, PAD + EDGE + ROWS)
BODY = slice(PAD, PAD + TALL)


def first_interior_kernel(
    tall_ref,
    depth_ref,
    model_ref,
    a_ref,
    b_ref,
    inner_ref,
    keep_ref,
    give_ref,
    base_ref,
    mask_ref,
    one_ref,
    two_ref,
    low_ref,
    high_ref,
    stand_ref,
):
    base_step(model_ref, depth_ref, a_ref, b_ref, base_ref, low_ref, high_ref, stand_ref)
    clear_pads(mask_ref, LEVELS)
    clear_pads(one_ref, PLANES)
    depth = depth_ref[...]
    for level in range(LEVELS):
        wet = jnp.where(depth > level, 1.0, 0.0)
        mask_ref[level, BODY, :] = wet
        for field in range(PAIR):
            plane = field * LEVELS + level
            one_ref[plane, BODY, :] = wet * tall_ref[plane]
    coefficients(mask_ref, LEVELS, keep_ref, give_ref)
    sweep_all(PLANES, LEVELS, keep_ref, give_ref, one_ref, two_ref)
    for plane in range(PLANES):
        inner_ref[plane] = one_ref[plane, CORE, :]


def next_interior_kernel(tall_ref, keep_ref, give_ref, inner_ref, one_ref, two_ref):
    clear_pads(one_ref, PLANES)
    for plane in range(PLANES):
        one_ref[plane, BODY, :] = tall_ref[plane]
    sweep_all(PLANES, LEVELS, keep_ref, give_ref, one_ref, two_ref)
    for plane in range(PLANES):
        inner_ref[plane] = one_ref[plane, CORE, :]


def fill_bands(first_ref, second_ref, west_ref, east_ref, one_ref, mask_ref):
    lane = lanes(TALL)
    before, after = sides(first_ref[:, :COLS], second_ref[:, :COLS], even_on("zon"))
    clear_pads(one_ref, 2 * BANDS)
    in_west = (lane >= HALO) & ((lane - HALO) % BAND < HALO)
    in_east = (lane >= 2 * HALO) & ((lane - 2 * HALO) % BAND < HALO)
    for group in range(BANDS):
        west = jnp.where(in_west, roll(before, -HALO * group), west_ref[group])
        east = jnp.where(in_east, roll(after, -HALO * group), east_ref[group])
        for index, value in ((group, west), (BANDS + group, east)):
            if mask_ref is not None:
                value = value * mask_ref[index, BODY, :]
            one_ref[index, BODY, :] = value


def join_bands(one_ref, plane, inner, lane):
    group, j = divmod(plane, LANES)
    value = jnp.where(
        window(lane, BAND * j + 2 * HALO, HALO),
        one_ref[group, CORE, :],
        one_ref[BANDS + group, CORE, :],
    )
    edge = (lane < HALO) | (lane >= COLS - HALO)
    return jnp.where(edge, roll(value, -turn(plane)), inner)


def first_bands_kernel(
    first_ref,
    second_ref,
    west_ref,
    east_ref,
    depth_ref,
    inner_ref,
    out_ref,
    keep_ref,
    give_ref,
    mask_ref,
    one_ref,
    two_ref,
):
    tall_lane = lanes(TALL)
    clear_pads(mask_ref, 2 * BANDS)
    before, after = sides(first_ref[:, COLS:], second_ref[:, COLS:], even_on("zon"))
    depth = depth_ref[...]
    blank = jnp.zeros((TALL, COLS), F32)
    west, east = [blank] * BANDS, [blank] * BANDS
    for j in range(LANES):
        at = BAND * j
        turned = roll(depth, turn(j))
        low = jnp.where(window(tall_lane, at + HALO, HALO), roll(before, at + HALO), turned)
        high = jnp.where(window(tall_lane, at + 2 * HALO, HALO), roll(after, at + 2 * HALO), turned)
        for group in range(BANDS):
            level = (group * LANES + j) % LEVELS
            west[group] = jnp.where(
                window(tall_lane, at + HALO, BAND), jnp.where(low > level, 1.0, 0.0), west[group]
            )
            east[group] = jnp.where(
                window(tall_lane, at, BAND), jnp.where(high > level, 1.0, 0.0), east[group]
            )
    for group in range(BANDS):
        mask_ref[group, BODY, :] = west[group]
        mask_ref[BANDS + group, BODY, :] = east[group]
    coefficients(mask_ref, 2 * BANDS, keep_ref, give_ref)
    fill_bands(first_ref, second_ref, west_ref, east_ref, one_ref, mask_ref)
    sweep_all(2 * BANDS, 2 * BANDS, keep_ref, give_ref, one_ref, two_ref)
    lane = lanes(ROWS)
    for plane in range(PLANES):
        out_ref[plane] = join_bands(one_ref, plane, inner_ref[plane], lane)


def gradient_kernel(
    first_ref,
    second_ref,
    west_ref,
    east_ref,
    inner_ref,
    keep_ref,
    give_ref,
    control_ref,
    out_ref,
    one_ref,
    two_ref,
):
    fill_bands(first_ref, second_ref, west_ref, east_ref, one_ref, None)
    sweep_all(2 * BANDS, 2 * BANDS, keep_ref, give_ref, one_ref, two_ref)
    lane = lanes(ROWS)
    for plane in range(PLANES):
        f, k = divmod(plane, LEVELS)
        out_ref[f, k] = control_ref[f, k] + join_bands(one_ref, plane, inner_ref[plane], lane)


def split(value):
    coarse = value.astype(jnp.bfloat16)
    return jnp.concatenate([coarse, (value - coarse.astype(F32)).astype(jnp.bfloat16)], axis=1)


def join(value):
    return value[:, :COLS] + value[:, COLS:]


def prepare_kernel(*refs):
    here_refs, out_refs, (*held_refs, sems) = refs[:8], refs[8:16], refs[16:]
    copies = [
        pltpu.make_async_copy(source, target, sems.at[i])
        for i, (source, target) in enumerate(zip(here_refs, held_refs))
    ]
    for copy in copies:
        copy.start()
    for copy in copies:
        copy.wait()
    count_ref, model_ref, error_ref, bottom_ref = held_refs[:4]
    corner_ref, weight_ref, value_ref, precision_ref = held_refs[4:]
    east_ref, west_ref, scale_ref, pick_ref, back_ref, lower_ref, upper_ref, want_ref = out_refs
    model_columns(model_ref, east_ref, west_ref)
    depth = bottom_ref[...]
    for plane in range(PLANES):
        f, k = divmod(plane, LEVELS)
        scale_ref[plane] = jnp.where(depth > k, error_ref[f, k], 0.0)
    slots = corner_ref.shape[-1]
    cells = PLANES * ROWS
    corner = corner_ref[0, 0]
    row = (corner >> 7).astype(F32)
    column = (corner & (COLS - 1)).astype(F32)
    stacked = jnp.concatenate(
        [weight_ref[0, 0, 0], value_ref[0, 0], precision_ref[0, 0], row, column], axis=0
    )
    tall = jnp.transpose(stacked)
    wide_row = lax.broadcasted_iota(jnp.int32, (slots, cells), 1).astype(F32)
    tall_row = lax.broadcasted_iota(jnp.int32, (cells, slots), 0).astype(F32)
    for step in range(2):
        here = slice(step * slots, (step + 1) * slots)
        pick_ref[here, :] = jnp.where(wide_row == tall[:, 6:7] + step, 1.0, 0.0).astype(jnp.bfloat16)
        back_ref[:, here] = jnp.where(tall_row == row + step, 1.0, 0.0).astype(jnp.bfloat16)
    lane = lanes(slots).astype(F32)
    at, beside = lane == tall[:, 7:8], lane == tall[:, 7:8] + 1.0
    lower_ref[...] = jnp.where(at, tall[:, 0:1], jnp.where(beside, tall[:, 1:2], 0.0))
    upper_ref[...] = jnp.where(at, tall[:, 2:3], jnp.where(beside, tall[:, 3:4], 0.0))
    live = lax.broadcasted_iota(jnp.int32, (slots, 8), 0) < count_ref[0]
    want_ref[...] = jnp.where(live, tall, 0.0)


def observe_kernel(
    smooth_ref,
    scale_ref,
    keep_ref,
    other_ref,
    pick_ref,
    back_ref,
    lower_ref,
    upper_ref,
    want_ref,
    field_ref,
    first_ref,
    second_ref,
    total_ref,
    low_ref,
    high_ref,
):
    group = lax.axis_index("grp")
    slots = want_ref.shape[0]
    for plane in range(PLANES):
        f, k = divmod(plane, LEVELS)
        held = group == k // HALF
        prior = jnp.where(held, keep_ref[f, k % HALF], other_ref[f, k % HALF])
        total_ref[plane * ROWS : (plane + 1) * ROWS, :] = (
            scale_ref[plane] * smooth_ref[plane] + prior
        )
    seen = join(jnp.dot(pick_ref[...], split(total_ref[...]), preferred_element_type=F32))
    lower, upper = lower_ref[...], upper_ref[...]
    observed = jnp.sum(lower * seen[:slots] + upper * seen[slots:], axis=1, keepdims=True)
    misfit = want_ref[:, 5:6] * (observed - want_ref[:, 4:5])
    spread = jnp.concatenate([lower * misfit, upper * misfit], axis=0)
    total_ref[...] = join(jnp.dot(back_ref[...], split(spread), preferred_element_type=F32))
    for plane in range(PLANES):
        field_ref[plane] = scale_ref[plane] * total_ref[plane * ROWS : (plane + 1) * ROWS, :]
    stage(
        low_ref,
        high_ref,
        lambda p: field_ref[p, :HALO, :],
        lambda p: field_ref[p, ROWS - HALO :, :],
    )
    blank = jnp.zeros((SHORT - DEPTH_ROW, COLS), F32)
    low_ref[DEPTH_ROW:, :] = blank
    high_ref[DEPTH_ROW:, :] = blank
    send_rows(low_ref, high_ref, first_ref, second_ref)


def call(kernel, outs, scratch=(), remote=0, work=0):
    space = pl.ANY if remote else VMEM

    def run(*args):
        return pl.pallas_call(
            kernel,
            out_shape=[jax.ShapeDtypeStruct(shape, kind) for shape, kind in outs],
            in_specs=[pl.BlockSpec(memory_space=space) for _ in args],
            out_specs=[pl.BlockSpec(memory_space=VMEM) for _ in outs],
            scratch_shapes=list(scratch),
            compiler_params=pltpu.CompilerParams(
                vmem_limit_bytes=int((remote or GRANT) * 2**20)
            ),
            cost_estimate=pl.CostEstimate(
                flops=work, bytes_accessed=work // 10, transcendentals=0
            )
            if work
            else None,
            name=kernel.__name__.removesuffix("_kernel"),
        )(*args)

    return run


def swap(value, axis, shift):
    size = lax.axis_size(axis)
    pairs = []
    for i in range(shift, size, 2):
        j = (i + 1) % size
        pairs += [(i, j), (j, i)]
    return lax.ppermute(value, axis, pairs)


def exchange(first, second, axis):
    return swap(first, axis, 0), swap(second, axis, 1)


FULL = ((PLANES, ROWS, COLS), F32)
RAISED = ((PLANES, TALL, COLS), F32)
SIDE = ((BANDS, TALL, COLS), F32)
STEP = ((FIELDS, HALF, ROWS, COLS), F32)
PART = ((PAIR, HALF, ROWS, COLS), F32)
MASKS = ((LEVELS, DEEP, COLS), F32)
STRIP = ((2 * BANDS, DEEP, COLS), F32)


def rows_of(count):
    return ((count, COLS), TRAVEL)


def columns_of(count):
    return ((TALL, count * COLS), TRAVEL)


def body(
    model_state,
    control,
    error_std,
    bottom_level,
    obs_count,
    obs_corner,
    obs_weight,
    obs_value,
    obs_precision,
):
    dma = pltpu.SemaphoreType.DMA
    long, short = VMEM((LONG, COLS), F32), VMEM((SHORT, COLS), F32)
    first, second = call(
        start_kernel,
        [rows_of(LONG)] * 2,
        [VMEM((PAIR, LEVELS, EDGE, COLS), F32)] * 2
        + [VMEM((FIELDS, HALF, 8, COLS), F32)] * 2
        + [VMEM((EDGE, COLS), jnp.int32)] * 2
        + [long, long, dma((6,))],
        remote=GRANT_MOST,
    )(model_state, control, bottom_level)
    mer = exchange(first, second, "mer")
    slots = obs_corner.shape[-1]
    inputs = (
        obs_count,
        model_state,
        error_std,
        bottom_level,
        obs_corner,
        obs_weight,
        obs_value,
        obs_precision,
    )
    model_east, model_west, scale, *operators = call(
        prepare_kernel,
        [((ROWS, COLS), F32)] * 2
        + [FULL]
        + [((2 * slots, PLANES * ROWS), jnp.bfloat16), ((PLANES * ROWS, 2 * slots), jnp.bfloat16)]
        + [((slots, COLS), F32)] * 2
        + [((slots, 8), F32)],
        [VMEM(value.shape, value.dtype) for value in inputs] + [dma((len(inputs),))],
        remote=GRANT_MORE,
        work=10**7,
    )(*inputs)
    tall, depth, west, east, first, second = call(
        first_columns_kernel,
        [RAISED, ((TALL, COLS), F32), SIDE, SIDE, columns_of(2), columns_of(2)],
        [long, long],
    )(control, bottom_level, model_east, model_west, *mer)
    zon = exchange(first, second, "zon")
    inner, keep_coef, give_coef, base = call(
        first_interior_kernel,
        [FULL, MASKS, MASKS, STEP],
        [VMEM(*MASKS)]
        + [VMEM((PLANES, DEEP, COLS), F32)] * 2
        + [long, long, VMEM((ROWS + 16, COLS), F32)],
        work=10**7,
    )(tall, depth, model_state, *mer)
    keep, send = call(background_kernel, [PART, PART])(model_state, depth, base, *zon)
    other = lax.ppermute(send, "grp", [(0, 1), (1, 0)])
    smoothed, keep_band, give_band = call(
        first_bands_kernel, [FULL, STRIP, STRIP], [VMEM(*STRIP)] * 3, work=10**7
    )(*zon, west, east, depth, inner)
    field, first, second = call(
        observe_kernel,
        [FULL, rows_of(SHORT), rows_of(SHORT)],
        [VMEM((PLANES * ROWS, COLS), F32), short, short],
    )(smoothed, scale, keep, other, *operators)
    mer = exchange(first, second, "mer")
    tall, west, east, first, second = call(
        next_columns_kernel, [RAISED, SIDE, SIDE, columns_of(1), columns_of(1)], [short, short]
    )(field, *mer)
    zon = exchange(first, second, "zon")
    (inner,) = call(
        next_interior_kernel, [FULL], [VMEM((PLANES, DEEP, COLS), F32)] * 2, work=10**7
    )(tall, keep_coef, give_coef)
    return call(gradient_kernel, [(control.shape, F32)], [VMEM(*STRIP)] * 2)(
        *zon, west, east, inner, keep_band, give_band, control
    )[0]


def solution(mesh):
    return jax.shard_map(
        body,
        mesh=mesh,
        in_specs=(
            P(None, "grp", "mer", "zon"),
            P("grp", None, "mer", "zon"),
            P("grp", None, "mer", "zon"),
            P("mer", "zon"),
            P("grp", "mer", "zon"),
            P("grp", "mer", "zon", None),
            P("grp", "mer", "zon", None, None),
            P("grp", "mer", "zon", None),
            P("grp", "mer", "zon", None),
        ),
        out_specs=P("grp", None, "mer", "zon"),
        check_vma=False,
    )
```

```python
import jax
import jax.numpy as jnp
from jax import lax
from jax.experimental import pallas as pl
from jax.experimental.pallas import tpu as pltpu
from jax.sharding import PartitionSpec as P

SWEEPS = 10
SMOOTHING = 0.2
ADVECTION = 0.1
MIXING = 0.15

PAIR = 2
LEVELS = 6
HALF = 3
FIELDS = 4
PLANES = PAIR * LEVELS
STEPPED = FIELDS * HALF
ROWS = 64
COLS = 128
HALO = SWEEPS
EDGE = 16
TALL = ROWS + 2 * EDGE
PAD = 8
DEEP = TALL + 2 * PAD
BAND = 3 * HALO
LANES = COLS // BAND
BANDS = PLANES // LANES
DEPTH_ROW = PLANES * HALO
MODEL_ROW = DEPTH_ROW + HALO
LONG = 160
SHORT = 128
MODEL_LANE = 16
TRAVEL = jnp.bfloat16
F32 = jnp.float32
VMEM = pltpu.VMEM
GRANT, GRANT_MOST = 24, 53.6


def lanes(rows):
    return lax.broadcasted_iota(jnp.int32, (rows, COLS), 1)


def window(lane, start, width):
    start %= COLS
    stop = start + width
    if stop > COLS:
        return (lane >= start) | (lane < stop - COLS)
    return (lane >= start) & (lane < stop)


def roll(value, shift):
    shift %= COLS
    return value if shift == 0 else pltpu.roll(value, shift, 1)


def mer_sides(first, second):
    low, high = sides(first, second, even_on("mer"))
    index = lax.axis_index("mer")
    return jnp.where(index == 0, 0.0, low), jnp.where(index == lax.axis_size("mer") - 1, 0.0, high)


def even_on(axis):
    return lax.axis_index(axis) % 2 == 0


def sides(first, second, even):
    first, second = first.astype(F32), second.astype(F32)
    return jnp.where(even, first, second), jnp.where(even, second, first)


def turn(plane):
    return BAND * (plane % LANES) + 2 * HALO


def stage(low_ref, high_ref, low, high):
    for plane in range(PLANES):
        here = slice(plane * HALO, (plane + 1) * HALO)
        low_ref[here, :] = low(plane)
        high_ref[here, :] = high(plane)


def send_rows(low_ref, high_ref, first_ref, second_ref):
    even = even_on("mer")
    low, high = low_ref[...], high_ref[...]
    first_ref[...] = jnp.where(even, high, low).astype(TRAVEL)
    second_ref[...] = jnp.where(even, low, high).astype(TRAVEL)


def rows_kernel(
    model_ref,
    control_ref,
    low_ref,
    high_ref,
    control_low,
    control_high,
    model_low,
    model_high,
    sems,
):
    ends = pl.ds(0, EDGE), pl.ds(ROWS - EDGE, EDGE)
    tips = pl.ds(0, 8), pl.ds(ROWS - 8, 8)
    copies = [
        pltpu.make_async_copy(control_ref.at[:, :, ends[0], :], control_low, sems.at[0]),
        pltpu.make_async_copy(control_ref.at[:, :, ends[1], :], control_high, sems.at[1]),
        pltpu.make_async_copy(model_ref.at[:, :, tips[0], :], model_low, sems.at[2]),
        pltpu.make_async_copy(model_ref.at[:, :, tips[1], :], model_high, sems.at[3]),
    ]
    for copy in copies:
        copy.start()
    for copy in copies:
        copy.wait()
    stage(
        low_ref,
        high_ref,
        lambda p: control_low[p // LEVELS, p % LEVELS, :HALO, :],
        lambda p: control_high[p // LEVELS, p % LEVELS, EDGE - HALO :, :],
    )
    for q in range(STEPPED):
        for ref, value in (
            (low_ref, model_low[q // HALF, q % HALF, :1, :]),
            (high_ref, model_high[q // HALF, q % HALF, 7:, :]),
        ):
            coarse = value.astype(TRAVEL).astype(F32)
            at = MODEL_ROW + q
            ref[at : at + 1, :] = coarse
            ref[at + STEPPED : at + STEPPED + 1, :] = value - coarse
    rest = MODEL_ROW + 2 * STEPPED
    low_ref[rest:, :] = jnp.zeros((LONG - rest, COLS), F32)
    high_ref[rest:, :] = jnp.zeros((LONG - rest, COLS), F32)


def start_kernel(bottom_ref, first_low, first_high, first_ref, second_ref, low_ref, high_ref):
    low_ref[...] = first_low[...]
    high_ref[...] = first_high[...]
    low_ref[DEPTH_ROW:MODEL_ROW, :] = bottom_ref[:HALO, :].astype(F32)
    high_ref[DEPTH_ROW:MODEL_ROW, :] = bottom_ref[ROWS - HALO :, :].astype(F32)
    send_rows(low_ref, high_ref, first_ref, second_ref)


def stand(value, low, high):
    blank = jnp.zeros((EDGE - HALO, COLS), F32)
    return jnp.concatenate([blank, low, value, high, blank], axis=0)


def stand_core(value):
    blank = jnp.zeros((EDGE, COLS), F32)
    return jnp.concatenate([blank, value, blank], axis=0)


def model_columns(model_ref, east_ref, west_ref):
    lane = lanes(ROWS)
    to_east = to_west = jnp.zeros((ROWS, COLS), F32)
    for q in range(STEPPED):
        value = model_ref[q // HALF, q % HALF]
        at = MODEL_LANE + 2 * q
        column = value[:, COLS - 1 :]
        coarse = column.astype(TRAVEL).astype(F32)
        to_east = jnp.where(lane == at, coarse, to_east)
        to_east = jnp.where(lane == at + 1, column - coarse, to_east)
        column = value[:, :1]
        coarse = column.astype(TRAVEL).astype(F32)
        to_west = jnp.where(lane == at - 1, coarse, to_west)
        to_west = jnp.where(lane == at - 2, column - coarse, to_west)
    east_ref[...] = to_east
    west_ref[...] = to_west


def raise_planes(read, first_ref, second_ref, low_ref, high_ref, tall_ref):
    low, high = mer_sides(first_ref[...], second_ref[...])
    low_ref[...] = low
    high_ref[...] = high
    blank = jnp.zeros((EDGE - HALO, COLS), F32)
    for plane in range(PLANES):
        here = slice(plane * HALO, (plane + 1) * HALO)
        tall_ref[plane, : EDGE - HALO, :] = blank
        tall_ref[plane, EDGE - HALO : EDGE, :] = low_ref[here, :]
        tall_ref[plane, EDGE : EDGE + ROWS, :] = read(plane)
        tall_ref[plane, EDGE + ROWS : EDGE + ROWS + HALO, :] = high_ref[here, :]
        tall_ref[plane, EDGE + ROWS + HALO :, :] = blank


def cut_bands(tall_ref, west_ref, east_ref):
    lane = lanes(TALL)
    blank = jnp.zeros((TALL, COLS), F32)
    to_east, to_west = blank, blank
    for group in range(BANDS):
        west = east = go_east = go_west = blank
        for j in range(LANES):
            plane = group * LANES + j
            turned = roll(tall_ref[plane], turn(plane))
            at = BAND * j
            west = jnp.where(window(lane, at + 2 * HALO, 2 * HALO), turned, west)
            east = jnp.where(window(lane, at, 2 * HALO), turned, east)
            go_east = jnp.where(window(lane, at + HALO, HALO), turned, go_east)
            go_west = jnp.where(window(lane, at + 2 * HALO, HALO), turned, go_west)
        west_ref[group] = west
        east_ref[group] = east
        to_east = to_east + roll(go_east, HALO * group)
        to_west = to_west + roll(go_west, HALO * group)
    return to_east, to_west


def send_columns(part, to_east, to_west, first_ref, second_ref):
    even = even_on("zon")
    here = slice(part * COLS, (part + 1) * COLS)
    first_ref[:, here] = jnp.where(even, to_east, to_west).astype(TRAVEL)
    second_ref[:, here] = jnp.where(even, to_west, to_east).astype(TRAVEL)


def first_columns_kernel(
    control_ref,
    bottom_ref,
    model_east_ref,
    model_west_ref,
    a_ref,
    b_ref,
    tall_ref,
    depth_ref,
    west_ref,
    east_ref,
    first_ref,
    second_ref,
    low_ref,
    high_ref,
):
    raise_planes(
        lambda p: control_ref[p // LEVELS, p % LEVELS], a_ref, b_ref, low_ref, high_ref, tall_ref
    )
    send_columns(0, *cut_bands(tall_ref, west_ref, east_ref), first_ref, second_ref)
    depth = stand(
        bottom_ref[...].astype(F32),
        low_ref[DEPTH_ROW:MODEL_ROW, :],
        high_ref[DEPTH_ROW:MODEL_ROW, :],
    )
    depth_ref[...] = depth
    mark = lanes(TALL) < HALO
    send_columns(
        1,
        jnp.where(mark, roll(depth, HALO), stand_core(model_east_ref[...])),
        jnp.where(mark, depth, stand_core(model_west_ref[...])),
        first_ref,
        second_ref,
    )


def next_columns_kernel(
    field_ref, a_ref, b_ref, tall_ref, west_ref, east_ref, first_ref, second_ref, low_ref, high_ref
):
    raise_planes(lambda p: field_ref[p], a_ref, b_ref, low_ref, high_ref, tall_ref)
    send_columns(0, *cut_bands(tall_ref, west_ref, east_ref), first_ref, second_ref)


def base_step(model_ref, depth_ref, a_ref, b_ref, base_ref, low_ref, high_ref, tall_ref):
    lane = lanes(ROWS)
    group = lax.axis_index("grp")
    low, high = mer_sides(a_ref[...], b_ref[...])
    low_ref[...] = low
    high_ref[...] = high
    core = slice(EDGE, EDGE + ROWS)
    south, north = slice(EDGE - 1, EDGE + ROWS - 1), slice(EDGE + 1, EDGE + ROWS + 1)
    depth = depth_ref[core, :]
    around = (
        depth,
        jnp.where(lane == COLS - 1, 0.0, roll(depth, -1)),
        jnp.where(lane == 0, 0.0, roll(depth, 1)),
        depth_ref[north, :],
        depth_ref[south, :],
    )
    for level in range(HALF):
        here = (group * HALF + level).astype(F32)
        wet, wet_e, wet_w, wet_n, wet_s = (jnp.where(v > here, 1.0, 0.0) for v in around)
        count = MIXING * (wet_e + wet_w + wet_n + wet_s)
        flow_x = 0.5 * ADVECTION * model_ref[2, level]
        flow_y = 0.5 * ADVECTION * model_ref[3, level]
        give_e, give_w = wet_e * (MIXING - flow_x), wet_w * (MIXING + flow_x)
        give_n, give_s = wet_n * (MIXING - flow_y), wet_s * (MIXING + flow_y)
        for field in range(FIELDS):
            at = MODEL_ROW + field * HALF + level
            value = model_ref[field, level]
            tall_ref[8 : 8 + ROWS, :] = value
            tall_ref[7:8, :] = low_ref[at : at + 1, :] + low_ref[at + STEPPED : at + STEPPED + 1, :]
            tall_ref[8 + ROWS : 9 + ROWS, :] = (
                high_ref[at : at + 1, :] + high_ref[at + STEPPED : at + STEPPED + 1, :]
            )
            base_ref[field, level] = wet * (
                value * (1.0 - count)
                + give_e * roll(value, -1)
                + give_w * roll(value, 1)
                + give_n * tall_ref[9 : 9 + ROWS, :]
                + give_s * tall_ref[7 : 7 + ROWS, :]
            )


def background_kernel(model_ref, depth_ref, base_ref, first_ref, second_ref, keep_ref, send_ref):
    lane = lanes(ROWS)
    group = lax.axis_index("grp")
    core = slice(EDGE, EDGE + ROWS)
    before, after = sides(first_ref[core, COLS:], second_ref[core, COLS:], even_on("zon"))
    at_west, at_east = lane == 0, lane == COLS - 1
    beside = jnp.where(at_west, roll(before, 1 - HALO), jnp.where(at_east, roll(after, -1), 0.0))
    depth = jnp.minimum(depth_ref[core, :], beside)
    columns = jnp.where(lane % 2 == 0, before + roll(before, -1), after + roll(after, 1))
    sign = jnp.where(at_west, 0.5 * ADVECTION, -0.5 * ADVECTION)
    for level in range(HALF):
        wet = depth > (group * HALF + level).astype(F32)
        gain = jnp.where(wet, MIXING + sign * model_ref[2, level], 0.0)
        loss = jnp.where(wet, MIXING, 0.0)
        for out_ref, pair in ((keep_ref, group), (send_ref, 1 - group)):
            for f in range(PAIR):
                field = PAIR * pair + f
                at = MODEL_LANE + 2 * (field * HALF + level)
                halo = pltpu.roll(columns, COLS - at, 1)
                out_ref[f, level] = base_ref[field, level] + (
                    gain * halo - loss * model_ref[field, level]
                )


def neighbour_sum(ref, index, start, rows):
    here = ref[index, pl.ds(start, rows), :]
    return here, (roll(here, -1) + roll(here, 1)) + (
        ref[index, pl.ds(start - 1, rows), :] + ref[index, pl.ds(start + 1, rows), :]
    )


def coefficients(mask_ref, count, keep_ref, give_ref):
    for index in range(count):
        wet, total = neighbour_sum(mask_ref, index, PAD, TALL)
        keep_ref[index, PAD : PAD + TALL, :] = wet * (1.0 - SMOOTHING * total)
        give_ref[index, PAD : PAD + TALL, :] = SMOOTHING * wet


def sweep_all(count, masks, keep_ref, give_ref, one_ref, two_ref):
    def sweep(source_ref, target_ref, start, rows):
        for index in range(count):
            here, total = neighbour_sum(source_ref, index, start, rows)
            at = pl.ds(start, rows)
            target_ref[index, at, :] = (
                keep_ref[index % masks, at, :] * here + give_ref[index % masks, at, :] * total
            )

    sweep(one_ref, two_ref, PAD, TALL)
    sweep(two_ref, one_ref, 2 * PAD, TALL - 2 * PAD)

    def step(index, carry):
        sweep(one_ref, two_ref, 2 * PAD, TALL - 2 * PAD)
        sweep(two_ref, one_ref, 2 * PAD, TALL - 2 * PAD)
        return carry

    lax.fori_loop(0, SWEEPS // 2 - 1, step, 0)


def clear_pads(ref, count):
    for index in range(count):
        ref[index, :PAD, :] = jnp.zeros((PAD, COLS), F32)
        ref[index, PAD + TALL :, :] = jnp.zeros((PAD, COLS), F32)


CORE = slice(PAD + EDGE, PAD + EDGE + ROWS)
BODY = slice(PAD, PAD + TALL)


def first_interior_kernel(
    tall_ref,
    depth_ref,
    model_ref,
    a_ref,
    b_ref,
    inner_ref,
    keep_ref,
    give_ref,
    base_ref,
    mask_ref,
    one_ref,
    two_ref,
    low_ref,
    high_ref,
    stand_ref,
):
    base_step(model_ref, depth_ref, a_ref, b_ref, base_ref, low_ref, high_ref, stand_ref)
    clear_pads(mask_ref, LEVELS)
    clear_pads(one_ref, PLANES)
    depth = depth_ref[...]
    for level in range(LEVELS):
        wet = jnp.where(depth > level, 1.0, 0.0)
        mask_ref[level, BODY, :] = wet
        for field in range(PAIR):
            plane = field * LEVELS + level
            one_ref[plane, BODY, :] = wet * tall_ref[plane]
    coefficients(mask_ref, LEVELS, keep_ref, give_ref)
    sweep_all(PLANES, LEVELS, keep_ref, give_ref, one_ref, two_ref)
    for plane in range(PLANES):
        inner_ref[plane] = one_ref[plane, CORE, :]


def next_interior_kernel(tall_ref, keep_ref, give_ref, inner_ref, one_ref, two_ref):
    clear_pads(one_ref, PLANES)
    for plane in range(PLANES):
        one_ref[plane, BODY, :] = tall_ref[plane]
    sweep_all(PLANES, LEVELS, keep_ref, give_ref, one_ref, two_ref)
    for plane in range(PLANES):
        inner_ref[plane] = one_ref[plane, CORE, :]


def fill_bands(first_ref, second_ref, west_ref, east_ref, one_ref, mask_ref):
    lane = lanes(TALL)
    before, after = sides(first_ref[:, :COLS], second_ref[:, :COLS], even_on("zon"))
    clear_pads(one_ref, 2 * BANDS)
    in_west = (lane >= HALO) & ((lane - HALO) % BAND < HALO)
    in_east = (lane >= 2 * HALO) & ((lane - 2 * HALO) % BAND < HALO)
    for group in range(BANDS):
        west = jnp.where(in_west, roll(before, -HALO * group), west_ref[group])
        east = jnp.where(in_east, roll(after, -HALO * group), east_ref[group])
        for index, value in ((group, west), (BANDS + group, east)):
            if mask_ref is not None:
                value = value * mask_ref[index, BODY, :]
            one_ref[index, BODY, :] = value


def join_bands(one_ref, plane, inner, lane):
    group, j = divmod(plane, LANES)
    value = jnp.where(
        window(lane, BAND * j + 2 * HALO, HALO),
        one_ref[group, CORE, :],
        one_ref[BANDS + group, CORE, :],
    )
    edge = (lane < HALO) | (lane >= COLS - HALO)
    return jnp.where(edge, roll(value, -turn(plane)), inner)


def first_bands_kernel(
    first_ref,
    second_ref,
    west_ref,
    east_ref,
    depth_ref,
    inner_ref,
    out_ref,
    keep_ref,
    give_ref,
    mask_ref,
    one_ref,
    two_ref,
):
    tall_lane = lanes(TALL)
    clear_pads(mask_ref, 2 * BANDS)
    before, after = sides(first_ref[:, COLS:], second_ref[:, COLS:], even_on("zon"))
    depth = depth_ref[...]
    blank = jnp.zeros((TALL, COLS), F32)
    west, east = [blank] * BANDS, [blank] * BANDS
    for j in range(LANES):
        at = BAND * j
        turned = roll(depth, turn(j))
        low = jnp.where(window(tall_lane, at + HALO, HALO), roll(before, at + HALO), turned)
        high = jnp.where(window(tall_lane, at + 2 * HALO, HALO), roll(after, at + 2 * HALO), turned)
        for group in range(BANDS):
            level = (group * LANES + j) % LEVELS
            west[group] = jnp.where(
                window(tall_lane, at + HALO, BAND), jnp.where(low > level, 1.0, 0.0), west[group]
            )
            east[group] = jnp.where(
                window(tall_lane, at, BAND), jnp.where(high > level, 1.0, 0.0), east[group]
            )
    for group in range(BANDS):
        mask_ref[group, BODY, :] = west[group]
        mask_ref[BANDS + group, BODY, :] = east[group]
    coefficients(mask_ref, 2 * BANDS, keep_ref, give_ref)
    fill_bands(first_ref, second_ref, west_ref, east_ref, one_ref, mask_ref)
    sweep_all(2 * BANDS, 2 * BANDS, keep_ref, give_ref, one_ref, two_ref)
    lane = lanes(ROWS)
    for plane in range(PLANES):
        out_ref[plane] = join_bands(one_ref, plane, inner_ref[plane], lane)


def gradient_kernel(
    first_ref,
    second_ref,
    west_ref,
    east_ref,
    inner_ref,
    keep_ref,
    give_ref,
    control_ref,
    out_ref,
    one_ref,
    two_ref,
):
    fill_bands(first_ref, second_ref, west_ref, east_ref, one_ref, None)
    sweep_all(2 * BANDS, 2 * BANDS, keep_ref, give_ref, one_ref, two_ref)
    lane = lanes(ROWS)
    for plane in range(PLANES):
        f, k = divmod(plane, LEVELS)
        out_ref[f, k] = control_ref[f, k] + join_bands(one_ref, plane, inner_ref[plane], lane)


def split(value):
    coarse = value.astype(jnp.bfloat16)
    return jnp.concatenate([coarse, (value - coarse.astype(F32)).astype(jnp.bfloat16)], axis=1)


def join(value):
    return value[:, :COLS] + value[:, COLS:]


def prepare_kernel(*refs):
    count_ref, model_ref, error_ref, bottom_ref, *observed_refs = refs[:8]
    corner_ref, weight_ref, value_ref, precision_ref = observed_refs
    east_ref, west_ref, scale_ref, pick_ref, back_ref, lower_ref, upper_ref, want_ref = refs[8:]
    model_columns(model_ref, east_ref, west_ref)
    depth = bottom_ref[...]
    for plane in range(PLANES):
        f, k = divmod(plane, LEVELS)
        scale_ref[plane] = jnp.where(depth > k, error_ref[f, k], 0.0)
    slots = corner_ref.shape[-1]
    cells = PLANES * ROWS
    corner = corner_ref[0, 0]
    row = (corner >> 7).astype(F32)
    column = (corner & (COLS - 1)).astype(F32)
    stacked = jnp.concatenate(
        [weight_ref[0, 0, 0], value_ref[0, 0], precision_ref[0, 0], row, column], axis=0
    )
    tall = jnp.transpose(stacked)
    wide_row = lax.broadcasted_iota(jnp.int32, (slots, cells), 1).astype(F32)
    tall_row = lax.broadcasted_iota(jnp.int32, (cells, slots), 0).astype(F32)
    for step in range(2):
        here = slice(step * slots, (step + 1) * slots)
        pick_ref[here, :] = jnp.where(wide_row == tall[:, 6:7] + step, 1.0, 0.0).astype(jnp.bfloat16)
        back_ref[:, here] = jnp.where(tall_row == row + step, 1.0, 0.0).astype(jnp.bfloat16)
    lane = lanes(slots).astype(F32)
    at, beside = lane == tall[:, 7:8], lane == tall[:, 7:8] + 1.0
    lower_ref[...] = jnp.where(at, tall[:, 0:1], jnp.where(beside, tall[:, 1:2], 0.0))
    upper_ref[...] = jnp.where(at, tall[:, 2:3], jnp.where(beside, tall[:, 3:4], 0.0))
    live = lax.broadcasted_iota(jnp.int32, (slots, 8), 0) < count_ref[0]
    want_ref[...] = jnp.where(live, tall, 0.0)


def observe_kernel(
    smooth_ref,
    scale_ref,
    keep_ref,
    other_ref,
    pick_ref,
    back_ref,
    lower_ref,
    upper_ref,
    want_ref,
    field_ref,
    first_ref,
    second_ref,
    total_ref,
    low_ref,
    high_ref,
):
    group = lax.axis_index("grp")
    slots = want_ref.shape[0]
    for plane in range(PLANES):
        f, k = divmod(plane, LEVELS)
        held = group == k // HALF
        prior = jnp.where(held, keep_ref[f, k % HALF], other_ref[f, k % HALF])
        total_ref[plane * ROWS : (plane + 1) * ROWS, :] = (
            scale_ref[plane] * smooth_ref[plane] + prior
        )
    seen = join(jnp.dot(pick_ref[...], split(total_ref[...]), preferred_element_type=F32))
    lower, upper = lower_ref[...], upper_ref[...]
    observed = jnp.sum(lower * seen[:slots] + upper * seen[slots:], axis=1, keepdims=True)
    misfit = want_ref[:, 5:6] * (observed - want_ref[:, 4:5])
    spread = jnp.concatenate([lower * misfit, upper * misfit], axis=0)
    total_ref[...] = join(jnp.dot(back_ref[...], split(spread), preferred_element_type=F32))
    for plane in range(PLANES):
        field_ref[plane] = scale_ref[plane] * total_ref[plane * ROWS : (plane + 1) * ROWS, :]
    stage(
        low_ref,
        high_ref,
        lambda p: field_ref[p, :HALO, :],
        lambda p: field_ref[p, ROWS - HALO :, :],
    )
    blank = jnp.zeros((SHORT - DEPTH_ROW, COLS), F32)
    low_ref[DEPTH_ROW:, :] = blank
    high_ref[DEPTH_ROW:, :] = blank
    send_rows(low_ref, high_ref, first_ref, second_ref)


def call(kernel, outs, scratch=(), remote=0, work=0):
    space = pl.ANY if remote else VMEM

    def run(*args):
        return pl.pallas_call(
            kernel,
            out_shape=[jax.ShapeDtypeStruct(shape, kind) for shape, kind in outs],
            in_specs=[pl.BlockSpec(memory_space=space) for _ in args],
            out_specs=[pl.BlockSpec(memory_space=VMEM) for _ in outs],
            scratch_shapes=list(scratch),
            compiler_params=pltpu.CompilerParams(
                vmem_limit_bytes=int((remote or GRANT) * 2**20)
            ),
            cost_estimate=pl.CostEstimate(
                flops=work, bytes_accessed=work // 10, transcendentals=0
            )
            if work
            else None,
            name=kernel.__name__.removesuffix("_kernel"),
        )(*args)

    return run


def swap(value, axis, shift):
    size = lax.axis_size(axis)
    pairs = []
    for i in range(shift, size, 2):
        j = (i + 1) % size
        pairs += [(i, j), (j, i)]
    return lax.ppermute(value, axis, pairs)


def exchange(first, second, axis):
    return swap(second, axis, 1), swap(first, axis, 0)


FULL = ((PLANES, ROWS, COLS), F32)
RAISED = ((PLANES, TALL, COLS), F32)
SIDE = ((BANDS, TALL, COLS), F32)
STEP = ((FIELDS, HALF, ROWS, COLS), F32)
PART = ((PAIR, HALF, ROWS, COLS), F32)
MASKS = ((LEVELS, DEEP, COLS), F32)
STRIP = ((2 * BANDS, DEEP, COLS), F32)


def rows_of(count):
    return ((count, COLS), TRAVEL)


def columns_of(count):
    return ((TALL, count * COLS), TRAVEL)


def body(
    model_state,
    control,
    error_std,
    bottom_level,
    obs_count,
    obs_corner,
    obs_weight,
    obs_value,
    obs_precision,
):
    dma = pltpu.SemaphoreType.DMA
    long, short = VMEM((LONG, COLS), F32), VMEM((SHORT, COLS), F32)
    low, high = call(
        rows_kernel,
        [((LONG, COLS), F32)] * 2,
        [VMEM((PAIR, LEVELS, EDGE, COLS), F32)] * 2
        + [VMEM((FIELDS, HALF, 8, COLS), F32)] * 2
        + [dma((4,))],
        remote=GRANT_MOST,
    )(model_state, control)
    first, second = call(start_kernel, [rows_of(LONG)] * 2, [long, long])(bottom_level, low, high)
    mer = exchange(first, second, "mer")
    slots = obs_corner.shape[-1]
    inputs = (
        obs_count,
        model_state,
        error_std,
        bottom_level,
        obs_corner,
        obs_weight,
        obs_value,
        obs_precision,
    )
    model_east, model_west, scale, *operators = call(
        prepare_kernel,
        [((ROWS, COLS), F32)] * 2
        + [FULL]
        + [((2 * slots, PLANES * ROWS), jnp.bfloat16), ((PLANES * ROWS, 2 * slots), jnp.bfloat16)]
        + [((slots, COLS), F32)] * 2
        + [((slots, 8), F32)],
        work=10**7,
    )(*inputs)
    tall, depth, west, east, first, second = call(
        first_columns_kernel,
        [RAISED, ((TALL, COLS), F32), SIDE, SIDE, columns_of(2), columns_of(2)],
        [long, long],
    )(control, bottom_level, model_east, model_west, *mer)
    zon = exchange(first, second, "zon")
    inner, keep_coef, give_coef, base = call(
        first_interior_kernel,
        [FULL, MASKS, MASKS, STEP],
        [VMEM(*MASKS)]
        + [VMEM((PLANES, DEEP, COLS), F32)] * 2
        + [long, long, VMEM((ROWS + 16, COLS), F32)],
        work=10**7,
    )(tall, depth, model_state, *mer)
    keep, send = call(background_kernel, [PART, PART])(model_state, depth, base, *zon)
    other = lax.ppermute(send, "grp", [(0, 1), (1, 0)])
    smoothed, keep_band, give_band = call(
        first_bands_kernel, [FULL, STRIP, STRIP], [VMEM(*STRIP)] * 3, work=10**7
    )(*zon, west, east, depth, inner)
    field, first, second = call(
        observe_kernel,
        [FULL, rows_of(SHORT), rows_of(SHORT)],
        [VMEM((PLANES * ROWS, COLS), F32), short, short],
    )(smoothed, scale, keep, other, *operators)
    mer = exchange(first, second, "mer")
    tall, west, east, first, second = call(
        next_columns_kernel, [RAISED, SIDE, SIDE, columns_of(1), columns_of(1)], [short, short]
    )(field, *mer)
    zon = exchange(first, second, "zon")
    (inner,) = call(
        next_interior_kernel, [FULL], [VMEM((PLANES, DEEP, COLS), F32)] * 2, work=10**7
    )(tall, keep_coef, give_coef)
    return call(gradient_kernel, [(control.shape, F32)], [VMEM(*STRIP)] * 2)(
        *zon, west, east, inner, keep_band, give_band, control
    )[0]


def solution(mesh):
    return jax.shard_map(
        body,
        mesh=mesh,
        in_specs=(
            P(None, "grp", "mer", "zon"),
            P("grp", None, "mer", "zon"),
            P("grp", None, "mer", "zon"),
            P("mer", "zon"),
            P("grp", "mer", "zon"),
            P("grp", "mer", "zon", None),
            P("grp", "mer", "zon", None, None),
            P("grp", "mer", "zon", None),
            P("grp", "mer", "zon", None),
        ),
        out_specs=P("grp", None, "mer", "zon"),
        check_vma=False,
    )
```

```python
import jax
import jax.numpy as jnp
from jax import lax
from jax.experimental import pallas as pl
from jax.experimental.pallas import tpu as pltpu
from jax.sharding import PartitionSpec as P

SWEEPS = 10
SMOOTHING = 0.2
ADVECTION = 0.1
MIXING = 0.15

PAIR = 2
LEVELS = 6
HALF = 3
FIELDS = 4
PLANES = PAIR * LEVELS
STEPPED = FIELDS * HALF
ROWS = 64
COLS = 128
HALO = SWEEPS
EDGE = 16
TALL = ROWS + 2 * EDGE
PAD = 8
DEEP = TALL + 2 * PAD
BAND = 2 * HALO + 1
BANDS = 2 * PAIR
DEPTH_ROW = PLANES * HALO
MODEL_ROW = DEPTH_ROW + HALO
LONG = 160
SHORT = 128
MODEL_LANE = 16
TRAVEL = jnp.bfloat16
F32 = jnp.float32
VMEM = pltpu.VMEM
GRANT, GRANT_MOST = 24, 53.6


def lanes(rows):
    return lax.broadcasted_iota(jnp.int32, (rows, COLS), 1)


def window(lane, start, width):
    start %= COLS
    stop = start + width
    if stop > COLS:
        return (lane >= start) | (lane < stop - COLS)
    return (lane >= start) & (lane < stop)


def roll(value, shift):
    shift %= COLS
    return value if shift == 0 else pltpu.roll(value, shift, 1)


def mer_sides(first, second):
    low, high = sides(first, second, even_on("mer"))
    index = lax.axis_index("mer")
    return jnp.where(index == 0, 0.0, low), jnp.where(index == lax.axis_size("mer") - 1, 0.0, high)


def even_on(axis):
    return lax.axis_index(axis) % 2 == 0


def sides(first, second, even):
    first, second = first.astype(F32), second.astype(F32)
    return jnp.where(even, first, second), jnp.where(even, second, first)


def turn(level):
    return BAND * level + HALO + 1


def stage(low_ref, high_ref, low, high):
    for plane in range(PLANES):
        here = slice(plane * HALO, (plane + 1) * HALO)
        low_ref[here, :] = low(plane)
        high_ref[here, :] = high(plane)


def send_rows(low_ref, high_ref, first_ref, second_ref):
    even = even_on("mer")
    low, high = low_ref[...], high_ref[...]
    first_ref[...] = jnp.where(even, high, low).astype(TRAVEL)
    second_ref[...] = jnp.where(even, low, high).astype(TRAVEL)


def rows_kernel(
    model_ref,
    control_ref,
    low_ref,
    high_ref,
    control_low,
    control_high,
    model_low,
    model_high,
    sems,
):
    ends = pl.ds(0, EDGE), pl.ds(ROWS - EDGE, EDGE)
    tips = pl.ds(0, 8), pl.ds(ROWS - 8, 8)
    copies = [
        pltpu.make_async_copy(control_ref.at[:, :, ends[0], :], control_low, sems.at[0]),
        pltpu.make_async_copy(control_ref.at[:, :, ends[1], :], control_high, sems.at[1]),
        pltpu.make_async_copy(model_ref.at[:, :, tips[0], :], model_low, sems.at[2]),
        pltpu.make_async_copy(model_ref.at[:, :, tips[1], :], model_high, sems.at[3]),
    ]
    for copy in copies:
        copy.start()
    for copy in copies:
        copy.wait()
    stage(
        low_ref,
        high_ref,
        lambda p: control_low[p // LEVELS, p % LEVELS, :HALO, :],
        lambda p: control_high[p // LEVELS, p % LEVELS, EDGE - HALO :, :],
    )
    for q in range(STEPPED):
        for ref, value in (
            (low_ref, model_low[q // HALF, q % HALF, :1, :]),
            (high_ref, model_high[q // HALF, q % HALF, 7:, :]),
        ):
            coarse = value.astype(TRAVEL).astype(F32)
            at = MODEL_ROW + q
            ref[at : at + 1, :] = coarse
            ref[at + STEPPED : at + STEPPED + 1, :] = value - coarse
    rest = MODEL_ROW + 2 * STEPPED
    low_ref[rest:, :] = jnp.zeros((LONG - rest, COLS), F32)
    high_ref[rest:, :] = jnp.zeros((LONG - rest, COLS), F32)


def start_kernel(bottom_ref, first_low, first_high, first_ref, second_ref, low_ref, high_ref):
    low_ref[...] = first_low[...]
    high_ref[...] = first_high[...]
    low_ref[DEPTH_ROW:MODEL_ROW, :] = bottom_ref[:HALO, :].astype(F32)
    high_ref[DEPTH_ROW:MODEL_ROW, :] = bottom_ref[ROWS - HALO :, :].astype(F32)
    send_rows(low_ref, high_ref, first_ref, second_ref)


def stand(value, low, high):
    blank = jnp.zeros((EDGE - HALO, COLS), F32)
    return jnp.concatenate([blank, low, value, high, blank], axis=0)


def stand_core(value):
    blank = jnp.zeros((EDGE, COLS), F32)
    return jnp.concatenate([blank, value, blank], axis=0)


def model_columns(model_ref, east_ref, west_ref):
    lane = lanes(ROWS)
    to_east = to_west = jnp.zeros((ROWS, COLS), F32)
    for q in range(STEPPED):
        value = model_ref[q // HALF, q % HALF]
        at = MODEL_LANE + 2 * q
        column = value[:, COLS - 1 :]
        coarse = column.astype(TRAVEL).astype(F32)
        to_east = jnp.where(lane == at, coarse, to_east)
        to_east = jnp.where(lane == at + 1, column - coarse, to_east)
        column = value[:, :1]
        coarse = column.astype(TRAVEL).astype(F32)
        to_west = jnp.where(lane == at - 1, coarse, to_west)
        to_west = jnp.where(lane == at - 2, column - coarse, to_west)
    east_ref[...] = to_east
    west_ref[...] = to_west


def raise_planes(read, first_ref, second_ref, low_ref, high_ref, tall_ref):
    low, high = mer_sides(first_ref[...], second_ref[...])
    low_ref[...] = low
    high_ref[...] = high
    blank = jnp.zeros((EDGE - HALO, COLS), F32)
    for plane in range(PLANES):
        here = slice(plane * HALO, (plane + 1) * HALO)
        tall_ref[plane, : EDGE - HALO, :] = blank
        tall_ref[plane, EDGE - HALO : EDGE, :] = low_ref[here, :]
        tall_ref[plane, EDGE : EDGE + ROWS, :] = read(plane)
        tall_ref[plane, EDGE + ROWS : EDGE + ROWS + HALO, :] = high_ref[here, :]
        tall_ref[plane, EDGE + ROWS + HALO :, :] = blank


def turn_planes(tall_ref, turned_ref):
    lane = lanes(TALL)
    to_east, to_west = [], []
    for f in range(PAIR):
        go_east = go_west = jnp.zeros((TALL, COLS), F32)
        for k in range(LEVELS):
            turned = roll(tall_ref[f * LEVELS + k], turn(k))
            turned_ref[f * LEVELS + k] = turned
            at = BAND * k
            go_east = jnp.where(window(lane, at + 1, HALO), turned, go_east)
            go_west = jnp.where(window(lane, at + 1 + HALO, HALO), turned, go_west)
        to_east.append(go_east)
        to_west.append(go_west)
    return to_east[0] + roll(to_east[1], HALO), to_west[0] + roll(to_west[1], -HALO)


def send_columns(part, to_east, to_west, first_ref, second_ref):
    even = even_on("zon")
    here = slice(part * COLS, (part + 1) * COLS)
    first_ref[:, here] = jnp.where(even, to_east, to_west).astype(TRAVEL)
    second_ref[:, here] = jnp.where(even, to_west, to_east).astype(TRAVEL)


def first_columns_kernel(
    control_ref,
    bottom_ref,
    model_east_ref,
    model_west_ref,
    a_ref,
    b_ref,
    turned_ref,
    depth_ref,
    first_ref,
    second_ref,
    low_ref,
    high_ref,
    tall_ref,
):
    raise_planes(
        lambda p: control_ref[p // LEVELS, p % LEVELS], a_ref, b_ref, low_ref, high_ref, tall_ref
    )
    send_columns(0, *turn_planes(tall_ref, turned_ref), first_ref, second_ref)
    depth = stand(
        bottom_ref[...].astype(F32),
        low_ref[DEPTH_ROW:MODEL_ROW, :],
        high_ref[DEPTH_ROW:MODEL_ROW, :],
    )
    depth_ref[...] = depth
    mark = lanes(TALL) < HALO
    send_columns(
        1,
        jnp.where(mark, roll(depth, HALO), stand_core(model_east_ref[...])),
        jnp.where(mark, depth, stand_core(model_west_ref[...])),
        first_ref,
        second_ref,
    )


def next_columns_kernel(
    field_ref, a_ref, b_ref, turned_ref, first_ref, second_ref, low_ref, high_ref, tall_ref
):
    raise_planes(lambda p: field_ref[p], a_ref, b_ref, low_ref, high_ref, tall_ref)
    send_columns(0, *turn_planes(tall_ref, turned_ref), first_ref, second_ref)


def base_step(model_ref, depth_ref, a_ref, b_ref, base_ref, low_ref, high_ref, tall_ref):
    lane = lanes(ROWS)
    group = lax.axis_index("grp")
    low, high = mer_sides(a_ref[...], b_ref[...])
    low_ref[...] = low
    high_ref[...] = high
    core = slice(EDGE, EDGE + ROWS)
    south, north = slice(EDGE - 1, EDGE + ROWS - 1), slice(EDGE + 1, EDGE + ROWS + 1)
    depth = depth_ref[core, :]
    around = (
        depth,
        jnp.where(lane == COLS - 1, 0.0, roll(depth, -1)),
        jnp.where(lane == 0, 0.0, roll(depth, 1)),
        depth_ref[north, :],
        depth_ref[south, :],
    )
    for level in range(HALF):
        here = (group * HALF + level).astype(F32)
        wet, wet_e, wet_w, wet_n, wet_s = (jnp.where(v > here, 1.0, 0.0) for v in around)
        count = MIXING * (wet_e + wet_w + wet_n + wet_s)
        flow_x = 0.5 * ADVECTION * model_ref[2, level]
        flow_y = 0.5 * ADVECTION * model_ref[3, level]
        give_e, give_w = wet_e * (MIXING - flow_x), wet_w * (MIXING + flow_x)
        give_n, give_s = wet_n * (MIXING - flow_y), wet_s * (MIXING + flow_y)
        for field in range(FIELDS):
            at = MODEL_ROW + field * HALF + level
            value = model_ref[field, level]
            tall_ref[8 : 8 + ROWS, :] = value
            tall_ref[7:8, :] = low_ref[at : at + 1, :] + low_ref[at + STEPPED : at + STEPPED + 1, :]
            tall_ref[8 + ROWS : 9 + ROWS, :] = (
                high_ref[at : at + 1, :] + high_ref[at + STEPPED : at + STEPPED + 1, :]
            )
            base_ref[field, level] = wet * (
                value * (1.0 - count)
                + give_e * roll(value, -1)
                + give_w * roll(value, 1)
                + give_n * tall_ref[9 : 9 + ROWS, :]
                + give_s * tall_ref[7 : 7 + ROWS, :]
            )


def background_kernel(model_ref, depth_ref, base_ref, first_ref, second_ref, keep_ref, send_ref):
    lane = lanes(ROWS)
    group = lax.axis_index("grp")
    core = slice(EDGE, EDGE + ROWS)
    before, after = sides(first_ref[core, COLS:], second_ref[core, COLS:], even_on("zon"))
    at_west, at_east = lane == 0, lane == COLS - 1
    beside = jnp.where(at_west, roll(before, 1 - HALO), jnp.where(at_east, roll(after, -1), 0.0))
    depth = jnp.minimum(depth_ref[core, :], beside)
    columns = jnp.where(lane % 2 == 0, before + roll(before, -1), after + roll(after, 1))
    sign = jnp.where(at_west, 0.5 * ADVECTION, -0.5 * ADVECTION)
    for level in range(HALF):
        wet = depth > (group * HALF + level).astype(F32)
        gain = jnp.where(wet, MIXING + sign * model_ref[2, level], 0.0)
        loss = jnp.where(wet, MIXING, 0.0)
        for out_ref, pair in ((keep_ref, group), (send_ref, 1 - group)):
            for f in range(PAIR):
                field = PAIR * pair + f
                at = MODEL_LANE + 2 * (field * HALF + level)
                halo = pltpu.roll(columns, COLS - at, 1)
                out_ref[f, level] = base_ref[field, level] + (
                    gain * halo - loss * model_ref[field, level]
                )


def neighbour_sum(ref, index, start, rows):
    here = ref[index, pl.ds(start, rows), :]
    return here, (roll(here, -1) + roll(here, 1)) + (
        ref[index, pl.ds(start - 1, rows), :] + ref[index, pl.ds(start + 1, rows), :]
    )


def coefficients(mask_ref, count, keep_ref, give_ref):
    for index in range(count):
        wet, total = neighbour_sum(mask_ref, index, PAD, TALL)
        keep_ref[index, PAD : PAD + TALL, :] = wet * (1.0 - SMOOTHING * total)
        give_ref[index, PAD : PAD + TALL, :] = SMOOTHING * wet


def sweep_all(sweep):
    sweep(0, 0, PAD, TALL)
    sweep(1, 1, 2 * PAD, TALL - 2 * PAD)

    def pair(step, carry):
        sweep(2 * step + 2, 0, 2 * PAD, TALL - 2 * PAD)
        sweep(2 * step + 3, 1, 2 * PAD, TALL - 2 * PAD)
        return carry

    lax.fori_loop(0, SWEEPS // 2 - 1, pair, 0)


def sweep_planes(keep_ref, give_ref, one_ref, two_ref, record_refs):
    def sweep(index, odd, start, rows):
        source_ref, target_ref = (two_ref, one_ref) if odd else (one_ref, two_ref)
        at = pl.ds(start, rows)
        lane = lanes(rows)
        for f in range(PAIR):
            west = east = jnp.zeros((rows, COLS), F32)
            for k in range(LEVELS):
                plane = f * LEVELS + k
                here, total = neighbour_sum(source_ref, plane, start, rows)
                target_ref[plane, at, :] = keep_ref[k, at, :] * here + give_ref[k, at, :] * total
                west = jnp.where(lane == BAND * (k + 1), here, west)
                east = jnp.where(lane == BAND * k, here, east)
            record_refs[f][index, at, :] = west
            record_refs[PAIR + f][index, at, :] = east

    sweep_all(sweep)


def sweep_bands(keep_ref, give_ref, one_ref, two_ref, record_refs):
    def sweep(index, odd, start, rows):
        source_ref, target_ref = (two_ref, one_ref) if odd else (one_ref, two_ref)
        at = pl.ds(start, rows)
        for tile in range(BANDS):
            here = source_ref[tile, at, :] + record_refs[tile][index, at, :]
            total = (roll(here, -1) + roll(here, 1)) + (
                source_ref[tile, pl.ds(start - 1, rows), :]
                + source_ref[tile, pl.ds(start + 1, rows), :]
            )
            side = tile // PAIR
            target_ref[tile, at, :] = keep_ref[side, at, :] * here + give_ref[side, at, :] * total

    sweep_all(sweep)


def clear_pads(ref, count):
    for index in range(count):
        ref[index, :PAD, :] = jnp.zeros((PAD, COLS), F32)
        ref[index, PAD + TALL :, :] = jnp.zeros((PAD, COLS), F32)


CORE = slice(PAD + EDGE, PAD + EDGE + ROWS)
BODY = slice(PAD, PAD + TALL)


def bands_of(one_ref, bands_ref):
    lane = lanes(TALL)
    for f in range(PAIR):
        west = east = jnp.zeros((TALL, COLS), F32)
        for k in range(LEVELS):
            value = one_ref[f * LEVELS + k, BODY, :]
            west = jnp.where(window(lane, BAND * k + 1 + HALO, HALO), value, west)
            east = jnp.where(window(lane, BAND * k + 1, HALO), value, east)
        bands_ref[f] = west
        bands_ref[PAIR + f] = east


def first_interior_kernel(
    turned_ref,
    depth_ref,
    model_ref,
    a_ref,
    b_ref,
    inner_ref,
    bands_ref,
    record_0,
    record_1,
    record_2,
    record_3,
    mask_ref,
    keep_ref,
    give_ref,
    base_ref,
    one_ref,
    two_ref,
    low_ref,
    high_ref,
    stand_ref,
):
    base_step(model_ref, depth_ref, a_ref, b_ref, base_ref, low_ref, high_ref, stand_ref)
    clear_pads(mask_ref, LEVELS)
    clear_pads(one_ref, PLANES)
    depth = depth_ref[...]
    for level in range(LEVELS):
        wet = roll(jnp.where(depth > level, 1.0, 0.0), turn(level))
        mask_ref[level, BODY, :] = wet
        for field in range(PAIR):
            plane = field * LEVELS + level
            one_ref[plane, BODY, :] = wet * turned_ref[plane]
    coefficients(mask_ref, LEVELS, keep_ref, give_ref)
    bands_of(one_ref, bands_ref)
    sweep_planes(keep_ref, give_ref, one_ref, two_ref, (record_0, record_1, record_2, record_3))
    for plane in range(PLANES):
        inner_ref[plane] = one_ref[plane, CORE, :]


def next_interior_kernel(
    turned_ref, keep_ref, give_ref, inner_ref, bands_ref, record_0, record_1, record_2, record_3, one_ref, two_ref
):
    clear_pads(one_ref, PLANES)
    for plane in range(PLANES):
        one_ref[plane, BODY, :] = turned_ref[plane]
    bands_of(one_ref, bands_ref)
    sweep_planes(keep_ref, give_ref, one_ref, two_ref, (record_0, record_1, record_2, record_3))
    for plane in range(PLANES):
        inner_ref[plane] = one_ref[plane, CORE, :]


def fill_bands(first_ref, second_ref, bands_ref, one_ref, mask_ref):
    inside = lanes(TALL) % BAND
    near, far = (inside >= 1) & (inside <= HALO), inside > HALO
    before, after = sides(first_ref[:, :COLS], second_ref[:, :COLS], even_on("zon"))
    clear_pads(one_ref, BANDS)
    for f in range(PAIR):
        west, east = (before, after) if f == 0 else (roll(before, -HALO), roll(after, HALO))
        if mask_ref is not None:
            west, east = west * mask_ref[0, BODY, :], east * mask_ref[1, BODY, :]
        one_ref[f, BODY, :] = jnp.where(near, west, bands_ref[f])
        one_ref[PAIR + f, BODY, :] = jnp.where(far, east, bands_ref[PAIR + f])


def join_bands(one_ref, plane, inner, lane):
    f, k = divmod(plane, LEVELS)
    at = BAND * k + 1
    value = jnp.where(window(lane, at, HALO), one_ref[PAIR + f, CORE, :], inner)
    value = jnp.where(window(lane, at + HALO, HALO), one_ref[f, CORE, :], value)
    return roll(value, -turn(k))


def first_bands_kernel(
    first_ref,
    second_ref,
    bands_ref,
    record_0,
    record_1,
    record_2,
    record_3,
    wet_ref,
    inner_ref,
    out_ref,
    keep_ref,
    give_ref,
    mask_ref,
    one_ref,
    two_ref,
):
    tall_lane = lanes(TALL)
    clear_pads(mask_ref, 2)
    before, after = sides(first_ref[:, COLS:], second_ref[:, COLS:], even_on("zon"))
    west = east = jnp.zeros((TALL, COLS), F32)
    for k in range(LEVELS):
        at = BAND * k
        wet = wet_ref[k, BODY, :]
        low = jnp.where(roll(before, at + 1) > k, 1.0, 0.0)
        high = jnp.where(roll(after, at + 1 + HALO) > k, 1.0, 0.0)
        west = jnp.where(window(tall_lane, at + 1, HALO), low, west)
        west = jnp.where(window(tall_lane, at + 1 + HALO, HALO + 1), wet, west)
        east = jnp.where(window(tall_lane, at, HALO + 1), wet, east)
        east = jnp.where(window(tall_lane, at + 1 + HALO, HALO), high, east)
    mask_ref[0, BODY, :] = west
    mask_ref[1, BODY, :] = east
    inside = jnp.where(tall_lane % BAND == 0, 0.0, 1.0)
    for side in range(2):
        wet, total = neighbour_sum(mask_ref, side, PAD, TALL)
        keep_ref[side, BODY, :] = inside * (wet * (1.0 - SMOOTHING * total))
        give_ref[side, BODY, :] = inside * (SMOOTHING * wet)
    fill_bands(first_ref, second_ref, bands_ref, one_ref, mask_ref)
    sweep_bands(keep_ref, give_ref, one_ref, two_ref, (record_0, record_1, record_2, record_3))
    lane = lanes(ROWS)
    for plane in range(PLANES):
        out_ref[plane] = join_bands(one_ref, plane, inner_ref[plane], lane)


def gradient_kernel(
    first_ref,
    second_ref,
    bands_ref,
    record_0,
    record_1,
    record_2,
    record_3,
    inner_ref,
    keep_ref,
    give_ref,
    control_ref,
    out_ref,
    one_ref,
    two_ref,
):
    fill_bands(first_ref, second_ref, bands_ref, one_ref, None)
    sweep_bands(keep_ref, give_ref, one_ref, two_ref, (record_0, record_1, record_2, record_3))
    lane = lanes(ROWS)
    for plane in range(PLANES):
        f, k = divmod(plane, LEVELS)
        out_ref[f, k] = control_ref[f, k] + join_bands(one_ref, plane, inner_ref[plane], lane)


def split(value):
    coarse = value.astype(jnp.bfloat16)
    return jnp.concatenate([coarse, (value - coarse.astype(F32)).astype(jnp.bfloat16)], axis=1)


def join(value):
    return value[:, :COLS] + value[:, COLS:]


def prepare_kernel(*refs):
    count_ref, model_ref, error_ref, bottom_ref, *observed_refs = refs[:8]
    corner_ref, weight_ref, value_ref, precision_ref = observed_refs
    east_ref, west_ref, copy_ref, scale_ref, pick_ref, back_ref = refs[8:14]
    lower_ref, upper_ref, want_ref = refs[14:]
    copy_ref[...] = model_ref[...]
    model_columns(model_ref, east_ref, west_ref)
    depth = bottom_ref[...]
    for plane in range(PLANES):
        f, k = divmod(plane, LEVELS)
        scale_ref[plane] = jnp.where(depth > k, error_ref[f, k], 0.0)
    slots = corner_ref.shape[-1]
    cells = PLANES * ROWS
    corner = corner_ref[0, 0]
    row = (corner >> 7).astype(F32)
    column = (corner & (COLS - 1)).astype(F32)
    stacked = jnp.concatenate(
        [weight_ref[0, 0, 0], value_ref[0, 0], precision_ref[0, 0], row, column], axis=0
    )
    tall = jnp.transpose(stacked)
    wide_row = lax.broadcasted_iota(jnp.int32, (slots, cells), 1).astype(F32)
    tall_row = lax.broadcasted_iota(jnp.int32, (cells, slots), 0).astype(F32)
    for step in range(2):
        here = slice(step * slots, (step + 1) * slots)
        pick_ref[here, :] = jnp.where(wide_row == tall[:, 6:7] + step, 1.0, 0.0).astype(jnp.bfloat16)
        back_ref[:, here] = jnp.where(tall_row == row + step, 1.0, 0.0).astype(jnp.bfloat16)
    lane = lanes(slots).astype(F32)
    at, beside = lane == tall[:, 7:8], lane == tall[:, 7:8] + 1.0
    lower_ref[...] = jnp.where(at, tall[:, 0:1], jnp.where(beside, tall[:, 1:2], 0.0))
    upper_ref[...] = jnp.where(at, tall[:, 2:3], jnp.where(beside, tall[:, 3:4], 0.0))
    live = lax.broadcasted_iota(jnp.int32, (slots, 8), 0) < count_ref[0]
    want_ref[...] = jnp.where(live, tall, 0.0)


def observe_kernel(
    smooth_ref,
    scale_ref,
    keep_ref,
    other_ref,
    pick_ref,
    back_ref,
    lower_ref,
    upper_ref,
    want_ref,
    field_ref,
    first_ref,
    second_ref,
    total_ref,
    low_ref,
    high_ref,
):
    group = lax.axis_index("grp")
    slots = want_ref.shape[0]
    for plane in range(PLANES):
        f, k = divmod(plane, LEVELS)
        held = group == k // HALF
        prior = jnp.where(held, keep_ref[f, k % HALF], other_ref[f, k % HALF])
        total_ref[plane * ROWS : (plane + 1) * ROWS, :] = (
            scale_ref[plane] * smooth_ref[plane] + prior
        )
    seen = join(jnp.dot(pick_ref[...], split(total_ref[...]), preferred_element_type=F32))
    lower, upper = lower_ref[...], upper_ref[...]
    observed = jnp.sum(lower * seen[:slots] + upper * seen[slots:], axis=1, keepdims=True)
    misfit = want_ref[:, 5:6] * (observed - want_ref[:, 4:5])
    spread = jnp.concatenate([lower * misfit, upper * misfit], axis=0)
    total_ref[...] = join(jnp.dot(back_ref[...], split(spread), preferred_element_type=F32))
    for plane in range(PLANES):
        field_ref[plane] = scale_ref[plane] * total_ref[plane * ROWS : (plane + 1) * ROWS, :]
    stage(
        low_ref,
        high_ref,
        lambda p: field_ref[p, :HALO, :],
        lambda p: field_ref[p, ROWS - HALO :, :],
    )
    blank = jnp.zeros((SHORT - DEPTH_ROW, COLS), F32)
    low_ref[DEPTH_ROW:, :] = blank
    high_ref[DEPTH_ROW:, :] = blank
    send_rows(low_ref, high_ref, first_ref, second_ref)


def call(kernel, outs, scratch=(), remote=0, work=0):
    space = pl.ANY if remote else VMEM

    def run(*args):
        return pl.pallas_call(
            kernel,
            out_shape=[jax.ShapeDtypeStruct(shape, kind) for shape, kind in outs],
            in_specs=[pl.BlockSpec(memory_space=space) for _ in args],
            out_specs=[pl.BlockSpec(memory_space=VMEM) for _ in outs],
            scratch_shapes=list(scratch),
            compiler_params=pltpu.CompilerParams(
                vmem_limit_bytes=int((remote or GRANT) * 2**20)
            ),
            cost_estimate=pl.CostEstimate(
                flops=work, bytes_accessed=work // 10, transcendentals=0
            )
            if work
            else None,
            name=kernel.__name__.removesuffix("_kernel"),
        )(*args)

    return run


def swap(value, axis, shift):
    size = lax.axis_size(axis)
    pairs = []
    for i in range(shift, size, 2):
        j = (i + 1) % size
        pairs += [(i, j), (j, i)]
    return lax.ppermute(value, axis, pairs)


def exchange(first, second, axis):
    return swap(second, axis, 1), swap(first, axis, 0)


FULL = ((PLANES, ROWS, COLS), F32)
RAISED = ((PLANES, TALL, COLS), F32)
CUT = ((BANDS, TALL, COLS), F32)
RECORD = ((SWEEPS, DEEP, COLS), F32)
STEP = ((FIELDS, HALF, ROWS, COLS), F32)
PART = ((PAIR, HALF, ROWS, COLS), F32)
MASKS = ((LEVELS, DEEP, COLS), F32)
STRIP = ((BANDS, DEEP, COLS), F32)
SIDES = ((2, DEEP, COLS), F32)


def rows_of(count):
    return ((count, COLS), TRAVEL)


def columns_of(count):
    return ((TALL, count * COLS), TRAVEL)


def body(
    model_state,
    control,
    error_std,
    bottom_level,
    obs_count,
    obs_corner,
    obs_weight,
    obs_value,
    obs_precision,
):
    dma = pltpu.SemaphoreType.DMA
    long, short = VMEM((LONG, COLS), F32), VMEM((SHORT, COLS), F32)
    low, high = call(
        rows_kernel,
        [((LONG, COLS), F32)] * 2,
        [VMEM((PAIR, LEVELS, EDGE, COLS), F32)] * 2
        + [VMEM((FIELDS, HALF, 8, COLS), F32)] * 2
        + [dma((4,))],
        remote=GRANT_MOST,
    )(model_state, control)
    first, second = call(start_kernel, [rows_of(LONG)] * 2, [long, long])(bottom_level, low, high)
    mer = exchange(first, second, "mer")
    slots = obs_corner.shape[-1]
    inputs = (
        obs_count,
        model_state,
        error_std,
        bottom_level,
        obs_corner,
        obs_weight,
        obs_value,
        obs_precision,
    )
    model_east, model_west, model, scale, *operators = call(
        prepare_kernel,
        [((ROWS, COLS), F32)] * 2
        + [STEP, FULL]
        + [((2 * slots, PLANES * ROWS), jnp.bfloat16), ((PLANES * ROWS, 2 * slots), jnp.bfloat16)]
        + [((slots, COLS), F32)] * 2
        + [((slots, 8), F32)],
        work=10**7,
    )(*inputs)
    turned, depth, first, second = call(
        first_columns_kernel,
        [RAISED, ((TALL, COLS), F32), columns_of(2), columns_of(2)],
        [long, long, VMEM(*RAISED)],
    )(control, bottom_level, model_east, model_west, *mer)
    zon = exchange(first, second, "zon")
    deep = [VMEM((PLANES, DEEP, COLS), F32)] * 2
    inner, bands, *record, wet, keep_coef, give_coef, base = call(
        first_interior_kernel,
        [FULL, CUT] + [RECORD] * BANDS + [MASKS, MASKS, MASKS, STEP],
        deep + [long, long, VMEM((ROWS + 16, COLS), F32)],
        work=10**7,
    )(turned, depth, model, *mer)
    keep, send = call(background_kernel, [PART, PART])(model, depth, base, *zon)
    other = lax.ppermute(send, "grp", [(0, 1), (1, 0)])
    smoothed, keep_band, give_band = call(
        first_bands_kernel, [FULL, SIDES, SIDES], [VMEM(*SIDES)] + [VMEM(*STRIP)] * 2, work=10**7
    )(*zon, bands, *record, wet, inner)
    field, first, second = call(
        observe_kernel,
        [FULL, rows_of(SHORT), rows_of(SHORT)],
        [VMEM((PLANES * ROWS, COLS), F32), short, short],
    )(smoothed, scale, keep, other, *operators)
    mer = exchange(first, second, "mer")
    turned, first, second = call(
        next_columns_kernel,
        [RAISED, columns_of(1), columns_of(1)],
        [short, short, VMEM(*RAISED)],
    )(field, *mer)
    zon = exchange(first, second, "zon")
    inner, bands, *record = call(
        next_interior_kernel, [FULL, CUT] + [RECORD] * BANDS, deep, work=10**7
    )(turned, keep_coef, give_coef)
    return call(gradient_kernel, [(control.shape, F32)], [VMEM(*STRIP)] * 2)(
        *zon, bands, *record, inner, keep_band, give_band, control
    )[0]


def solution(mesh):
    return jax.shard_map(
        body,
        mesh=mesh,
        in_specs=(
            P(None, "grp", "mer", "zon"),
            P("grp", None, "mer", "zon"),
            P("grp", None, "mer", "zon"),
            P("mer", "zon"),
            P("grp", "mer", "zon"),
            P("grp", "mer", "zon", None),
            P("grp", "mer", "zon", None, None),
            P("grp", "mer", "zon", None),
            P("grp", "mer", "zon", None),
        ),
        out_specs=P("grp", None, "mer", "zon"),
        check_vma=False,
    )
```

```python
import jax
import jax.numpy as jnp
from jax import lax
from jax.experimental import pallas as pl
from jax.experimental.pallas import tpu as pltpu
from jax.sharding import PartitionSpec as P

SWEEPS = 10
SMOOTHING = 0.2
ADVECTION = 0.1
MIXING = 0.15

PAIR = 2
LEVELS = 6
HALF = 3
FIELDS = 4
PLANES = PAIR * LEVELS
STEPPED = FIELDS * HALF
ROWS = 64
COLS = 128
HALO = SWEEPS
EDGE = 16
TALL = ROWS + 2 * EDGE
PAD = 8
DEEP = TALL + 2 * PAD
BAND = 2 * HALO + 1
BANDS = 2 * PAIR
DEPTH_ROW = PLANES * HALO
MODEL_ROW = DEPTH_ROW + HALO
LONG = 160
SHORT = 128
MODEL_LANE = 16
TRAVEL = jnp.bfloat16
F32 = jnp.float32
VMEM = pltpu.VMEM
GRANT, GRANT_MOST = 24, 53.6


def lanes(rows):
    return lax.broadcasted_iota(jnp.int32, (rows, COLS), 1)


def window(lane, start, width):
    start %= COLS
    stop = start + width
    if stop > COLS:
        return (lane >= start) | (lane < stop - COLS)
    return (lane >= start) & (lane < stop)


def roll(value, shift):
    shift %= COLS
    return value if shift == 0 else pltpu.roll(value, shift, 1)


def mer_sides(first, second):
    low, high = sides(first, second, even_on("mer"))
    index = lax.axis_index("mer")
    return jnp.where(index == 0, 0.0, low), jnp.where(index == lax.axis_size("mer") - 1, 0.0, high)


def even_on(axis):
    return lax.axis_index(axis) % 2 == 0


def sides(first, second, even):
    first, second = first.astype(F32), second.astype(F32)
    return jnp.where(even, first, second), jnp.where(even, second, first)


def turn(level):
    return BAND * level + HALO + 1


def stage(low_ref, high_ref, low, high):
    for plane in range(PLANES):
        here = slice(plane * HALO, (plane + 1) * HALO)
        low_ref[here, :] = low(plane)
        high_ref[here, :] = high(plane)


def send_rows(low_ref, high_ref, first_ref, second_ref):
    even = even_on("mer")
    low, high = low_ref[...], high_ref[...]
    first_ref[...] = jnp.where(even, high, low).astype(TRAVEL)
    second_ref[...] = jnp.where(even, low, high).astype(TRAVEL)


def rows_kernel(
    model_ref,
    control_ref,
    low_ref,
    high_ref,
    control_low,
    control_high,
    model_low,
    model_high,
    sems,
):
    ends = pl.ds(0, EDGE), pl.ds(ROWS - EDGE, EDGE)
    tips = pl.ds(0, 8), pl.ds(ROWS - 8, 8)
    copies = [
        pltpu.make_async_copy(control_ref.at[:, :, ends[0], :], control_low, sems.at[0]),
        pltpu.make_async_copy(control_ref.at[:, :, ends[1], :], control_high, sems.at[1]),
        pltpu.make_async_copy(model_ref.at[:, :, tips[0], :], model_low, sems.at[2]),
        pltpu.make_async_copy(model_ref.at[:, :, tips[1], :], model_high, sems.at[3]),
    ]
    for copy in copies:
        copy.start()
    for copy in copies:
        copy.wait()
    stage(
        low_ref,
        high_ref,
        lambda p: control_low[p // LEVELS, p % LEVELS, :HALO, :],
        lambda p: control_high[p // LEVELS, p % LEVELS, EDGE - HALO :, :],
    )
    for q in range(STEPPED):
        for ref, value in (
            (low_ref, model_low[q // HALF, q % HALF, :1, :]),
            (high_ref, model_high[q // HALF, q % HALF, 7:, :]),
        ):
            coarse = value.astype(TRAVEL).astype(F32)
            at = MODEL_ROW + q
            ref[at : at + 1, :] = coarse
            ref[at + STEPPED : at + STEPPED + 1, :] = value - coarse
    rest = MODEL_ROW + 2 * STEPPED
    low_ref[rest:, :] = jnp.zeros((LONG - rest, COLS), F32)
    high_ref[rest:, :] = jnp.zeros((LONG - rest, COLS), F32)


def start_kernel(bottom_ref, first_low, first_high, first_ref, second_ref, low_ref, high_ref):
    low_ref[...] = first_low[...]
    high_ref[...] = first_high[...]
    low_ref[DEPTH_ROW:MODEL_ROW, :] = bottom_ref[:HALO, :].astype(F32)
    high_ref[DEPTH_ROW:MODEL_ROW, :] = bottom_ref[ROWS - HALO :, :].astype(F32)
    send_rows(low_ref, high_ref, first_ref, second_ref)


def stand(value, low, high):
    blank = jnp.zeros((EDGE - HALO, COLS), F32)
    return jnp.concatenate([blank, low, value, high, blank], axis=0)


def stand_core(value):
    blank = jnp.zeros((EDGE, COLS), F32)
    return jnp.concatenate([blank, value, blank], axis=0)


def model_columns(model_ref, east_ref, west_ref):
    lane = lanes(ROWS)
    to_east = to_west = jnp.zeros((ROWS, COLS), F32)
    for q in range(STEPPED):
        value = model_ref[q // HALF, q % HALF]
        at = MODEL_LANE + 2 * q
        column = value[:, COLS - 1 :]
        coarse = column.astype(TRAVEL).astype(F32)
        to_east = jnp.where(lane == at, coarse, to_east)
        to_east = jnp.where(lane == at + 1, column - coarse, to_east)
        column = value[:, :1]
        coarse = column.astype(TRAVEL).astype(F32)
        to_west = jnp.where(lane == at - 1, coarse, to_west)
        to_west = jnp.where(lane == at - 2, column - coarse, to_west)
    east_ref[...] = to_east
    west_ref[...] = to_west


def raise_planes(read, first_ref, second_ref, low_ref, high_ref, tall_ref):
    low, high = mer_sides(first_ref[...], second_ref[...])
    low_ref[...] = low
    high_ref[...] = high
    blank = jnp.zeros((EDGE - HALO, COLS), F32)
    for plane in range(PLANES):
        here = slice(plane * HALO, (plane + 1) * HALO)
        tall_ref[plane, : EDGE - HALO, :] = blank
        tall_ref[plane, EDGE - HALO : EDGE, :] = low_ref[here, :]
        tall_ref[plane, EDGE : EDGE + ROWS, :] = read(plane)
        tall_ref[plane, EDGE + ROWS : EDGE + ROWS + HALO, :] = high_ref[here, :]
        tall_ref[plane, EDGE + ROWS + HALO :, :] = blank


def turn_planes(tall_ref, turned_ref):
    lane = lanes(TALL)
    to_east, to_west = [], []
    for f in range(PAIR):
        go_east = go_west = jnp.zeros((TALL, COLS), F32)
        for k in range(LEVELS):
            turned = tall_ref[f * LEVELS + k]
            if turned_ref is not None:
                turned = roll(turned, turn(k))
                turned_ref[f * LEVELS + k] = turned
            at = BAND * k
            go_east = jnp.where(window(lane, at + 1, HALO), turned, go_east)
            go_west = jnp.where(window(lane, at + 1 + HALO, HALO), turned, go_west)
        to_east.append(go_east)
        to_west.append(go_west)
    return to_east[0] + roll(to_east[1], HALO), to_west[0] + roll(to_west[1], -HALO)


def send_columns(part, to_east, to_west, first_ref, second_ref):
    even = even_on("zon")
    here = slice(part * COLS, (part + 1) * COLS)
    first_ref[:, here] = jnp.where(even, to_east, to_west).astype(TRAVEL)
    second_ref[:, here] = jnp.where(even, to_west, to_east).astype(TRAVEL)


def first_columns_kernel(
    control_ref,
    bottom_ref,
    model_east_ref,
    model_west_ref,
    a_ref,
    b_ref,
    turned_ref,
    depth_ref,
    first_ref,
    second_ref,
    low_ref,
    high_ref,
    tall_ref,
):
    raise_planes(
        lambda p: control_ref[p // LEVELS, p % LEVELS], a_ref, b_ref, low_ref, high_ref, tall_ref
    )
    send_columns(0, *turn_planes(tall_ref, turned_ref), first_ref, second_ref)
    depth = stand(
        bottom_ref[...].astype(F32),
        low_ref[DEPTH_ROW:MODEL_ROW, :],
        high_ref[DEPTH_ROW:MODEL_ROW, :],
    )
    depth_ref[...] = depth
    mark = lanes(TALL) < HALO
    send_columns(
        1,
        jnp.where(mark, roll(depth, HALO), stand_core(model_east_ref[...])),
        jnp.where(mark, depth, stand_core(model_west_ref[...])),
        first_ref,
        second_ref,
    )


def next_columns_kernel(
    field_ref, a_ref, b_ref, turned_ref, first_ref, second_ref, low_ref, high_ref
):
    raise_planes(lambda p: field_ref[p], a_ref, b_ref, low_ref, high_ref, turned_ref)
    send_columns(0, *turn_planes(turned_ref, None), first_ref, second_ref)


def base_step(model_ref, depth_ref, a_ref, b_ref, base_ref, low_ref, high_ref, tall_ref):
    lane = lanes(ROWS)
    group = lax.axis_index("grp")
    low, high = mer_sides(a_ref[...], b_ref[...])
    low_ref[...] = low
    high_ref[...] = high
    core = slice(EDGE, EDGE + ROWS)
    south, north = slice(EDGE - 1, EDGE + ROWS - 1), slice(EDGE + 1, EDGE + ROWS + 1)
    depth = depth_ref[core, :]
    around = (
        depth,
        jnp.where(lane == COLS - 1, 0.0, roll(depth, -1)),
        jnp.where(lane == 0, 0.0, roll(depth, 1)),
        depth_ref[north, :],
        depth_ref[south, :],
    )
    for level in range(HALF):
        here = (group * HALF + level).astype(F32)
        wet, wet_e, wet_w, wet_n, wet_s = (jnp.where(v > here, 1.0, 0.0) for v in around)
        count = MIXING * (wet_e + wet_w + wet_n + wet_s)
        flow_x = 0.5 * ADVECTION * model_ref[2, level]
        flow_y = 0.5 * ADVECTION * model_ref[3, level]
        give_e, give_w = wet_e * (MIXING - flow_x), wet_w * (MIXING + flow_x)
        give_n, give_s = wet_n * (MIXING - flow_y), wet_s * (MIXING + flow_y)
        for field in range(FIELDS):
            at = MODEL_ROW + field * HALF + level
            value = model_ref[field, level]
            tall_ref[8 : 8 + ROWS, :] = value
            tall_ref[7:8, :] = low_ref[at : at + 1, :] + low_ref[at + STEPPED : at + STEPPED + 1, :]
            tall_ref[8 + ROWS : 9 + ROWS, :] = (
                high_ref[at : at + 1, :] + high_ref[at + STEPPED : at + STEPPED + 1, :]
            )
            base_ref[field, level] = wet * (
                value * (1.0 - count)
                + give_e * roll(value, -1)
                + give_w * roll(value, 1)
                + give_n * tall_ref[9 : 9 + ROWS, :]
                + give_s * tall_ref[7 : 7 + ROWS, :]
            )


def background_kernel(model_ref, depth_ref, base_ref, first_ref, second_ref, keep_ref, send_ref):
    lane = lanes(ROWS)
    group = lax.axis_index("grp")
    core = slice(EDGE, EDGE + ROWS)
    before, after = sides(first_ref[core, COLS:], second_ref[core, COLS:], even_on("zon"))
    at_west, at_east = lane == 0, lane == COLS - 1
    beside = jnp.where(at_west, roll(before, 1 - HALO), jnp.where(at_east, roll(after, -1), 0.0))
    depth = jnp.minimum(depth_ref[core, :], beside)
    columns = jnp.where(lane % 2 == 0, before + roll(before, -1), after + roll(after, 1))
    sign = jnp.where(at_west, 0.5 * ADVECTION, -0.5 * ADVECTION)
    for level in range(HALF):
        wet = depth > (group * HALF + level).astype(F32)
        gain = jnp.where(wet, MIXING + sign * model_ref[2, level], 0.0)
        loss = jnp.where(wet, MIXING, 0.0)
        for out_ref, pair in ((keep_ref, group), (send_ref, 1 - group)):
            for f in range(PAIR):
                field = PAIR * pair + f
                at = MODEL_LANE + 2 * (field * HALF + level)
                halo = pltpu.roll(columns, COLS - at, 1)
                out_ref[f, level] = base_ref[field, level] + (
                    gain * halo - loss * model_ref[field, level]
                )


def neighbour_sum(ref, index, start, rows):
    here = ref[index, pl.ds(start, rows), :]
    return here, (roll(here, -1) + roll(here, 1)) + (
        ref[index, pl.ds(start - 1, rows), :] + ref[index, pl.ds(start + 1, rows), :]
    )


def coefficients(mask_ref, count, keep_ref, give_ref):
    for index in range(count):
        wet, total = neighbour_sum(mask_ref, index, PAD, TALL)
        keep_ref[index, PAD : PAD + TALL, :] = wet * (1.0 - SMOOTHING * total)
        give_ref[index, PAD : PAD + TALL, :] = SMOOTHING * wet


def sweep_all(sweep):
    sweep(0, 0, PAD, TALL)
    sweep(1, 1, 2 * PAD, TALL - 2 * PAD)

    def pair(step, carry):
        sweep(2 * step + 2, 0, 2 * PAD, TALL - 2 * PAD)
        sweep(2 * step + 3, 1, 2 * PAD, TALL - 2 * PAD)
        return carry

    lax.fori_loop(0, SWEEPS // 2 - 1, pair, 0)


def sweep_planes(keep_ref, give_ref, one_ref, two_ref, record_refs):
    def sweep(index, odd, start, rows):
        source_ref, target_ref = (two_ref, one_ref) if odd else (one_ref, two_ref)
        at = pl.ds(start, rows)
        lane = lanes(rows)
        for f in range(PAIR):
            west = east = jnp.zeros((rows, COLS), F32)
            for k in range(LEVELS):
                plane = f * LEVELS + k
                here, total = neighbour_sum(source_ref, plane, start, rows)
                target_ref[plane, at, :] = keep_ref[k, at, :] * here + give_ref[k, at, :] * total
                west = jnp.where(lane == BAND * (k + 1), here, west)
                east = jnp.where(lane == BAND * k, here, east)
            record_refs[f][index, at, :] = west
            record_refs[PAIR + f][index, at, :] = east

    sweep_all(sweep)


def sweep_bands(keep_ref, give_ref, one_ref, two_ref, record_refs):
    def sweep(index, odd, start, rows):
        source_ref, target_ref = (two_ref, one_ref) if odd else (one_ref, two_ref)
        at = pl.ds(start, rows)
        for tile in range(BANDS):
            here = source_ref[tile, at, :] + record_refs[tile][index, at, :]
            total = (roll(here, -1) + roll(here, 1)) + (
                source_ref[tile, pl.ds(start - 1, rows), :]
                + source_ref[tile, pl.ds(start + 1, rows), :]
            )
            side = tile // PAIR
            target_ref[tile, at, :] = keep_ref[side, at, :] * here + give_ref[side, at, :] * total

    sweep_all(sweep)


def clear_pads(ref, count):
    for index in range(count):
        ref[index, :PAD, :] = jnp.zeros((PAD, COLS), F32)
        ref[index, PAD + TALL :, :] = jnp.zeros((PAD, COLS), F32)


CORE = slice(PAD + EDGE, PAD + EDGE + ROWS)
BODY = slice(PAD, PAD + TALL)


def bands_of(one_ref, bands_ref):
    lane = lanes(TALL)
    for f in range(PAIR):
        west = east = jnp.zeros((TALL, COLS), F32)
        for k in range(LEVELS):
            value = one_ref[f * LEVELS + k, BODY, :]
            west = jnp.where(window(lane, BAND * k + 1 + HALO, HALO), value, west)
            east = jnp.where(window(lane, BAND * k + 1, HALO), value, east)
        bands_ref[f] = west
        bands_ref[PAIR + f] = east


def first_interior_kernel(
    turned_ref,
    depth_ref,
    model_ref,
    a_ref,
    b_ref,
    inner_ref,
    bands_ref,
    record_0,
    record_1,
    record_2,
    record_3,
    mask_ref,
    keep_ref,
    give_ref,
    base_ref,
    one_ref,
    two_ref,
    low_ref,
    high_ref,
    stand_ref,
):
    base_step(model_ref, depth_ref, a_ref, b_ref, base_ref, low_ref, high_ref, stand_ref)
    clear_pads(mask_ref, LEVELS)
    clear_pads(one_ref, PLANES)
    depth = depth_ref[...]
    for level in range(LEVELS):
        wet = roll(jnp.where(depth > level, 1.0, 0.0), turn(level))
        mask_ref[level, BODY, :] = wet
        for field in range(PAIR):
            plane = field * LEVELS + level
            one_ref[plane, BODY, :] = wet * turned_ref[plane]
    coefficients(mask_ref, LEVELS, keep_ref, give_ref)
    bands_of(one_ref, bands_ref)
    sweep_planes(keep_ref, give_ref, one_ref, two_ref, (record_0, record_1, record_2, record_3))
    for plane in range(PLANES):
        inner_ref[plane] = one_ref[plane, CORE, :]


def next_interior_kernel(
    turned_ref, keep_ref, give_ref, inner_ref, bands_ref, record_0, record_1, record_2, record_3, one_ref, two_ref
):
    clear_pads(one_ref, PLANES)
    for plane in range(PLANES):
        one_ref[plane, BODY, :] = turned_ref[plane]
    bands_of(one_ref, bands_ref)
    sweep_planes(keep_ref, give_ref, one_ref, two_ref, (record_0, record_1, record_2, record_3))
    for plane in range(PLANES):
        inner_ref[plane] = one_ref[plane, CORE, :]


def fill_bands(first_ref, second_ref, bands_ref, one_ref, mask_ref):
    inside = lanes(TALL) % BAND
    near, far = (inside >= 1) & (inside <= HALO), inside > HALO
    before, after = sides(first_ref[:, :COLS], second_ref[:, :COLS], even_on("zon"))
    clear_pads(one_ref, BANDS)
    for f in range(PAIR):
        west, east = (before, after) if f == 0 else (roll(before, -HALO), roll(after, HALO))
        if mask_ref is not None:
            west, east = west * mask_ref[0, BODY, :], east * mask_ref[1, BODY, :]
        one_ref[f, BODY, :] = jnp.where(near, west, bands_ref[f])
        one_ref[PAIR + f, BODY, :] = jnp.where(far, east, bands_ref[PAIR + f])


def join_bands(one_ref, plane, inner, lane):
    f, k = divmod(plane, LEVELS)
    at = BAND * k + 1
    value = jnp.where(window(lane, at, HALO), one_ref[PAIR + f, CORE, :], inner)
    value = jnp.where(window(lane, at + HALO, HALO), one_ref[f, CORE, :], value)
    return roll(value, -turn(k))


def first_bands_kernel(
    first_ref,
    second_ref,
    bands_ref,
    record_0,
    record_1,
    record_2,
    record_3,
    wet_ref,
    inner_ref,
    out_ref,
    keep_ref,
    give_ref,
    mask_ref,
    one_ref,
    two_ref,
):
    tall_lane = lanes(TALL)
    clear_pads(mask_ref, 2)
    before, after = sides(first_ref[:, COLS:], second_ref[:, COLS:], even_on("zon"))
    west = east = jnp.zeros((TALL, COLS), F32)
    for k in range(LEVELS):
        at = BAND * k
        wet = wet_ref[k, BODY, :]
        low = jnp.where(roll(before, at + 1) > k, 1.0, 0.0)
        high = jnp.where(roll(after, at + 1 + HALO) > k, 1.0, 0.0)
        west = jnp.where(window(tall_lane, at + 1, HALO), low, west)
        west = jnp.where(window(tall_lane, at + 1 + HALO, HALO + 1), wet, west)
        east = jnp.where(window(tall_lane, at, HALO + 1), wet, east)
        east = jnp.where(window(tall_lane, at + 1 + HALO, HALO), high, east)
    mask_ref[0, BODY, :] = west
    mask_ref[1, BODY, :] = east
    inside = jnp.where(tall_lane % BAND == 0, 0.0, 1.0)
    for side in range(2):
        wet, total = neighbour_sum(mask_ref, side, PAD, TALL)
        keep_ref[side, BODY, :] = inside * (wet * (1.0 - SMOOTHING * total))
        give_ref[side, BODY, :] = inside * (SMOOTHING * wet)
    fill_bands(first_ref, second_ref, bands_ref, one_ref, mask_ref)
    sweep_bands(keep_ref, give_ref, one_ref, two_ref, (record_0, record_1, record_2, record_3))
    lane = lanes(ROWS)
    for plane in range(PLANES):
        out_ref[plane] = join_bands(one_ref, plane, inner_ref[plane], lane)


def gradient_kernel(
    first_ref,
    second_ref,
    bands_ref,
    record_0,
    record_1,
    record_2,
    record_3,
    inner_ref,
    keep_ref,
    give_ref,
    control_ref,
    out_ref,
    one_ref,
    two_ref,
    whole_ref,
    sems,
):
    fill_bands(first_ref, second_ref, bands_ref, one_ref, None)
    sweep_bands(keep_ref, give_ref, one_ref, two_ref, (record_0, record_1, record_2, record_3))
    lane = lanes(ROWS)
    copies = []
    for plane in range(PLANES):
        f, k = divmod(plane, LEVELS)
        whole_ref[f, k] = control_ref[f, k] + join_bands(one_ref, plane, inner_ref[plane], lane)
        part, last = divmod(plane, 3)
        if last == 2:
            here = pl.ds(k - 2, 3)
            copies.append(
                pltpu.make_async_copy(whole_ref.at[f, here], out_ref.at[f, here], sems.at[part])
            )
            copies[-1].start()
    for copy in copies:
        copy.wait()


def split(value):
    coarse = value.astype(jnp.bfloat16)
    return jnp.concatenate([coarse, (value - coarse.astype(F32)).astype(jnp.bfloat16)], axis=1)


def join(value):
    return value[:, :COLS] + value[:, COLS:]


def prepare_kernel(*refs):
    count_ref, model_ref, error_ref, bottom_ref, *observed_refs = refs[:8]
    corner_ref, weight_ref, value_ref, precision_ref = observed_refs
    east_ref, west_ref, copy_ref, scale_ref, turned_ref, pick_ref, back_ref = refs[8:15]
    lower_ref, upper_ref, lower_turned, upper_turned, value_out, gain_out = refs[15:]
    copy_ref[...] = model_ref[...]
    model_columns(model_ref, east_ref, west_ref)
    depth = bottom_ref[...]
    for plane in range(PLANES):
        f, k = divmod(plane, LEVELS)
        scale = jnp.where(depth > k, error_ref[f, k], 0.0)
        scale_ref[plane] = scale
        turned_ref[plane] = roll(scale, turn(k))
    slots = corner_ref.shape[-1]
    cells = PLANES * ROWS
    corner = corner_ref[0, 0]
    row = (corner >> 7).astype(F32)
    column = (corner & (COLS - 1)).astype(F32)
    stacked = jnp.concatenate(
        [weight_ref[0, 0, 0], value_ref[0, 0], precision_ref[0, 0], row, column], axis=0
    )
    tall = jnp.transpose(stacked)
    wide_row = lax.broadcasted_iota(jnp.int32, (slots, cells), 1).astype(F32)
    tall_row = lax.broadcasted_iota(jnp.int32, (cells, slots), 0).astype(F32)
    for step in range(2):
        here = slice(step * slots, (step + 1) * slots)
        pick_ref[here, :] = jnp.where(wide_row == tall[:, 6:7] + step, 1.0, 0.0).astype(jnp.bfloat16)
        back_ref[:, here] = jnp.where(tall_row == row + step, 1.0, 0.0).astype(jnp.bfloat16)
    lane = lanes(slots).astype(F32)
    level = (tall[:, 6:7].astype(jnp.int32) // ROWS) % LEVELS
    column_turned = (tall[:, 7:8].astype(jnp.int32) + turn(level)) % COLS
    for left, low_out, high_out in (
        (tall[:, 7:8].astype(jnp.int32), lower_ref, upper_ref),
        (column_turned, lower_turned, upper_turned),
    ):
        at = lane == left.astype(F32)
        beside = lane == ((left + 1) % COLS).astype(F32)
        low_out[...] = jnp.where(at, tall[:, 0:1], jnp.where(beside, tall[:, 1:2], 0.0))
        high_out[...] = jnp.where(at, tall[:, 2:3], jnp.where(beside, tall[:, 3:4], 0.0))
    live = lax.broadcasted_iota(jnp.int32, (slots, COLS), 0) < count_ref[0]
    value_out[...] = jnp.broadcast_to(tall[:, 4:5], (slots, COLS))
    gain_out[...] = jnp.where(live, jnp.broadcast_to(tall[:, 5:6], (slots, COLS)), 0.0)


def observe_kernel(
    smooth_ref,
    scale_ref,
    keep_ref,
    other_ref,
    turned_ref,
    pick_ref,
    back_ref,
    lower_ref,
    upper_ref,
    lower_turned,
    upper_turned,
    value_ref,
    gain_ref,
    field_ref,
    first_ref,
    second_ref,
    total_ref,
    low_ref,
    high_ref,
):
    group = lax.axis_index("grp")
    slots = value_ref.shape[0]
    for plane in range(PLANES):
        f, k = divmod(plane, LEVELS)
        held = group == k // HALF
        prior = jnp.where(held, keep_ref[f, k % HALF], other_ref[f, k % HALF])
        total_ref[plane * ROWS : (plane + 1) * ROWS, :] = (
            scale_ref[plane] * smooth_ref[plane] + prior
        )
    seen = join(jnp.dot(pick_ref[...], split(total_ref[...]), preferred_element_type=F32))
    lower, upper = lower_ref[...], upper_ref[...]
    weighted = split(lower * seen[:slots] + upper * seen[slots:])
    ones = jnp.ones((2 * COLS, COLS), jnp.bfloat16)
    observed = jnp.dot(weighted, ones, preferred_element_type=F32)
    misfit = gain_ref[...] * (observed - value_ref[...])
    spread = jnp.concatenate([lower_turned[...] * misfit, upper_turned[...] * misfit], axis=0)
    total_ref[...] = join(jnp.dot(back_ref[...], split(spread), preferred_element_type=F32))
    for plane in range(PLANES):
        field_ref[plane] = turned_ref[plane] * total_ref[plane * ROWS : (plane + 1) * ROWS, :]
    stage(
        low_ref,
        high_ref,
        lambda p: field_ref[p, :HALO, :],
        lambda p: field_ref[p, ROWS - HALO :, :],
    )
    blank = jnp.zeros((SHORT - DEPTH_ROW, COLS), F32)
    low_ref[DEPTH_ROW:, :] = blank
    high_ref[DEPTH_ROW:, :] = blank
    send_rows(low_ref, high_ref, first_ref, second_ref)


def call(kernel, outs, scratch=(), remote=0, work=0, out_space=VMEM):
    space = pl.ANY if remote else VMEM

    def run(*args):
        return pl.pallas_call(
            kernel,
            out_shape=[jax.ShapeDtypeStruct(shape, kind) for shape, kind in outs],
            in_specs=[pl.BlockSpec(memory_space=space) for _ in args],
            out_specs=[pl.BlockSpec(memory_space=out_space) for _ in outs],
            scratch_shapes=list(scratch),
            compiler_params=pltpu.CompilerParams(
                vmem_limit_bytes=int((remote or GRANT) * 2**20)
            ),
            cost_estimate=pl.CostEstimate(
                flops=work, bytes_accessed=work // 10, transcendentals=0
            )
            if work
            else None,
            name=kernel.__name__.removesuffix("_kernel"),
        )(*args)

    return run


def swap(value, axis, shift):
    size = lax.axis_size(axis)
    pairs = []
    for i in range(shift, size, 2):
        j = (i + 1) % size
        pairs += [(i, j), (j, i)]
    return lax.ppermute(value, axis, pairs)


def exchange(first, second, axis):
    return swap(second, axis, 1), swap(first, axis, 0)


FULL = ((PLANES, ROWS, COLS), F32)
RAISED = ((PLANES, TALL, COLS), F32)
CUT = ((BANDS, TALL, COLS), F32)
RECORD = ((SWEEPS, DEEP, COLS), F32)
STEP = ((FIELDS, HALF, ROWS, COLS), F32)
PART = ((PAIR, HALF, ROWS, COLS), F32)
MASKS = ((LEVELS, DEEP, COLS), F32)
STRIP = ((BANDS, DEEP, COLS), F32)
SIDES = ((2, DEEP, COLS), F32)


def rows_of(count):
    return ((count, COLS), TRAVEL)


def columns_of(count):
    return ((TALL, count * COLS), TRAVEL)


def body(
    model_state,
    control,
    error_std,
    bottom_level,
    obs_count,
    obs_corner,
    obs_weight,
    obs_value,
    obs_precision,
):
    dma = pltpu.SemaphoreType.DMA
    long, short = VMEM((LONG, COLS), F32), VMEM((SHORT, COLS), F32)
    low, high = call(
        rows_kernel,
        [((LONG, COLS), F32)] * 2,
        [VMEM((PAIR, LEVELS, EDGE, COLS), F32)] * 2
        + [VMEM((FIELDS, HALF, 8, COLS), F32)] * 2
        + [dma((4,))],
        remote=GRANT_MOST,
    )(model_state, control)
    first, second = call(start_kernel, [rows_of(LONG)] * 2, [long, long])(bottom_level, low, high)
    mer = exchange(first, second, "mer")
    slots = obs_corner.shape[-1]
    inputs = (
        obs_count,
        model_state,
        error_std,
        bottom_level,
        obs_corner,
        obs_weight,
        obs_value,
        obs_precision,
    )
    model_east, model_west, model, scale, *operators = call(
        prepare_kernel,
        [((ROWS, COLS), F32)] * 2
        + [STEP, FULL, FULL]
        + [((2 * slots, PLANES * ROWS), jnp.bfloat16), ((PLANES * ROWS, 2 * slots), jnp.bfloat16)]
        + [((slots, COLS), F32)] * 6,
        work=10**7,
    )(*inputs)
    turned, depth, first, second = call(
        first_columns_kernel,
        [RAISED, ((TALL, COLS), F32), columns_of(2), columns_of(2)],
        [long, long, VMEM(*RAISED)],
    )(control, bottom_level, model_east, model_west, *mer)
    zon = exchange(first, second, "zon")
    deep = [VMEM((PLANES, DEEP, COLS), F32)] * 2
    inner, bands, *record, wet, keep_coef, give_coef, base = call(
        first_interior_kernel,
        [FULL, CUT] + [RECORD] * BANDS + [MASKS, MASKS, MASKS, STEP],
        deep + [long, long, VMEM((ROWS + 16, COLS), F32)],
        work=10**7,
    )(turned, depth, model, *mer)
    keep, send = call(background_kernel, [PART, PART])(model, depth, base, *zon)
    other = lax.ppermute(send, "grp", [(0, 1), (1, 0)])
    smoothed, keep_band, give_band = call(
        first_bands_kernel, [FULL, SIDES, SIDES], [VMEM(*SIDES)] + [VMEM(*STRIP)] * 2, work=10**7
    )(*zon, bands, *record, wet, inner)
    field, first, second = call(
        observe_kernel,
        [FULL, rows_of(SHORT), rows_of(SHORT)],
        [VMEM((PLANES * ROWS, COLS), F32), short, short],
    )(smoothed, scale, keep, other, *operators)
    mer = exchange(first, second, "mer")
    turned, first, second = call(
        next_columns_kernel,
        [RAISED, columns_of(1), columns_of(1)],
        [short, short],
    )(field, *mer)
    zon = exchange(first, second, "zon")
    inner, bands, *record = call(
        next_interior_kernel, [FULL, CUT] + [RECORD] * BANDS, deep, work=10**7
    )(turned, keep_coef, give_coef)
    whole = [VMEM(control.shape, F32), dma((4,))]
    return call(
        gradient_kernel, [(control.shape, F32)], [VMEM(*STRIP)] * 2 + whole, out_space=pl.ANY
    )(
        *zon, bands, *record, inner, keep_band, give_band, control
    )[0]


def solution(mesh):
    return jax.shard_map(
        body,
        mesh=mesh,
        in_specs=(
            P(None, "grp", "mer", "zon"),
            P("grp", None, "mer", "zon"),
            P("grp", None, "mer", "zon"),
            P("mer", "zon"),
            P("grp", "mer", "zon"),
            P("grp", "mer", "zon", None),
            P("grp", "mer", "zon", None, None),
            P("grp", "mer", "zon", None),
            P("grp", "mer", "zon", None),
        ),
        out_specs=P("grp", None, "mer", "zon"),
        check_vma=False,
    )
```

```python
import jax
import jax.numpy as jnp
from jax import lax
from jax.experimental import pallas as pl
from jax.experimental.pallas import tpu as pltpu
from jax.sharding import PartitionSpec as P

SWEEPS = 10
SMOOTHING = 0.2
ADVECTION = 0.1
MIXING = 0.15

PAIR = 2
LEVELS = 6
HALF = 3
FIELDS = 4
PLANES = PAIR * LEVELS
STEPPED = FIELDS * HALF
ROWS = 64
COLS = 128
HALO = SWEEPS
EDGE = 16
TALL = ROWS + 2 * EDGE
PAD = 8
DEEP = TALL + 2 * PAD
BAND = 2 * HALO + 1
BANDS = 2 * PAIR
DEPTH_ROW = PLANES * HALO
MODEL_ROW = DEPTH_ROW + HALO
LONG = 160
SHORT = 128
MODEL_LANE = 16
TRAVEL = jnp.bfloat16
F32 = jnp.float32
VMEM = pltpu.VMEM
GRANT, GRANT_MOST = 24, 53.6


def lanes(rows):
    return lax.broadcasted_iota(jnp.int32, (rows, COLS), 1)


def window(lane, start, width):
    start %= COLS
    stop = start + width
    if stop > COLS:
        return (lane >= start) | (lane < stop - COLS)
    return (lane >= start) & (lane < stop)


def roll(value, shift):
    shift %= COLS
    return value if shift == 0 else pltpu.roll(value, shift, 1)


def mer_sides(first, second):
    low, high = sides(first, second, even_on("mer"))
    index = lax.axis_index("mer")
    return jnp.where(index == 0, 0.0, low), jnp.where(index == lax.axis_size("mer") - 1, 0.0, high)


def even_on(axis):
    return lax.axis_index(axis) % 2 == 0


def sides(first, second, even):
    first, second = first.astype(F32), second.astype(F32)
    return jnp.where(even, first, second), jnp.where(even, second, first)


def turn(level):
    return BAND * level + HALO + 1


def stage(low_ref, high_ref, low, high):
    for plane in range(PLANES):
        here = slice(plane * HALO, (plane + 1) * HALO)
        low_ref[here, :] = low(plane)
        high_ref[here, :] = high(plane)


def send_rows(low_ref, high_ref, first_ref, second_ref):
    even = even_on("mer")
    low, high = low_ref[...], high_ref[...]
    first_ref[...] = jnp.where(even, high, low).astype(TRAVEL)
    second_ref[...] = jnp.where(even, low, high).astype(TRAVEL)


def rows_kernel(
    model_ref,
    control_ref,
    low_ref,
    high_ref,
    control_low,
    control_high,
    model_low,
    model_high,
    sems,
):
    ends = pl.ds(0, EDGE), pl.ds(ROWS - EDGE, EDGE)
    tips = pl.ds(0, 8), pl.ds(ROWS - 8, 8)
    copies = [
        pltpu.make_async_copy(control_ref.at[:, :, ends[0], :], control_low, sems.at[0]),
        pltpu.make_async_copy(control_ref.at[:, :, ends[1], :], control_high, sems.at[1]),
        pltpu.make_async_copy(model_ref.at[:, :, tips[0], :], model_low, sems.at[2]),
        pltpu.make_async_copy(model_ref.at[:, :, tips[1], :], model_high, sems.at[3]),
    ]
    for copy in copies:
        copy.start()
    for copy in copies:
        copy.wait()
    stage(
        low_ref,
        high_ref,
        lambda p: control_low[p // LEVELS, p % LEVELS, :HALO, :],
        lambda p: control_high[p // LEVELS, p % LEVELS, EDGE - HALO :, :],
    )
    for q in range(STEPPED):
        for ref, value in (
            (low_ref, model_low[q // HALF, q % HALF, :1, :]),
            (high_ref, model_high[q // HALF, q % HALF, 7:, :]),
        ):
            coarse = value.astype(TRAVEL).astype(F32)
            at = MODEL_ROW + q
            ref[at : at + 1, :] = coarse
            ref[at + STEPPED : at + STEPPED + 1, :] = value - coarse
    rest = MODEL_ROW + 2 * STEPPED
    low_ref[rest:, :] = jnp.zeros((LONG - rest, COLS), F32)
    high_ref[rest:, :] = jnp.zeros((LONG - rest, COLS), F32)


def start_kernel(bottom_ref, first_low, first_high, first_ref, second_ref, low_ref, high_ref):
    low_ref[...] = first_low[...]
    high_ref[...] = first_high[...]
    low_ref[DEPTH_ROW:MODEL_ROW, :] = bottom_ref[:HALO, :].astype(F32)
    high_ref[DEPTH_ROW:MODEL_ROW, :] = bottom_ref[ROWS - HALO :, :].astype(F32)
    send_rows(low_ref, high_ref, first_ref, second_ref)


def stand(value, low, high):
    blank = jnp.zeros((EDGE - HALO, COLS), F32)
    return jnp.concatenate([blank, low, value, high, blank], axis=0)


def stand_core(value):
    blank = jnp.zeros((EDGE, COLS), F32)
    return jnp.concatenate([blank, value, blank], axis=0)


def model_columns(model_ref, east_ref, west_ref):
    lane = lanes(ROWS)
    to_east = to_west = jnp.zeros((ROWS, COLS), F32)
    for q in range(STEPPED):
        value = model_ref[q // HALF, q % HALF]
        at = MODEL_LANE + 2 * q
        column = value[:, COLS - 1 :]
        coarse = column.astype(TRAVEL).astype(F32)
        to_east = jnp.where(lane == at, coarse, to_east)
        to_east = jnp.where(lane == at + 1, column - coarse, to_east)
        column = value[:, :1]
        coarse = column.astype(TRAVEL).astype(F32)
        to_west = jnp.where(lane == at - 1, coarse, to_west)
        to_west = jnp.where(lane == at - 2, column - coarse, to_west)
    east_ref[...] = to_east
    west_ref[...] = to_west


def raise_planes(read, first_ref, second_ref, low_ref, high_ref, tall_ref):
    low, high = mer_sides(first_ref[...], second_ref[...])
    low_ref[...] = low
    high_ref[...] = high
    blank = jnp.zeros((EDGE - HALO, COLS), F32)
    for plane in range(PLANES):
        here = slice(plane * HALO, (plane + 1) * HALO)
        tall_ref[plane, : EDGE - HALO, :] = blank
        tall_ref[plane, EDGE - HALO : EDGE, :] = low_ref[here, :]
        tall_ref[plane, EDGE : EDGE + ROWS, :] = read(plane)
        tall_ref[plane, EDGE + ROWS : EDGE + ROWS + HALO, :] = high_ref[here, :]
        tall_ref[plane, EDGE + ROWS + HALO :, :] = blank


def turn_planes(tall_ref, turned_ref):
    lane = lanes(TALL)
    to_east, to_west = [], []
    for f in range(PAIR):
        go_east = go_west = jnp.zeros((TALL, COLS), F32)
        for k in range(LEVELS):
            turned = tall_ref[f * LEVELS + k]
            if turned_ref is not None:
                turned = roll(turned, turn(k))
                turned_ref[f * LEVELS + k] = turned
            at = BAND * k
            go_east = jnp.where(window(lane, at + 1, HALO), turned, go_east)
            go_west = jnp.where(window(lane, at + 1 + HALO, HALO), turned, go_west)
        to_east.append(go_east)
        to_west.append(go_west)
    return to_east[0] + roll(to_east[1], HALO), to_west[0] + roll(to_west[1], -HALO)


def send_columns(part, to_east, to_west, first_ref, second_ref):
    even = even_on("zon")
    here = slice(part * COLS, (part + 1) * COLS)
    first_ref[:, here] = jnp.where(even, to_east, to_west).astype(TRAVEL)
    second_ref[:, here] = jnp.where(even, to_west, to_east).astype(TRAVEL)


def first_columns_kernel(
    control_ref,
    bottom_ref,
    model_east_ref,
    model_west_ref,
    a_ref,
    b_ref,
    turned_ref,
    depth_ref,
    first_ref,
    second_ref,
    low_ref,
    high_ref,
    tall_ref,
):
    raise_planes(
        lambda p: control_ref[p // LEVELS, p % LEVELS], a_ref, b_ref, low_ref, high_ref, tall_ref
    )
    send_columns(0, *turn_planes(tall_ref, turned_ref), first_ref, second_ref)
    depth = stand(
        bottom_ref[...].astype(F32),
        low_ref[DEPTH_ROW:MODEL_ROW, :],
        high_ref[DEPTH_ROW:MODEL_ROW, :],
    )
    depth_ref[...] = depth
    mark = lanes(TALL) < HALO
    send_columns(
        1,
        jnp.where(mark, roll(depth, HALO), stand_core(model_east_ref[...])),
        jnp.where(mark, depth, stand_core(model_west_ref[...])),
        first_ref,
        second_ref,
    )


def next_columns_kernel(
    field_ref, a_ref, b_ref, turned_ref, first_ref, second_ref, low_ref, high_ref
):
    raise_planes(lambda p: field_ref[p], a_ref, b_ref, low_ref, high_ref, turned_ref)
    send_columns(0, *turn_planes(turned_ref, None), first_ref, second_ref)


def base_step(model_ref, depth_ref, a_ref, b_ref, base_ref, low_ref, high_ref, tall_ref):
    lane = lanes(ROWS)
    group = lax.axis_index("grp")
    low, high = mer_sides(a_ref[...], b_ref[...])
    low_ref[...] = low
    high_ref[...] = high
    core = slice(EDGE, EDGE + ROWS)
    south, north = slice(EDGE - 1, EDGE + ROWS - 1), slice(EDGE + 1, EDGE + ROWS + 1)
    depth = depth_ref[core, :]
    around = (
        depth,
        jnp.where(lane == COLS - 1, 0.0, roll(depth, -1)),
        jnp.where(lane == 0, 0.0, roll(depth, 1)),
        depth_ref[north, :],
        depth_ref[south, :],
    )
    for level in range(HALF):
        here = (group * HALF + level).astype(F32)
        wet, wet_e, wet_w, wet_n, wet_s = (jnp.where(v > here, 1.0, 0.0) for v in around)
        count = MIXING * (wet_e + wet_w + wet_n + wet_s)
        flow_x = 0.5 * ADVECTION * model_ref[2, level]
        flow_y = 0.5 * ADVECTION * model_ref[3, level]
        give_e, give_w = wet_e * (MIXING - flow_x), wet_w * (MIXING + flow_x)
        give_n, give_s = wet_n * (MIXING - flow_y), wet_s * (MIXING + flow_y)
        for field in range(FIELDS):
            at = MODEL_ROW + field * HALF + level
            value = model_ref[field, level]
            tall_ref[8 : 8 + ROWS, :] = value
            tall_ref[7:8, :] = low_ref[at : at + 1, :] + low_ref[at + STEPPED : at + STEPPED + 1, :]
            tall_ref[8 + ROWS : 9 + ROWS, :] = (
                high_ref[at : at + 1, :] + high_ref[at + STEPPED : at + STEPPED + 1, :]
            )
            base_ref[field, level] = wet * (
                value * (1.0 - count)
                + give_e * roll(value, -1)
                + give_w * roll(value, 1)
                + give_n * tall_ref[9 : 9 + ROWS, :]
                + give_s * tall_ref[7 : 7 + ROWS, :]
            )


def background_kernel(model_ref, depth_ref, base_ref, first_ref, second_ref, keep_ref, send_ref):
    lane = lanes(ROWS)
    group = lax.axis_index("grp")
    core = slice(EDGE, EDGE + ROWS)
    before, after = sides(first_ref[core, COLS:], second_ref[core, COLS:], even_on("zon"))
    at_west, at_east = lane == 0, lane == COLS - 1
    beside = jnp.where(at_west, roll(before, 1 - HALO), jnp.where(at_east, roll(after, -1), 0.0))
    depth = jnp.minimum(depth_ref[core, :], beside)
    columns = jnp.where(lane % 2 == 0, before + roll(before, -1), after + roll(after, 1))
    sign = jnp.where(at_west, 0.5 * ADVECTION, -0.5 * ADVECTION)
    for level in range(HALF):
        wet = depth > (group * HALF + level).astype(F32)
        gain = jnp.where(wet, MIXING + sign * model_ref[2, level], 0.0)
        loss = jnp.where(wet, MIXING, 0.0)
        for out_ref, pair in ((keep_ref, group), (send_ref, 1 - group)):
            for f in range(PAIR):
                field = PAIR * pair + f
                at = MODEL_LANE + 2 * (field * HALF + level)
                halo = pltpu.roll(columns, COLS - at, 1)
                out_ref[f, level] = base_ref[field, level] + (
                    gain * halo - loss * model_ref[field, level]
                )


def neighbour_sum(ref, index, start, rows):
    here = ref[index, pl.ds(start, rows), :]
    return here, (roll(here, -1) + roll(here, 1)) + (
        ref[index, pl.ds(start - 1, rows), :] + ref[index, pl.ds(start + 1, rows), :]
    )


def coefficients(mask_ref, count, keep_ref, give_ref):
    for index in range(count):
        wet, total = neighbour_sum(mask_ref, index, PAD, TALL)
        keep_ref[index, PAD : PAD + TALL, :] = wet * (1.0 - SMOOTHING * total)
        give_ref[index, PAD : PAD + TALL, :] = SMOOTHING * wet


def sweep_all(sweep):
    sweep(0, 0, PAD, TALL)
    sweep(1, 1, 2 * PAD, TALL - 2 * PAD)

    def pair(step, carry):
        sweep(2 * step + 2, 0, 2 * PAD, TALL - 2 * PAD)
        sweep(2 * step + 3, 1, 2 * PAD, TALL - 2 * PAD)
        return carry

    lax.fori_loop(0, SWEEPS // 2 - 2, pair, 0)
    sweep(SWEEPS - 2, 0, 2 * PAD, TALL - 2 * PAD)
    sweep(SWEEPS - 1, 1, PAD + EDGE, ROWS)


def sweep_planes(keep_ref, give_ref, one_ref, two_ref, record_refs):
    def sweep(index, odd, start, rows):
        source_ref, target_ref = (two_ref, one_ref) if odd else (one_ref, two_ref)
        at = pl.ds(start, rows)
        lane = lanes(rows)
        for f in range(PAIR):
            west = east = jnp.zeros((rows, COLS), F32)
            for k in range(LEVELS):
                plane = f * LEVELS + k
                here, total = neighbour_sum(source_ref, plane, start, rows)
                target_ref[plane, at, :] = keep_ref[k, at, :] * here + give_ref[k, at, :] * total
                west = jnp.where(lane == BAND * (k + 1), here, west)
                east = jnp.where(lane == BAND * k, here, east)
            record_refs[f][index, at, :] = west
            record_refs[PAIR + f][index, at, :] = east

    sweep_all(sweep)


def sweep_bands(keep_ref, give_ref, one_ref, two_ref, record_refs):
    def sweep(index, odd, start, rows):
        source_ref, target_ref = (two_ref, one_ref) if odd else (one_ref, two_ref)
        at = pl.ds(start, rows)
        for tile in range(BANDS):
            here = source_ref[tile, at, :] + record_refs[tile][index, at, :]
            total = (roll(here, -1) + roll(here, 1)) + (
                source_ref[tile, pl.ds(start - 1, rows), :]
                + source_ref[tile, pl.ds(start + 1, rows), :]
            )
            side = tile // PAIR
            target_ref[tile, at, :] = keep_ref[side, at, :] * here + give_ref[side, at, :] * total

    sweep_all(sweep)


def clear_pads(ref, count):
    for index in range(count):
        ref[index, :PAD, :] = jnp.zeros((PAD, COLS), F32)
        ref[index, PAD + TALL :, :] = jnp.zeros((PAD, COLS), F32)


CORE = slice(PAD + EDGE, PAD + EDGE + ROWS)
BODY = slice(PAD, PAD + TALL)


def bands_of(one_ref, bands_ref):
    lane = lanes(TALL)
    for f in range(PAIR):
        west = east = jnp.zeros((TALL, COLS), F32)
        for k in range(LEVELS):
            value = one_ref[f * LEVELS + k, BODY, :]
            west = jnp.where(window(lane, BAND * k + 1 + HALO, HALO), value, west)
            east = jnp.where(window(lane, BAND * k + 1, HALO), value, east)
        bands_ref[f] = west
        bands_ref[PAIR + f] = east


def first_interior_kernel(
    turned_ref,
    depth_ref,
    model_ref,
    a_ref,
    b_ref,
    inner_ref,
    bands_ref,
    record_0,
    record_1,
    record_2,
    record_3,
    mask_ref,
    keep_ref,
    give_ref,
    base_ref,
    one_ref,
    two_ref,
    low_ref,
    high_ref,
    stand_ref,
):
    base_step(model_ref, depth_ref, a_ref, b_ref, base_ref, low_ref, high_ref, stand_ref)
    clear_pads(mask_ref, LEVELS)
    clear_pads(one_ref, PLANES)
    depth = depth_ref[...]
    for level in range(LEVELS):
        wet = roll(jnp.where(depth > level, 1.0, 0.0), turn(level))
        mask_ref[level, BODY, :] = wet
        for field in range(PAIR):
            plane = field * LEVELS + level
            one_ref[plane, BODY, :] = wet * turned_ref[plane]
    coefficients(mask_ref, LEVELS, keep_ref, give_ref)
    bands_of(one_ref, bands_ref)
    sweep_planes(keep_ref, give_ref, one_ref, two_ref, (record_0, record_1, record_2, record_3))
    for plane in range(PLANES):
        inner_ref[plane] = one_ref[plane, CORE, :]


def next_interior_kernel(
    turned_ref, keep_ref, give_ref, inner_ref, bands_ref, record_0, record_1, record_2, record_3, one_ref, two_ref
):
    clear_pads(one_ref, PLANES)
    for plane in range(PLANES):
        one_ref[plane, BODY, :] = turned_ref[plane]
    bands_of(one_ref, bands_ref)
    sweep_planes(keep_ref, give_ref, one_ref, two_ref, (record_0, record_1, record_2, record_3))
    for plane in range(PLANES):
        inner_ref[plane] = one_ref[plane, CORE, :]


def fill_bands(first_ref, second_ref, bands_ref, one_ref, mask_ref):
    inside = lanes(TALL) % BAND
    near, far = (inside >= 1) & (inside <= HALO), inside > HALO
    before, after = sides(first_ref[:, :COLS], second_ref[:, :COLS], even_on("zon"))
    clear_pads(one_ref, BANDS)
    for f in range(PAIR):
        west, east = (before, after) if f == 0 else (roll(before, -HALO), roll(after, HALO))
        if mask_ref is not None:
            west, east = west * mask_ref[0, BODY, :], east * mask_ref[1, BODY, :]
        one_ref[f, BODY, :] = jnp.where(near, west, bands_ref[f])
        one_ref[PAIR + f, BODY, :] = jnp.where(far, east, bands_ref[PAIR + f])


def join_bands(one_ref, plane, inner, lane):
    f, k = divmod(plane, LEVELS)
    at = BAND * k + 1
    value = jnp.where(window(lane, at, HALO), one_ref[PAIR + f, CORE, :], inner)
    value = jnp.where(window(lane, at + HALO, HALO), one_ref[f, CORE, :], value)
    return roll(value, -turn(k))


def first_bands_kernel(
    first_ref,
    second_ref,
    bands_ref,
    record_0,
    record_1,
    record_2,
    record_3,
    wet_ref,
    inner_ref,
    out_ref,
    keep_ref,
    give_ref,
    mask_ref,
    one_ref,
    two_ref,
):
    tall_lane = lanes(TALL)
    clear_pads(mask_ref, 2)
    before, after = sides(first_ref[:, COLS:], second_ref[:, COLS:], even_on("zon"))
    west = east = jnp.zeros((TALL, COLS), F32)
    for k in range(LEVELS):
        at = BAND * k
        wet = wet_ref[k, BODY, :]
        low = jnp.where(roll(before, at + 1) > k, 1.0, 0.0)
        high = jnp.where(roll(after, at + 1 + HALO) > k, 1.0, 0.0)
        west = jnp.where(window(tall_lane, at + 1, HALO), low, west)
        west = jnp.where(window(tall_lane, at + 1 + HALO, HALO + 1), wet, west)
        east = jnp.where(window(tall_lane, at, HALO + 1), wet, east)
        east = jnp.where(window(tall_lane, at + 1 + HALO, HALO), high, east)
    mask_ref[0, BODY, :] = west
    mask_ref[1, BODY, :] = east
    inside = jnp.where(tall_lane % BAND == 0, 0.0, 1.0)
    for side in range(2):
        wet, total = neighbour_sum(mask_ref, side, PAD, TALL)
        keep_ref[side, BODY, :] = inside * (wet * (1.0 - SMOOTHING * total))
        give_ref[side, BODY, :] = inside * (SMOOTHING * wet)
    fill_bands(first_ref, second_ref, bands_ref, one_ref, mask_ref)
    sweep_bands(keep_ref, give_ref, one_ref, two_ref, (record_0, record_1, record_2, record_3))
    lane = lanes(ROWS)
    for plane in range(PLANES):
        out_ref[plane] = join_bands(one_ref, plane, inner_ref[plane], lane)


def gradient_kernel(
    first_ref,
    second_ref,
    bands_ref,
    record_0,
    record_1,
    record_2,
    record_3,
    inner_ref,
    keep_ref,
    give_ref,
    control_ref,
    out_ref,
    one_ref,
    two_ref,
    whole_ref,
    sems,
):
    fill_bands(first_ref, second_ref, bands_ref, one_ref, None)
    sweep_bands(keep_ref, give_ref, one_ref, two_ref, (record_0, record_1, record_2, record_3))
    lane = lanes(ROWS)
    copies = []
    for plane in range(PLANES):
        f, k = divmod(plane, LEVELS)
        whole_ref[f, k] = control_ref[f, k] + join_bands(one_ref, plane, inner_ref[plane], lane)
        part, last = divmod(plane, 3)
        if last == 2:
            here = pl.ds(k - 2, 3)
            copies.append(
                pltpu.make_async_copy(whole_ref.at[f, here], out_ref.at[f, here], sems.at[part])
            )
            copies[-1].start()
    for copy in copies:
        copy.wait()


def split(value):
    coarse = value.astype(jnp.bfloat16)
    return jnp.concatenate([coarse, (value - coarse.astype(F32)).astype(jnp.bfloat16)], axis=1)


def join(value):
    return value[:, :COLS] + value[:, COLS:]


def prepare_kernel(*refs):
    count_ref, model_ref, error_ref, bottom_ref, *observed_refs = refs[:8]
    corner_ref, weight_ref, value_ref, precision_ref = observed_refs
    east_ref, west_ref, copy_ref, scale_ref, turned_ref, pick_ref, back_ref = refs[8:15]
    lower_ref, upper_ref, lower_turned, upper_turned, value_out, gain_out = refs[15:]
    copy_ref[...] = model_ref[...]
    model_columns(model_ref, east_ref, west_ref)
    depth = bottom_ref[...]
    for plane in range(PLANES):
        f, k = divmod(plane, LEVELS)
        scale = jnp.where(depth > k, error_ref[f, k], 0.0)
        scale_ref[plane] = scale
        turned_ref[plane] = roll(scale, turn(k))
    slots = corner_ref.shape[-1]
    cells = PLANES * ROWS
    corner = corner_ref[0, 0]
    row = (corner >> 7).astype(F32)
    column = (corner & (COLS - 1)).astype(F32)
    stacked = jnp.concatenate(
        [weight_ref[0, 0, 0], value_ref[0, 0], precision_ref[0, 0], row, column], axis=0
    )
    tall = jnp.transpose(stacked)
    wide_row = lax.broadcasted_iota(jnp.int32, (slots, cells), 1).astype(F32)
    tall_row = lax.broadcasted_iota(jnp.int32, (cells, slots), 0).astype(F32)
    for step in range(2):
        here = slice(step * slots, (step + 1) * slots)
        pick_ref[here, :] = jnp.where(wide_row == tall[:, 6:7] + step, 1.0, 0.0).astype(jnp.bfloat16)
        back_ref[:, here] = jnp.where(tall_row == row + step, 1.0, 0.0).astype(jnp.bfloat16)
    lane = lanes(slots).astype(F32)
    level = (tall[:, 6:7].astype(jnp.int32) // ROWS) % LEVELS
    column_turned = (tall[:, 7:8].astype(jnp.int32) + turn(level)) % COLS
    for left, low_out, high_out in (
        (tall[:, 7:8].astype(jnp.int32), lower_ref, upper_ref),
        (column_turned, lower_turned, upper_turned),
    ):
        at = lane == left.astype(F32)
        beside = lane == ((left + 1) % COLS).astype(F32)
        low_out[...] = jnp.where(at, tall[:, 0:1], jnp.where(beside, tall[:, 1:2], 0.0))
        high_out[...] = jnp.where(at, tall[:, 2:3], jnp.where(beside, tall[:, 3:4], 0.0))
    live = lax.broadcasted_iota(jnp.int32, (slots, COLS), 0) < count_ref[0]
    value_out[...] = jnp.broadcast_to(tall[:, 4:5], (slots, COLS))
    gain_out[...] = jnp.where(live, jnp.broadcast_to(tall[:, 5:6], (slots, COLS)), 0.0)


def observe_kernel(
    smooth_ref,
    scale_ref,
    keep_ref,
    other_ref,
    turned_ref,
    pick_ref,
    back_ref,
    lower_ref,
    upper_ref,
    lower_turned,
    upper_turned,
    value_ref,
    gain_ref,
    field_ref,
    first_ref,
    second_ref,
    total_ref,
    low_ref,
    high_ref,
):
    group = lax.axis_index("grp")
    slots = value_ref.shape[0]
    for plane in range(PLANES):
        f, k = divmod(plane, LEVELS)
        held = group == k // HALF
        prior = jnp.where(held, keep_ref[f, k % HALF], other_ref[f, k % HALF])
        total_ref[plane * ROWS : (plane + 1) * ROWS, :] = (
            scale_ref[plane] * smooth_ref[plane] + prior
        )
    seen = join(jnp.dot(pick_ref[...], split(total_ref[...]), preferred_element_type=F32))
    lower, upper = lower_ref[...], upper_ref[...]
    weighted = split(lower * seen[:slots] + upper * seen[slots:])
    ones = jnp.ones((2 * COLS, COLS), jnp.bfloat16)
    observed = jnp.dot(weighted, ones, preferred_element_type=F32)
    misfit = gain_ref[...] * (observed - value_ref[...])
    spread = jnp.concatenate([lower_turned[...] * misfit, upper_turned[...] * misfit], axis=0)
    total_ref[...] = join(jnp.dot(back_ref[...], split(spread), preferred_element_type=F32))
    for plane in range(PLANES):
        field_ref[plane] = turned_ref[plane] * total_ref[plane * ROWS : (plane + 1) * ROWS, :]
    stage(
        low_ref,
        high_ref,
        lambda p: field_ref[p, :HALO, :],
        lambda p: field_ref[p, ROWS - HALO :, :],
    )
    blank = jnp.zeros((SHORT - DEPTH_ROW, COLS), F32)
    low_ref[DEPTH_ROW:, :] = blank
    high_ref[DEPTH_ROW:, :] = blank
    send_rows(low_ref, high_ref, first_ref, second_ref)


def call(kernel, outs, scratch=(), remote=0, work=0, out_space=VMEM):
    space = pl.ANY if remote else VMEM

    def run(*args):
        return pl.pallas_call(
            kernel,
            out_shape=[jax.ShapeDtypeStruct(shape, kind) for shape, kind in outs],
            in_specs=[pl.BlockSpec(memory_space=space) for _ in args],
            out_specs=[pl.BlockSpec(memory_space=out_space) for _ in outs],
            scratch_shapes=list(scratch),
            compiler_params=pltpu.CompilerParams(
                vmem_limit_bytes=int((remote or GRANT) * 2**20)
            ),
            cost_estimate=pl.CostEstimate(
                flops=work, bytes_accessed=work // 10, transcendentals=0
            )
            if work
            else None,
            name=kernel.__name__.removesuffix("_kernel"),
        )(*args)

    return run


def swap(value, axis, shift):
    size = lax.axis_size(axis)
    pairs = []
    for i in range(shift, size, 2):
        j = (i + 1) % size
        pairs += [(i, j), (j, i)]
    return lax.ppermute(value, axis, pairs)


def exchange(first, second, axis):
    return swap(second, axis, 1), swap(first, axis, 0)


FULL = ((PLANES, ROWS, COLS), F32)
RAISED = ((PLANES, TALL, COLS), F32)
CUT = ((BANDS, TALL, COLS), F32)
RECORD = ((SWEEPS, DEEP, COLS), F32)
STEP = ((FIELDS, HALF, ROWS, COLS), F32)
PART = ((PAIR, HALF, ROWS, COLS), F32)
MASKS = ((LEVELS, DEEP, COLS), F32)
STRIP = ((BANDS, DEEP, COLS), F32)
SIDES = ((2, DEEP, COLS), F32)


def rows_of(count):
    return ((count, COLS), TRAVEL)


def columns_of(count):
    return ((TALL, count * COLS), TRAVEL)


def body(
    model_state,
    control,
    error_std,
    bottom_level,
    obs_count,
    obs_corner,
    obs_weight,
    obs_value,
    obs_precision,
):
    dma = pltpu.SemaphoreType.DMA
    long, short = VMEM((LONG, COLS), F32), VMEM((SHORT, COLS), F32)
    low, high = call(
        rows_kernel,
        [((LONG, COLS), F32)] * 2,
        [VMEM((PAIR, LEVELS, EDGE, COLS), F32)] * 2
        + [VMEM((FIELDS, HALF, 8, COLS), F32)] * 2
        + [dma((4,))],
        remote=GRANT_MOST,
    )(model_state, control)
    first, second = call(start_kernel, [rows_of(LONG)] * 2, [long, long])(bottom_level, low, high)
    mer = exchange(first, second, "mer")
    slots = obs_corner.shape[-1]
    inputs = (
        obs_count,
        model_state,
        error_std,
        bottom_level,
        obs_corner,
        obs_weight,
        obs_value,
        obs_precision,
    )
    model_east, model_west, model, scale, *operators = call(
        prepare_kernel,
        [((ROWS, COLS), F32)] * 2
        + [STEP, FULL, FULL]
        + [((2 * slots, PLANES * ROWS), jnp.bfloat16), ((PLANES * ROWS, 2 * slots), jnp.bfloat16)]
        + [((slots, COLS), F32)] * 6,
        work=10**7,
    )(*inputs)
    turned, depth, first, second = call(
        first_columns_kernel,
        [RAISED, ((TALL, COLS), F32), columns_of(2), columns_of(2)],
        [long, long, VMEM(*RAISED)],
    )(control, bottom_level, model_east, model_west, *mer)
    zon = exchange(first, second, "zon")
    deep = [VMEM((PLANES, DEEP, COLS), F32)] * 2
    inner, bands, *record, wet, keep_coef, give_coef, base = call(
        first_interior_kernel,
        [FULL, CUT] + [RECORD] * BANDS + [MASKS, MASKS, MASKS, STEP],
        deep + [long, long, VMEM((ROWS + 16, COLS), F32)],
        work=10**7,
    )(turned, depth, model, *mer)
    keep, send = call(background_kernel, [PART, PART])(model, depth, base, *zon)
    other = lax.ppermute(send, "grp", [(0, 1), (1, 0)])
    smoothed, keep_band, give_band = call(
        first_bands_kernel, [FULL, SIDES, SIDES], [VMEM(*SIDES)] + [VMEM(*STRIP)] * 2, work=10**7
    )(*zon, bands, *record, wet, inner)
    field, first, second = call(
        observe_kernel,
        [FULL, rows_of(SHORT), rows_of(SHORT)],
        [VMEM((PLANES * ROWS, COLS), F32), short, short],
    )(smoothed, scale, keep, other, *operators)
    mer = exchange(first, second, "mer")
    turned, first, second = call(
        next_columns_kernel,
        [RAISED, columns_of(1), columns_of(1)],
        [short, short],
    )(field, *mer)
    zon = exchange(first, second, "zon")
    inner, bands, *record = call(
        next_interior_kernel, [FULL, CUT] + [RECORD] * BANDS, deep, work=10**7
    )(turned, keep_coef, give_coef)
    whole = [VMEM(control.shape, F32), dma((4,))]
    return call(
        gradient_kernel, [(control.shape, F32)], [VMEM(*STRIP)] * 2 + whole, out_space=pl.ANY
    )(
        *zon, bands, *record, inner, keep_band, give_band, control
    )[0]


def solution(mesh):
    return jax.shard_map(
        body,
        mesh=mesh,
        in_specs=(
            P(None, "grp", "mer", "zon"),
            P("grp", None, "mer", "zon"),
            P("grp", None, "mer", "zon"),
            P("mer", "zon"),
            P("grp", "mer", "zon"),
            P("grp", "mer", "zon", None),
            P("grp", "mer", "zon", None, None),
            P("grp", "mer", "zon", None),
            P("grp", "mer", "zon", None),
        ),
        out_specs=P("grp", None, "mer", "zon"),
        check_vma=False,
    )
```
